32 devices in a mesh: dp: 8 (over z, y), tensor: 4 (over x, core).
Axes of the slice: x: 2, y: 2, z: 4, core: 2. Of those that a mesh axis runs over, the one named last changes fastest.
Arguments:
- hidden_in: bfloat16 [8, 8, 256, 768], P(None, 'dp', 'tensor'), may hold values from -6 to 6
- lengths: int32 [8], replicated, may hold values from 1537 to 2048, as said below
- order: int32 [8], replicated, may hold values from 0 to 7, each once
- in_gain: float32 [2, 768], replicated, may hold values from 0.1 to 1.9
- w_z: bfloat16 [2, 768, 1536], P(None, 'dp', 'tensor'), may hold values from -0.21875 to 0.21875
- w_x: bfloat16 [2, 768, 1536], P(None, 'dp', 'tensor'), may hold values from -0.21875 to 0.21875
- w_bc: bfloat16 [2, 768, 256], P(None, 'dp'), may hold values from -0.21875 to 0.21875
- w_dt: bfloat16 [2, 768, 24], P(None, 'dp', 'tensor'), may hold values from -0.21875 to 0.21875
- conv_x: float32 [2, 5, 1536], replicated, may hold values from -3 to 3
- conv_bc: float32 [2, 5, 256], replicated, may hold values from -3 to 3
- dt_bias: float32 [2, 24], replicated, may hold values from -4 to -2
- a_log: float32 [2, 24], replicated, may hold values from -5.3 to 0
- d_skip: float32 [2, 24], replicated, may hold values from 0.5 to 1.5
- gated_gain: float32 [2, 1536], replicated, may hold values from 0.1 to 1.9
- w_out: bfloat16 [2, 768, 1536], P(None, 'dp', 'tensor'), may hold values from -0.15625 to 0.15625
- cotangent: bfloat16 [8, 8, 256, 768], P('dp', None, 'tensor'), may hold values from -6 to 6
Outputs:
- block_out: bfloat16 [8, 8, 256, 768], P('dp', None, 'tensor')
- input_grad: bfloat16 [8, 8, 256, 768], P(None, 'dp', 'tensor')
- grad_in_gain: float32 [2, 768], replicated
- grad_w_z: float32 [2, 768, 1536], P(None, 'dp', 'tensor')
- grad_w_x: float32 [2, 768, 1536], P(None, 'dp', 'tensor')
- grad_w_bc: float32 [2, 768, 256], P(None, 'dp')
- grad_w_dt: float32 [2, 768, 24], P(None, 'dp', 'tensor')
- grad_conv_x: float32 [2, 5, 1536], replicated
- grad_conv_bc: float32 [2, 5, 256], replicated
- grad_dt_bias: float32 [2, 24], replicated
- grad_a_log: float32 [2, 24], replicated
- grad_d_skip: float32 [2, 24], replicated
- grad_gated_gain: float32 [2, 1536], replicated
- grad_w_out: float32 [2, 768, 1536], P(None, 'dp', 'tensor')
The draws below stay inside these ranges and needn't reach their ends.
Inputs may be any that keep to these rules, and one draw needn't show every extreme that they name: `lengths`: every length is over 1536 and one sequence has exactly 2048. `order`: each sequence number once.
All inputs are finite; a program needn't handle non-finite values.
Results may differ from the reference program's by a relative error of at most 0.03.
The reference program's roundings to bfloat16 on the way count: a program that leaves them out, or rounds other values in their place, can miss the bound.
Values may be sent and summed in bfloat16 or wider, within the bound.
A program may use at most 256 MiB of HBM per device.

```python
import jax
import jax.numpy as jnp
from jax import lax

D = 768
HEADS = 24
HEAD_DIM = 64
STATE = 128
KERNEL = 4
SCAN_BLOCK = 256
LAYERS = 2
LEN = 2048
INNER = 1536
SEQS = 8
PARTS_SIZE = 8
PART_LEN = 256


def draw_lengths(key, part):
    key = jax.random.fold_in(key, 11)
    first_key, second_key = jax.random.split(key)
    drawn = jax.random.randint(first_key, (SEQS,), 3 * LEN // 4 + 1, LEN + 1)
    chosen = jax.random.randint(second_key, (), 0, SEQS)
    return jnp.where(jnp.arange(SEQS) == chosen, LEN, drawn).astype(jnp.int32)


def shard_levels(rng, dims, cuts, smallest, high):
    factor_of = 1.0
    for dim, shards_of in cuts:
        heights = jax.random.uniform(jax.random.fold_in(jax.random.fold_in(rng, 6), dim), (shards_of,), jnp.float32, smallest / len(cuts), high / len(cuts))
        factor_of = factor_of * jnp.repeat(jnp.exp(heights), dims[dim] // shards_of).reshape((-1,) + (1,) * (len(dims) - 1 - dim))
    return factor_of


def bell_draw(stream_key, shape, scale, reach, cuts=(), dtype=jnp.bfloat16):
    factor_of = shard_levels(stream_key, shape, cuts, -0.22, 0.18) if cuts else 1.0
    values = jax.random.normal(stream_key, shape, jnp.float32) * scale * factor_of
    return jnp.minimum(jnp.maximum(values, -reach), reach).astype(dtype)


def setup_inputs(seed: int = 0) -> dict:
    key_of = jax.random.split(jax.random.key(seed), 17)
    hidden_in = bell_draw(key_of[0], (SEQS, PARTS_SIZE, PART_LEN, D), 1.0, 6.0, ((1, 8), (2, 4)))
    lengths = draw_lengths(jax.random.fold_in(key_of[16], 71), 0)
    order = jax.random.permutation(key_of[2], SEQS).astype(jnp.int32)
    in_gain = jnp.clip(1.0 + 0.18 * jax.random.normal(key_of[3], (LAYERS, D), jnp.float32), 0.1, 1.9)
    w_z = bell_draw(key_of[4], (LAYERS, D, INNER), D ** -0.5, 0.21875, ((1, 8), (2, 4)))
    w_x = bell_draw(key_of[5], (LAYERS, D, INNER), D ** -0.5, 0.21875, ((1, 8), (2, 4)))
    w_bc = bell_draw(key_of[6], (LAYERS, D, 2 * STATE), D ** -0.5, 0.21875, ((1, 8),))
    w_dt = bell_draw(key_of[7], (LAYERS, D, HEADS), D ** -0.5, 0.21875, ((1, 8), (2, 4)))
    conv_x = bell_draw(key_of[8], (LAYERS, KERNEL + 1, INNER), KERNEL ** -0.5, 3.0, (), jnp.float32)
    conv_bc = bell_draw(key_of[9], (LAYERS, KERNEL + 1, 2 * STATE), KERNEL ** -0.5, 3.0, (), jnp.float32)
    dt_bias = jnp.clip(jax.random.uniform(key_of[10], (LAYERS, HEADS), jnp.float32, -4.0, -2.0), -4.0, -2.0)
    a_log = jnp.clip(jax.random.uniform(key_of[11], (LAYERS, HEADS), jnp.float32, -5.3, 0.0), -5.3, 0.0)
    d_skip = jnp.clip(jax.random.uniform(key_of[12], (LAYERS, HEADS), jnp.float32, 0.5, 1.5), 0.5, 1.5)
    gated_gain = jnp.clip(1.0 + 0.18 * jax.random.normal(key_of[13], (LAYERS, INNER), jnp.float32), 0.1, 1.9)
    w_out = bell_draw(key_of[14], (LAYERS, D, INNER), INNER ** -0.5, 0.15625, ((1, 8), (2, 4)))
    cotangent = bell_draw(key_of[15], (SEQS, PARTS_SIZE, PART_LEN, D), 1.0, 6.0, ((0, 8), (2, 4)))
    return dict(hidden_in=hidden_in, lengths=lengths, order=order, in_gain=in_gain, w_z=w_z, w_x=w_x, w_bc=w_bc, w_dt=w_dt, conv_x=conv_x, conv_bc=conv_bc, dt_bias=dt_bias, a_log=a_log, d_skip=d_skip, gated_gain=gated_gain, w_out=w_out, cotangent=cotangent)


EPS = 1e-05
HIGH = lax.Precision.HIGHEST

@jax.custom_vjp
def low(v):
    return lax.optimization_barrier(v.astype(jnp.bfloat16)).astype(jnp.float32)

@jax.custom_vjp
def low_back(v):
    return v

def low_keep(v):
    return (low(v), None)

def low_pass(kept, grad):
    return (grad,)

def back_keep(v):
    return (v, None)

def back_low(kept, grad):
    return (low(grad),)
low.defvjp(low_keep, low_pass)
low_back.defvjp(back_keep, back_low)

def conv_silu(values, taps):
    width = taps.shape[0] - 1
    length_all = values.shape[0]
    padded = jnp.pad(values, ((width - 1, 0), (0, 0)))
    mixed_sum = taps[width] + taps[0] * padded[0:length_all]
    for offset in range(1, width):
        mixed_sum = mixed_sum + taps[offset] * padded[offset:offset + length_all]
    return jax.nn.silu(mixed_sum)

def scan_product(inputs, b_matrix, c_matrix, step_sizes, decay):
    length_all, head_count, head_size = inputs.shape
    state_size = b_matrix.shape[1]
    block_count = length_all // SCAN_BLOCK
    pieces = (inputs.reshape(block_count, SCAN_BLOCK, head_count, head_size), b_matrix.reshape(block_count, SCAN_BLOCK, state_size), c_matrix.reshape(block_count, SCAN_BLOCK, state_size), step_sizes.reshape(block_count, SCAN_BLOCK, head_count))
    causal = (jnp.arange(SCAN_BLOCK)[:, None] >= jnp.arange(SCAN_BLOCK)[None, :])[:, :, None]

    def advance(carried, block_in):
        x_part, b_part, c_part, step_part = block_in
        log_rates = -step_part * decay[None, :]
        running = jnp.cumsum(log_rates, axis=0)
        spread = running[:, None, :] - running[None, :, :]
        within = jnp.where(causal, jnp.exp(jnp.where(causal, spread, 0.0)), 0.0)
        scores = jnp.einsum('tn,sn->ts', c_part, b_part, precision=HIGH)
        mixing = scores[:, :, None] * within * step_part[None, :, :]
        local_out = jnp.einsum('tsh,shp->thp', mixing, x_part, precision=HIGH)
        from_state = jnp.exp(running)[:, :, None] * jnp.einsum('tn,hnp->thp', c_part, carried, precision=HIGH)
        remain = jnp.exp(running[-1][None, :] - running) * step_part
        carried = jnp.exp(running[-1])[:, None, None] * carried + jnp.einsum('sh,sn,shp->hnp', remain, b_part, x_part, precision=HIGH)
        return (carried, local_out + from_state)
    initial = jnp.zeros((head_count, state_size, head_size), jnp.float32)
    final_state, outputs = lax.scan(jax.checkpoint(advance), initial, pieces)
    return outputs.reshape(length_all, head_count, head_size)

def one_sequence(sequence, seq_length, params):
    in_gain, w_z, w_x, w_bc, w_dt, conv_x, conv_bc, dt_bias, a_log, d_skip, gated_gain, w_out = params
    length_all = sequence.shape[0]
    live_rows = (jnp.arange(length_all) < seq_length).astype(jnp.float32)[:, None]
    hidden = sequence
    for layer_idx in range(LAYERS):
        inv_rms = lax.rsqrt(lax.optimization_barrier(jnp.mean(hidden * hidden, axis=-1, keepdims=True)) + EPS)
        normed = low(hidden * inv_rms * in_gain[layer_idx])
        gate_in = low_back(jnp.dot(normed, w_z[layer_idx], precision=HIGH))
        x_raw = low_back(jnp.dot(normed, w_x[layer_idx], precision=HIGH))
        bc_raw = low_back(jnp.dot(normed, w_bc[layer_idx], precision=HIGH))
        dt_raw = low_back(jnp.dot(normed, w_dt[layer_idx], precision=HIGH))
        x_conv = low(conv_silu(x_raw, conv_x[layer_idx]))
        bc_conv = low(conv_silu(bc_raw, conv_bc[layer_idx]))
        step_sizes = jax.nn.softplus(dt_raw + dt_bias[layer_idx]) * live_rows
        x_heads = x_conv.reshape(length_all, HEADS, HEAD_DIM)
        mixed_heads = scan_product(x_heads, bc_conv[:, :STATE], bc_conv[:, STATE:], step_sizes, jnp.exp(a_log[layer_idx])) + d_skip[layer_idx][None, :, None] * x_heads
        gated_mix = mixed_heads.reshape(length_all, INNER) * jax.nn.silu(gate_in)
        gate_rms = lax.rsqrt(lax.optimization_barrier(jnp.mean(gated_mix * gated_mix, axis=-1, keepdims=True)) + EPS)
        gated_out = low(gated_mix * gate_rms * gated_gain[layer_idx])
        branch = low_back(jnp.dot(gated_out, w_out[layer_idx].T, precision=HIGH))
        hidden = (hidden + branch) * live_rows
    return hidden

def reference(hidden_in, lengths, order, in_gain, w_z, w_x, w_bc, w_dt, conv_x, conv_bc, dt_bias, a_log, d_skip, gated_gain, w_out, cotangent):
    params = tuple((argument.astype(jnp.float32) for argument in (in_gain, w_z, w_x, w_bc, w_dt, conv_x, conv_bc, dt_bias, a_log, d_skip, gated_gain, w_out)))
    inputs_all = hidden_in.astype(jnp.float32).reshape(SEQS, LEN, D)
    dealt_lengths = jnp.take(lengths, order)
    run_one = jax.checkpoint(one_sequence)

    def forward(inputs, weights):
        dealt = jnp.take(inputs, order, axis=0)

        def single(seq_pair):
            return run_one(seq_pair[0], seq_pair[1], weights)
        return lax.map(single, (dealt, dealt_lengths))
    outputs, pullback = jax.vjp(forward, inputs_all, params)
    grad_inputs, grad_params = pullback(cotangent.astype(jnp.float32).reshape(SEQS, LEN, D))
    shaped = (SEQS, PARTS_SIZE, PART_LEN, D)
    return (outputs.reshape(shaped).astype(jnp.bfloat16), grad_inputs.reshape(shaped).astype(jnp.bfloat16), grad_params[0], grad_params[1], grad_params[2], grad_params[3], grad_params[4], grad_params[5], grad_params[6], grad_params[7], grad_params[8], grad_params[9], grad_params[10], grad_params[11])
```

```python
from functools import partial

import jax
import jax.numpy as jnp
from jax import lax
from jax.experimental import pallas as pl
from jax.experimental.pallas import tpu as pltpu
from jax.sharding import PartitionSpec as P

SCAN_BLOCK = 256
EPS = 1e-05
LOG2E = 1.4426950408889634
F32, BF16 = jnp.float32, jnp.bfloat16
LANES = 128
GROUP = 256
PAD = 16
ROWS = 128
WIDTH = 4
NN = (((1,), (0,)), ((), ()))
NT = (((1,), (1,)), ((), ()))


def mm(left, right, dims=NN):
    return lax.dot_general(left, right, dims, preferred_element_type=F32)


def exact(left, right):
    return lax.dot_general(
        left, right, NN, precision=lax.Precision.HIGHEST, preferred_element_type=F32
    )


def halves(values):
    high = values.astype(BF16)
    return high, (values - high.astype(F32)).astype(BF16)


def beside(values):
    return jnp.concatenate(halves(values), axis=1)


def lanes_of(step, size):
    return pl.ds(pl.multiple_of(step * size, size), size)


def conv_rows(raw, taps, start, columns):
    total = taps[WIDTH : WIDTH + 1, columns]
    for tap in range(WIDTH):
        first = PAD - (WIDTH - 1) + tap + start
        total = total + taps[tap : tap + 1, columns] * raw[pl.ds(first, ROWS), columns]
    return total


def step_terms(dtp, live, aneg, dt, run, run_t, step_two, grow_two, keep_two, decay, spread, block):
    rows = pl.ds(block * SCAN_BLOCK, SCAN_BLOCK)
    value = dtp[rows, :]
    size = (jnp.maximum(value, 0.0) + jnp.log1p(jnp.exp(-jnp.abs(value)))) * live[rows, :]
    dt[block] = size
    row_id = lax.broadcasted_iota(jnp.int32, (SCAN_BLOCK, SCAN_BLOCK), 0)
    col_id = lax.broadcasted_iota(jnp.int32, (SCAN_BLOCK, SCAN_BLOCK), 1)
    earlier = (row_id >= col_id).astype(F32)
    running = exact(earlier, size * (aneg[0:1, :] * LOG2E))
    run[block] = running
    run_t[block] = running.T
    total = running[SCAN_BLOCK - 1 : SCAN_BLOCK, :]
    step_two[block] = beside(size)
    grow_two[block] = beside(jnp.exp2(running))
    keep_two[block] = beside(jnp.exp2(total - running))
    whole = jnp.broadcast_to(jnp.exp2(total), (8, LANES))
    decay[block] = mm(beside(whole), spread[...])


def split_narrow(narrow, select, wbc, wdt):
    wbc[...] = mm(narrow[...], select[:, : wbc.shape[1]]).astype(BF16)
    wdt[...] = mm(narrow[...], select[:, wbc.shape[1] :]).astype(BF16)


def small_rows(width, inner, state):
    sizes = (
        ("heads", 8),
        ("gain", -(-width // LANES // 8) * 8),
        ("gate_gain", inner // LANES),
        ("tap_x", (WIDTH + 1) * (inner // LANES)),
        ("tap_b", (WIDTH + 1) * (2 * state // LANES)),
    )
    starts, total = {}, 0
    for name, size in sizes:
        starts[name] = total
        total += size
    starts["all"] = -(-total // 8) * 8
    return starts


def forward_kernel(
    n_tensor,
    n_blocks,
    head_size,
    h,
    gain,
    tap_x,
    tap_b,
    dt_bias,
    aneg,
    skip,
    gate_gain,
    live,
    spread,
    select,
    wz_in,
    wx_in,
    wn_in,
    wo_in,
    h_next,
    nx,
    gate,
    xraw,
    braw,
    xc,
    bc,
    dtp,
    mixed,
    states,
    rms,
    wz,
    wx,
    wn,
    wo,
    wbc,
    wdt,
    halo,
    dt,
    run,
    run_t,
    step_two,
    grow_two,
    keep_two,
    decay,
    pair,
    fresh,
    carry_out,
    carry_in,
    gm,
    go,
    squares,
    w_sem,
    halo_send,
    halo_recv,
    carry_send,
    carry_recv,
):
    me = lax.axis_index("tensor")
    tokens, width = h.shape
    inner = gate.shape[1]
    state = fresh.shape[1]
    groups = inner // GROUP
    per_group = GROUP // head_size

    loads = {
        "wz": pltpu.make_async_copy(wz_in, wz, w_sem.at[0]),
        "wx": pltpu.make_async_copy(wx_in, wx, w_sem.at[1]),
        "wo": pltpu.make_async_copy(wo_in, wo, w_sem.at[2]),
        "wn": pltpu.make_async_copy(wn_in, wn, w_sem.at[3]),
    }
    for load in loads.values():
        load.start()

    barrier = pltpu.get_barrier_semaphore()

    @pl.when(me > 0)
    def _():
        pl.semaphore_signal(
            barrier, inc=1, device_id={"tensor": me - 1}, device_id_type=pl.DeviceIdType.MESH
        )

    @pl.when(me < n_tensor - 1)
    def _():
        pl.semaphore_wait(barrier, 1)

    following = lax.rem(me + 1, n_tensor)
    halo_copy = pltpu.make_async_remote_copy(
        src_ref=h.at[pl.ds(tokens - PAD, PAD), :],
        dst_ref=halo,
        send_sem=halo_send,
        recv_sem=halo_recv,
        device_id={"tensor": following},
        device_id_type=pl.DeviceIdType.MESH,
    )
    carry_copies = [
        pltpu.make_async_remote_copy(
            src_ref=carry_out.at[group],
            dst_ref=carry_in.at[group],
            send_sem=carry_send.at[group],
            recv_sem=carry_recv.at[group],
            device_id={"tensor": following},
            device_id_type=pl.DeviceIdType.MESH,
        )
        for group in range(groups)
    ]

    @pl.when(me < n_tensor - 1)
    def _():
        halo_copy.start()

    def normalize(values):
        inv = lax.rsqrt(jnp.mean(values * values, axis=-1, keepdims=True) + EPS)
        return (values * inv * gain[0:1, :]).astype(BF16)

    @pl.loop(0, tokens // ROWS)
    def _(step):
        rows = pl.ds(pl.multiple_of(step * ROWS, ROWS), ROWS)
        nx[pl.ds(pl.multiple_of(PAD + step * ROWS, PAD), ROWS), :] = normalize(h[rows, :])

    loads["wz"].wait()

    @pl.loop(0, groups)
    def _(step):
        columns = lanes_of(step, GROUP)
        gate[:, columns] = mm(nx[pl.ds(PAD, tokens), :], wz[:, columns])

    @pl.when(me > 0)
    def _():
        halo_copy.wait_recv()
        nx[0:PAD, :] = normalize(halo[...])

    @pl.when(me == 0)
    def _():
        nx[0:PAD, :] = jnp.zeros((PAD, width), BF16)

    loads["wx"].wait()

    def convolve(weights, taps, raw, out, columns):
        raw[:, columns] = mm(nx[...], weights[:, columns])
        for start in range(0, tokens, ROWS):
            before = conv_rows(raw, taps, start, columns)
            out[pl.ds(start, ROWS), columns] = (before * jax.nn.sigmoid(before)).astype(BF16)

    @pl.loop(0, groups)
    def _(step):
        convolve(wx, tap_x, xraw, xc, lanes_of(step, GROUP))

    loads["wn"].wait()
    split_narrow(wn, select, wbc, wdt)
    for step in range(bc.shape[1] // GROUP):
        convolve(wbc, tap_b, braw, bc, pl.ds(step * GROUP, GROUP))
    dtp[...] = mm(nx[pl.ds(PAD, tokens), :], wdt[...]) + dt_bias[0:1, :]

    row_id = lax.broadcasted_iota(jnp.int32, (SCAN_BLOCK, SCAN_BLOCK), 0)
    col_id = lax.broadcasted_iota(jnp.int32, (SCAN_BLOCK, SCAN_BLOCK), 1)
    head_of = lax.broadcasted_iota(jnp.int32, (SCAN_BLOCK, GROUP), 1) // head_size
    for block in range(n_blocks):
        step_terms(
            dtp, live, aneg, dt, run, run_t, step_two, grow_two, keep_two, decay, spread, block
        )
        rows = pl.ds(block * SCAN_BLOCK, SCAN_BLOCK)
        scores = mm(bc[rows, state:], bc[rows, :state], NT)
        pair[block] = jnp.where(row_id >= col_id, scores, 0.0)
        b_rows = bc[rows, :state].astype(F32).T.astype(BF16)

        @pl.loop(0, groups)
        def _(group):
            columns = lanes_of(group, GROUP)
            sizes = mm(step_two[block], spread[:, columns])
            keeps = mm(keep_two[block], spread[:, columns])
            weighted = (xc[rows, columns].astype(F32) * sizes * keeps).astype(BF16)
            fresh[block, :, columns] = mm(b_rows, weighted)

    for group in range(groups):
        columns = pl.ds(group * GROUP, GROUP)

        @pl.when(me > 0)
        def _():
            carry_copies[group].wait_recv()
            states[0, :, columns] = carry_in[group].astype(F32)

        @pl.when(me == 0)
        def _():
            states[0, :, columns] = jnp.zeros((state, GROUP), F32)

        for block in range(n_blocks):
            states[block + 1, :, columns] = (
                states[block, :, columns] * decay[block, 0:1, columns] + fresh[block, :, columns]
            )
        carry_out[group] = states[n_blocks, :, columns].astype(BF16)

        @pl.when(me < n_tensor - 1)
        def _():
            carry_copies[group].start()

    squares[...] = jnp.zeros_like(squares)
    for block in range(n_blocks):
        rows = pl.ds(block * SCAN_BLOCK, SCAN_BLOCK)

        @pl.loop(0, groups)
        def _(group):
            columns = lanes_of(group, GROUP)
            sizes = mm(step_two[block], spread[:, columns])
            grown = mm(grow_two[block], spread[:, columns])
            x_here = xc[rows, columns].astype(F32)
            stepped = (x_here * sizes).astype(BF16)
            rolled = pltpu.roll(run[block], lax.rem(LANES - per_group * group, LANES), 1)
            total = grown * mm(bc[rows, state:], states[block, :, columns].astype(BF16))
            total = total + skip[0:1, columns] * x_here
            for head in range(per_group):
                spread_out = (
                    rolled[:, head : head + 1] - run_t[block, pl.ds(per_group * group + head, 1), :]
                )
                mixing = (pair[block] * jnp.exp2(jnp.minimum(spread_out, 0.0))).astype(BF16)
                total = total + mm(mixing, jnp.where(head_of == head, stepped, jnp.zeros_like(stepped)))
            mixed[rows, columns] = total
            gate_in = gate[rows, columns]
            gated = total * gate_in * jax.nn.sigmoid(gate_in)
            gm[rows, columns] = gated
            squared = gated * gated
            for lane in range(0, GROUP, LANES):
                squares[rows, :] += squared[:, lane : lane + LANES]

    rms[...] = jnp.broadcast_to(
        lax.rsqrt(jnp.sum(squares[...], axis=-1, keepdims=True) / inner + EPS), rms.shape
    )

    @pl.loop(0, groups)
    def _(group):
        columns = lanes_of(group, GROUP)
        for start in range(0, tokens, ROWS):
            rows = pl.ds(start, ROWS)
            go[rows, columns] = (
                gm[rows, columns] * rms[rows, 0:1] * gate_gain[0:1, columns]
            ).astype(BF16)

    loads["wo"].wait()

    @pl.loop(0, width // GROUP)
    def _(step):
        columns = lanes_of(step, GROUP)
        branch = mm(go[...], wo[columns, :], NT)
        h_next[:, columns] = (h[:, columns] + branch) * live[:, 0:1]

    @pl.when(me < n_tensor - 1)
    def _():
        halo_copy.wait_send()
        for copy in carry_copies:
            copy.wait_send()


def backward_kernel(
    n_tensor,
    n_blocks,
    head_size,
    gh,
    h,
    gain,
    tap_x,
    tap_b,
    aneg,
    skip,
    gate_gain,
    live,
    spread,
    select,
    collect,
    nx,
    gate,
    xraw,
    braw,
    xc,
    bc,
    dtp,
    mixed,
    states,
    rms,
    wz_in,
    wx_in,
    wn_in,
    wo_in,
    gh_next,
    g_wz,
    g_wx,
    g_wo,
    g_narrow,
    g_small,
    wz,
    wx,
    wn,
    wo,
    wbc,
    wdt,
    g_branch,
    g_branch_t,
    normed_t,
    dt,
    run,
    run_t,
    step_two,
    grow_two,
    keep_two,
    decay,
    pair_t,
    g_pair_t,
    gq,
    gb,
    pz,
    px,
    pb,
    pd,
    fresh,
    d_states,
    carry_out,
    carry_in,
    g_heads,
    along,
    direct,
    g_run,
    d_b,
    d_c,
    gn,
    g_gain,
    w_sem,
    halo_send,
    halo_recv,
    carry_send,
    carry_recv,
):
    me = lax.axis_index("tensor")
    tokens, width = h.shape
    inner = gate.shape[1]
    state = fresh.shape[1]
    groups = inner // GROUP
    per_group = GROUP // head_size

    loads = {
        "wo": pltpu.make_async_copy(wo_in, wo, w_sem.at[0]),
        "wz": pltpu.make_async_copy(wz_in, wz, w_sem.at[1]),
        "wx": pltpu.make_async_copy(wx_in, wx, w_sem.at[2]),
        "wn": pltpu.make_async_copy(wn_in, wn, w_sem.at[3]),
    }
    for load in loads.values():
        load.start()

    barrier = pltpu.get_barrier_semaphore()

    @pl.when(me < n_tensor - 1)
    def _():
        pl.semaphore_signal(
            barrier, inc=1, device_id={"tensor": me + 1}, device_id_type=pl.DeviceIdType.MESH
        )

    @pl.when(me > 0)
    def _():
        pl.semaphore_wait(barrier, 1)

    previous = lax.rem(me + n_tensor - 1, n_tensor)
    carry_copies = [
        pltpu.make_async_remote_copy(
            src_ref=carry_out.at[group],
            dst_ref=carry_in.at[group],
            send_sem=carry_send.at[group],
            recv_sem=carry_recv.at[group],
            device_id={"tensor": previous},
            device_id_type=pl.DeviceIdType.MESH,
        )
        for group in range(groups)
    ]
    halo_copies = [
        pltpu.make_async_remote_copy(
            src_ref=buffer.at[pl.ds(0, PAD), :],
            dst_ref=buffer.at[pl.ds(tokens, PAD), :],
            send_sem=halo_send.at[index],
            recv_sem=halo_recv.at[index],
            device_id={"tensor": previous},
            device_id_type=pl.DeviceIdType.MESH,
        )
        for index, buffer in enumerate((gq, gb))
    ]

    @pl.loop(0, tokens // ROWS)
    def _(step):
        rows = pl.ds(pl.multiple_of(step * ROWS, ROWS), ROWS)
        low = (gh[rows, :] * live[rows, 0:1]).astype(BF16)
        g_branch[rows, :] = low
        columns = lanes_of(step, ROWS)
        g_branch_t[:, columns] = low.T
        normed_t[:, columns] = nx[pl.ds(pl.multiple_of(PAD + step * ROWS, PAD), ROWS), :].T

    for block in range(n_blocks):
        step_terms(
            dtp, live, aneg, dt, run, run_t, step_two, grow_two, keep_two, decay, spread, block
        )

    at = small_rows(width, inner, state)

    def put_small(name, row, tile, values):
        for lane in range(0, values.shape[1], LANES):
            g_small[pl.ds(at[name] + row + tile + lane // LANES, 1), :] = values[:, lane : lane + LANES]

    loads["wo"].wait()
    along[...] = jnp.zeros_like(along)

    @pl.loop(0, groups)
    def _(group):
        columns = lanes_of(group, GROUP)
        gained = jnp.zeros((1, GROUP), F32)
        gq[pl.ds(0, tokens), columns] = mm(g_branch[...], wo[:, columns])
        for start in range(0, tokens, ROWS):
            rows = pl.ds(start, ROWS)
            gate_in = gate[rows, columns]
            gated = mixed[rows, columns] * gate_in * jax.nn.sigmoid(gate_in)
            scaled = gated * rms[rows, 0:1]
            px[rows, columns] = (scaled * gate_gain[0:1, columns]).astype(BF16)
            g_gated = gq[rows, columns]
            gained = gained + jnp.sum(g_gated * scaled, axis=0, keepdims=True)
            back = g_gated * gate_gain[0:1, columns]
            gq[rows, columns] = back
            product = back * gated
            for lane in range(0, GROUP, LANES):
                along[rows, :] += product[:, lane : lane + LANES]
        put_small("gate_gain", 0, group * (GROUP // LANES), gained)
        g_wo[:, columns] = mm(g_branch_t[...], px[:, columns]).astype(BF16)

    along[...] = jnp.broadcast_to(
        jnp.sum(along[...], axis=-1, keepdims=True) / inner, along.shape
    )
    loads["wz"].wait()

    @pl.loop(0, groups)
    def _(group):
        columns = lanes_of(group, GROUP)
        for start in range(0, tokens, ROWS):
            rows = pl.ds(start, ROWS)
            gate_in = gate[rows, columns]
            sig = jax.nn.sigmoid(gate_in)
            act = gate_in * sig
            here = mixed[rows, columns]
            scale = rms[rows, 0:1]
            g_mix = scale * gq[rows, columns] - here * act * (scale * scale * scale * along[rows, 0:1])
            gq[rows, columns] = g_mix * act
            pz[rows, columns] = (g_mix * here * sig * (1.0 + gate_in * (1.0 - sig))).astype(BF16)
        g_wz[:, columns] = mm(normed_t[...], pz[:, columns]).astype(BF16)

    row_id = lax.broadcasted_iota(jnp.int32, (SCAN_BLOCK, SCAN_BLOCK), 0)
    col_id = lax.broadcasted_iota(jnp.int32, (SCAN_BLOCK, SCAN_BLOCK), 1)
    head_of = lax.broadcasted_iota(jnp.int32, (SCAN_BLOCK, GROUP), 1) // head_size
    for block in range(n_blocks):
        rows = pl.ds(block * SCAN_BLOCK, SCAN_BLOCK)
        scores = mm(bc[rows, :state], bc[rows, state:], NT)
        pair_t[block] = jnp.where(row_id <= col_id, scores, 0.0)
        c_rows = bc[rows, state:].astype(F32).T.astype(BF16)

        @pl.loop(0, groups)
        def _(group):
            columns = lanes_of(group, GROUP)
            grown = mm(grow_two[block], spread[:, columns])
            fresh[block, :, columns] = mm(c_rows, (gq[rows, columns] * grown).astype(BF16))

    for group in range(groups):
        columns = pl.ds(group * GROUP, GROUP)

        @pl.when(me < n_tensor - 1)
        def _():
            carry_copies[group].wait_recv()
            d_states[n_blocks, :, columns] = carry_in[group].astype(F32)

        @pl.when(me == n_tensor - 1)
        def _():
            d_states[n_blocks, :, columns] = jnp.zeros((state, GROUP), F32)

        for block in reversed(range(n_blocks)):
            d_states[block, :, columns] = (
                d_states[block + 1, :, columns] * decay[block, 0:1, columns]
                + fresh[block, :, columns]
            )
        carry_out[group] = d_states[0, :, columns].astype(BF16)

        @pl.when(me > 0)
        def _():
            carry_copies[group].start()

    g_heads[...] = jnp.zeros_like(g_heads)
    for block in range(n_blocks):
        rows = pl.ds(block * SCAN_BLOCK, SCAN_BLOCK)
        g_pair_t[...] = jnp.zeros_like(g_pair_t)
        d_b[...] = jnp.zeros_like(d_b)
        d_c[...] = jnp.zeros_like(d_c)
        direct[...] = jnp.zeros_like(direct)
        g_run[...] = jnp.zeros_like(g_run)

        @pl.loop(0, groups)
        def _(group):
            columns = lanes_of(group, GROUP)
            sizes = mm(step_two[block], spread[:, columns])
            grown = mm(grow_two[block], spread[:, columns])
            keeps = mm(keep_two[block], spread[:, columns])
            x_here = xc[rows, columns].astype(F32)
            stepped = (x_here * sizes).astype(BF16)
            g_out = gq[rows, columns]
            g_low = g_out.astype(BF16)
            rolled = pltpu.roll(run[block], lax.rem(LANES - per_group * group, LANES), 1)
            d_here = d_states[block + 1, :, columns].astype(BF16)
            d_x = keeps * mm(bc[rows, :state], d_here)
            d_b[...] += mm((x_here * sizes * keeps).astype(BF16), d_here, NT)
            d_c[...] += mm(
                (g_out * grown).astype(BF16), states[block, :, columns].astype(BF16), NT
            )
            for head in range(per_group):
                spread_out = (
                    run_t[block, pl.ds(per_group * group + head, 1), :] - rolled[:, head : head + 1]
                )
                factor = jnp.exp2(jnp.minimum(spread_out, 0.0))
                mixing = (pair_t[block] * factor).astype(BF16)
                g_one = jnp.where(head_of == head, g_low, jnp.zeros_like(g_low))
                d_x = d_x + mm(mixing, g_one)
                g_pair_t[...] += mm(stepped, g_one, NT) * factor
            skipped = skip[0:1, columns]
            toward = g_out * (mixed[rows, columns] - skipped * x_here) - stepped.astype(F32) * d_x
            for values, target in ((d_x * x_here, direct), (toward, g_run)):
                high, low = halves(values)
                target[...] += mm(high, collect[columns, :]) + mm(low, collect[columns, :])
            skip_sum = jnp.broadcast_to(
                jnp.sum(g_out * x_here, axis=0, keepdims=True), (8, GROUP)
            )
            high, low = halves(skip_sum)
            g_heads[2:3, :] += (mm(high, collect[columns, :]) + mm(low, collect[columns, :]))[0:1, :]
            gq[rows, columns] = sizes * d_x + skipped * g_out

        g_scores = jnp.where(row_id <= col_id, g_pair_t[...], 0.0)
        g_low = g_scores.astype(BF16)
        gb[rows, :state] = d_b[...] + mm(g_low, bc[rows, state:])
        gb[rows, state:] = d_c[...] + mm(g_scores.T.astype(BF16), bc[rows, :state])
        end_sum = jnp.broadcast_to(
            jnp.sum(d_states[block + 1] * states[block + 1], axis=0, keepdims=True), (8, inner)
        )
        high, low = halves(end_sum)
        at_end = (mm(high, collect[...]) + mm(low, collect[...]))[0:1, :]
        later = (row_id <= col_id).astype(F32)
        g_rate = exact(later, g_run[...]) + at_end
        value = dtp[rows, :]
        g_dt = (aneg[0:1, :] * g_rate + direct[...]) * live[rows, :] * jax.nn.sigmoid(value)
        pd[rows, :] = g_dt.astype(BF16)
        g_heads[0:1, :] += jnp.sum(g_dt, axis=0, keepdims=True)
        g_heads[1:2, :] += jnp.sum(g_rate * dt[block], axis=0, keepdims=True) * aneg[0:1, :]

    def before_conv(taps, raw, grad, columns):
        for start in range(0, tokens, ROWS):
            rows = pl.ds(start, ROWS)
            before = conv_rows(raw, taps, start, columns)
            sig = jax.nn.sigmoid(before)
            grad[rows, columns] = grad[rows, columns] * (sig * (1.0 + before * (1.0 - sig)))

    def through_conv(taps, raw, grad, columns, name, tile, low):
        sums = [jnp.zeros((1, GROUP), F32) for tap in range(WIDTH + 1)]
        for start in range(0, tokens, ROWS):
            total = jnp.zeros((ROWS, GROUP), F32)
            here = grad[pl.ds(start, ROWS), columns]
            for tap in range(WIDTH):
                shift = WIDTH - 1 - tap
                total = total + taps[tap : tap + 1, columns] * grad[pl.ds(start + shift, ROWS), columns]
                sums[tap] = sums[tap] + jnp.sum(
                    here * raw[pl.ds(PAD - shift + start, ROWS), columns], axis=0, keepdims=True
                )
            sums[WIDTH] = sums[WIDTH] + jnp.sum(here, axis=0, keepdims=True)
            low[pl.ds(start, ROWS), columns] = total.astype(BF16)
        for tap in range(WIDTH + 1):
            put_small(name, tap * (grad.shape[1] // LANES), tile, sums[tap])

    for step in range(bc.shape[1] // GROUP):
        before_conv(tap_b, braw, gb, pl.ds(step * GROUP, GROUP))

    @pl.loop(0, groups)
    def _(step):
        before_conv(tap_x, xraw, gq, lanes_of(step, GROUP))

    @pl.when(me > 0)
    def _():
        for copy in halo_copies:
            copy.start()

    g_narrow[:, 2 * state : 2 * state + LANES] = mm(normed_t[...], pd[...]).astype(BF16)
    g_narrow[:, 2 * state + LANES :] = jnp.zeros((width, LANES), BF16)
    loads["wx"].wait()
    loads["wn"].wait()
    split_narrow(wn, select, wbc, wdt)

    @pl.when(me < n_tensor - 1)
    def _():
        for copy in halo_copies:
            copy.wait_recv()

    @pl.when(me == n_tensor - 1)
    def _():
        for buffer in (gq, gb):
            buffer[pl.ds(tokens, PAD), :] = jnp.zeros((PAD, buffer.shape[1]), F32)

    for step in range(bc.shape[1] // GROUP):
        columns = pl.ds(step * GROUP, GROUP)
        through_conv(tap_b, braw, gb, columns, "tap_b", step * (GROUP // LANES), pb)
        g_narrow[:, columns] = mm(normed_t[...], pb[:, columns]).astype(BF16)

    @pl.loop(0, groups)
    def _(step):
        columns = lanes_of(step, GROUP)
        through_conv(tap_x, xraw, gq, columns, "tap_x", step * (GROUP // LANES), px)
        g_wx[:, columns] = mm(normed_t[...], px[:, columns]).astype(BF16)

    @pl.loop(0, width // GROUP)
    def _(step):
        columns = lanes_of(step, GROUP)
        gn[:, columns] = (
            mm(pz[...], wz[columns, :], NT)
            + mm(px[...], wx[columns, :], NT)
            + mm(pb[...], wbc[columns, :], NT)
            + mm(pd[...], wdt[columns, :], NT)
        )

    g_gain[...] = jnp.zeros_like(g_gain)
    g_small[pl.ds(at["heads"], 8), :] = g_heads[...]
    g_small[pl.ds(at["gain"], 8), :] = jnp.zeros((8, LANES), F32)

    @pl.loop(0, tokens // ROWS)
    def _(step):
        rows = pl.ds(pl.multiple_of(step * ROWS, ROWS), ROWS)
        values = h[rows, :]
        inv = lax.rsqrt(jnp.mean(values * values, axis=-1, keepdims=True) + EPS)
        g_normed = gn[rows, :]
        g_gain[0:1, :] += jnp.sum(g_normed * values * inv, axis=0, keepdims=True)
        scaled = g_normed * gain[0:1, :]
        along_h = jnp.mean(scaled * values, axis=-1, keepdims=True)
        gh_next[rows, :] = (
            gh[rows, :] * live[rows, 0:1] + inv * scaled - values * (inv * inv * inv * along_h)
        )

    put_small("gain", 0, 0, g_gain[0:1, :])

    @pl.when(me > 0)
    def _():
        for copy in halo_copies:
            copy.wait_send()
        for copy in carry_copies:
            copy.wait_send()


VMEM = pl.BlockSpec(memory_space=pltpu.VMEM)
ANY = pl.BlockSpec(memory_space=pl.ANY)


def shaped(shape, dtype=F32):
    return jax.ShapeDtypeStruct(shape, dtype)


def weight_scratch(width, inner, state, narrow):
    return [
        pltpu.VMEM((width, inner), BF16),
        pltpu.VMEM((width, inner), BF16),
        pltpu.VMEM((width, narrow), BF16),
        pltpu.VMEM((width, inner), BF16),
        pltpu.VMEM((width, 2 * state), BF16),
        pltpu.VMEM((width, LANES), BF16),
    ]


def block_scratch(n_blocks, inner):
    return [
        pltpu.VMEM((n_blocks, SCAN_BLOCK, LANES), F32),
        pltpu.VMEM((n_blocks, SCAN_BLOCK, LANES), F32),
        pltpu.VMEM((n_blocks, LANES, SCAN_BLOCK), F32),
        pltpu.VMEM((n_blocks, SCAN_BLOCK, 2 * LANES), BF16),
        pltpu.VMEM((n_blocks, SCAN_BLOCK, 2 * LANES), BF16),
        pltpu.VMEM((n_blocks, SCAN_BLOCK, 2 * LANES), BF16),
        pltpu.VMEM((n_blocks, 8, inner), F32),
    ]


def layer_forward(n_tensor, head_size, state, h, small, weights):
    tokens, width = h.shape
    inner = small["skip"].shape[1]
    n_blocks = tokens // SCAN_BLOCK
    groups = inner // GROUP
    operands = [h] + [
        small[name]
        for name in ("gain", "tap_x", "tap_b", "dt_bias", "aneg", "skip", "gate_gain", "live", "spread", "select")
    ]
    return pl.pallas_call(
        partial(forward_kernel, n_tensor, n_blocks, head_size),
        out_shape=[
            shaped((tokens, width)),
            shaped((PAD + tokens, width), BF16),
            shaped((tokens, inner)),
            shaped((PAD + tokens, inner)),
            shaped((PAD + tokens, 2 * state)),
            shaped((tokens, inner), BF16),
            shaped((tokens, 2 * state), BF16),
            shaped((tokens, LANES)),
            shaped((tokens, inner)),
            shaped((n_blocks + 1, state, inner)),
            shaped((tokens, LANES)),
        ],
        in_specs=[VMEM] * len(operands) + [ANY] * 4,
        out_specs=[VMEM] * 11,
        scratch_shapes=weight_scratch(width, inner, state, weights[2].shape[1])
        + [pltpu.VMEM((PAD, width), F32)]
        + block_scratch(n_blocks, inner)
        + [
            pltpu.VMEM((n_blocks, SCAN_BLOCK, SCAN_BLOCK), F32),
            pltpu.VMEM((n_blocks, state, inner), F32),
            pltpu.VMEM((groups, state, GROUP), BF16),
            pltpu.VMEM((groups, state, GROUP), BF16),
            pltpu.VMEM((tokens, inner), F32),
            pltpu.VMEM((tokens, inner), BF16),
            pltpu.VMEM((tokens, LANES), F32),
            pltpu.SemaphoreType.DMA((4,)),
            pltpu.SemaphoreType.DMA,
            pltpu.SemaphoreType.DMA,
            pltpu.SemaphoreType.DMA((groups,)),
            pltpu.SemaphoreType.DMA((groups,)),
        ],
        compiler_params=pltpu.CompilerParams(
            collective_id=1, has_side_effects=True, vmem_limit_bytes=60 * 1024 * 1024
        ),
        name="layer_forward",
    )(*operands, *weights)


def layer_backward(n_tensor, head_size, state, gh, h, small, saved, weights):
    tokens, width = h.shape
    inner = small["skip"].shape[1]
    n_blocks = tokens // SCAN_BLOCK
    groups = inner // GROUP
    operands = (
        [gh, h]
        + [
            small[name]
            for name in ("gain", "tap_x", "tap_b", "aneg", "skip", "gate_gain", "live", "spread", "select", "collect")
        ]
        + list(saved)
    )
    return pl.pallas_call(
        partial(backward_kernel, n_tensor, n_blocks, head_size),
        out_shape=[
            shaped((tokens, width)),
            shaped((width, inner), BF16),
            shaped((width, inner), BF16),
            shaped((width, inner), BF16),
            shaped((width, 2 * state + 2 * LANES), BF16),
            shaped((small_rows(width, inner, state)["all"], LANES)),
        ],
        in_specs=[VMEM] * len(operands) + [ANY] * 4,
        out_specs=[VMEM] * 6,
        scratch_shapes=weight_scratch(width, inner, state, weights[2].shape[1])
        + [
            pltpu.VMEM((tokens, width), BF16),
            pltpu.VMEM((width, tokens), BF16),
            pltpu.VMEM((width, tokens), BF16),
        ]
        + block_scratch(n_blocks, inner)
        + [
            pltpu.VMEM((n_blocks, SCAN_BLOCK, SCAN_BLOCK), F32),
            pltpu.VMEM((SCAN_BLOCK, SCAN_BLOCK), F32),
            pltpu.VMEM((tokens + PAD, inner), F32),
            pltpu.VMEM((tokens + PAD, 2 * state), F32),
            pltpu.VMEM((tokens, inner), BF16),
            pltpu.VMEM((tokens, inner), BF16),
            pltpu.VMEM((tokens, 2 * state), BF16),
            pltpu.VMEM((tokens, LANES), BF16),
            pltpu.VMEM((n_blocks, state, inner), F32),
            pltpu.VMEM((n_blocks + 1, state, inner), F32),
            pltpu.VMEM((groups, state, GROUP), BF16),
            pltpu.VMEM((groups, state, GROUP), BF16),
            pltpu.VMEM((8, LANES), F32),
            pltpu.VMEM((tokens, LANES), F32),
            pltpu.VMEM((SCAN_BLOCK, LANES), F32),
            pltpu.VMEM((SCAN_BLOCK, LANES), F32),
            pltpu.VMEM((SCAN_BLOCK, state), F32),
            pltpu.VMEM((SCAN_BLOCK, state), F32),
            pltpu.VMEM((tokens, width), F32),
            pltpu.VMEM((8, width), F32),
            pltpu.SemaphoreType.DMA((4,)),
            pltpu.SemaphoreType.DMA((2,)),
            pltpu.SemaphoreType.DMA((2,)),
            pltpu.SemaphoreType.DMA((groups,)),
            pltpu.SemaphoreType.DMA((groups,)),
        ],
        compiler_params=pltpu.CompilerParams(
            collective_id=2, has_side_effects=True, vmem_limit_bytes=60 * 1024 * 1024
        ),
        name="layer_backward",
    )(*operands, *weights)


def reduce_kernel(layers, part, state, *refs):
    n_units = 3 * (part // LANES) + 1
    wide = refs[: 4 * layers]
    small = refs[4 * layers]
    out_wide = refs[4 * layers + 1 : 4 * layers + 4]
    out_narrow, out_small = refs[4 * layers + 4 : 4 * layers + 6]
    total = layers * n_units
    rest = refs[4 * layers + 6 :]
    first, second, third, fourth = (rest[k * total : (k + 1) * total] for k in range(4))
    (small_core, small_x, small_y, small_z, sum_core, sum_x) = rest[4 * total : 4 * total + 6]
    sems = rest[4 * total + 6 :]
    send0, recv0, send1, recv1, send2, recv2, send3, recv3, send_n, recv_n, send_s, recv_s = sems

    n_dp, n_tensor = lax.axis_size("dp"), lax.axis_size("tensor")
    dp, tensor = lax.axis_index("dp"), lax.axis_index("tensor")
    core, x = lax.rem(tensor, 2), tensor // 2
    y, z = lax.rem(dp, 2), dp // 2
    depth = n_dp // 2
    rows = out_narrow.shape[2]
    to_core = {"tensor": tensor + 1 - 2 * core}
    to_x = {"tensor": lax.rem(tensor + 2, n_tensor)}
    to_y = {"dp": dp + 1 - 2 * y}
    to_z = [{"dp": lax.rem(z + k, depth) * 2 + y} for k in range(1, depth)]
    to_diagonal = {"tensor": n_tensor - 1 - tensor}

    barrier = pltpu.get_barrier_semaphore()
    partners = [to_core, to_x, to_diagonal, to_y] + to_z
    for partner in partners:
        pl.semaphore_signal(barrier, inc=1, device_id=partner, device_id_type=pl.DeviceIdType.MESH)
    pl.semaphore_wait(barrier, len(partners))

    def remote(source, target, send, recv, device):
        return pltpu.make_async_remote_copy(
            src_ref=source,
            dst_ref=target,
            send_sem=send,
            recv_sem=recv,
            device_id=device,
            device_id_type=pl.DeviceIdType.MESH,
        )

    units = []
    for layer in range(layers):
        for member in (2, 0, 1, 3):
            block = LANES if member == 3 else part
            for column in range(0, block, LANES):
                units.append((layer, member, block, column))

    def plan(index):
        layer, member, block, column = units[index]
        source = wide[4 * layer + member]
        r0, r1, r2, r3 = first[index], second[index], third[index], fourth[index]
        x_first = index % 2 == 0

        def lanes(side, which):
            return pl.ds(pl.multiple_of((2 * side + which) * block + column, LANES), LANES)

        copies0 = [
            remote(
                source.at[:, :, :, lanes(side, 1 - core)],
                r0.at[side],
                send0.at[index, side],
                recv0.at[index, side],
                to_core,
            )
            for side in range(2)
        ]
        if x_first:
            copy1 = remote(r0.at[1 - x], r1, send1.at[index], recv1.at[index], to_x)
            copy2 = remote(r1.at[:, 1 - y], r2, send2.at[index], recv2.at[index], to_y)
        else:
            copy1 = remote(r0.at[:, :, 1 - y], r1, send1.at[index], recv1.at[index], to_y)
            copy2 = remote(r1.at[1 - x], r2, send2.at[index], recv2.at[index], to_x)
        copies3 = [
            remote(
                r2.at[lax.rem(z + k, depth)],
                r3.at[k - 1],
                send3.at[index, k - 1],
                recv3.at[index, k - 1],
                to_z[k - 1],
            )
            for k in range(1, depth)
        ]

        def begin():
            for copy in copies0:
                copy.start()

        def after_core():
            for copy in copies0:
                copy.wait_recv()

            @pl.loop(0, 2 * depth)
            def _(step):
                high, low = step // 2, lax.rem(step, 2)
                for side in range(2):
                    r0[side, high, low] = (
                        r0[side, high, low].astype(F32)
                        + source[high, low, :, lanes(side, core)].astype(F32)
                    ).astype(BF16)

            copy1.start()

        def after_first():
            copy1.wait_recv()

            @pl.loop(0, depth)
            def _(high):
                for side in range(2):
                    if x_first:
                        r1[high, side] = (
                            r1[high, side].astype(F32) + r0[x, high, side].astype(F32)
                        ).astype(BF16)
                    else:
                        r1[side, high] = (
                            r1[side, high].astype(F32) + r0[side, high, y].astype(F32)
                        ).astype(BF16)

            copy2.start()

        def after_second():
            copy2.wait_recv()

            @pl.loop(0, depth)
            def _(high):
                mine = r1[high, y] if x_first else r1[x, high]
                r2[high] = (r2[high].astype(F32) + mine.astype(F32)).astype(BF16)

            for copy in copies3:
                copy.start()

        def finish():
            value = r2[z].astype(F32)
            for k, copy in enumerate(copies3):
                copy.wait_recv()
                value = value + r3[k].astype(F32)
            if member == 3:
                out_narrow[layer, tensor] = value
            else:
                out_wide[member][layer, :, column : column + LANES] = value

        def drain():
            for copy in copies0 + [copy1, copy2] + copies3:
                copy.wait_send()

        return begin, after_core, after_first, after_second, finish, drain

    plans = [plan(index) for index in range(total)]

    small_first = remote(small, small_core, send_s.at[0], recv_s.at[0], to_core)
    small_second = remote(sum_core, small_x, send_s.at[1], recv_s.at[1], to_x)
    small_third = remote(sum_x, small_y, send_s.at[2], recv_s.at[2], to_y)
    small_last = [
        remote(
            small_z.at[z], small_z.at[z], send_s.at[2 + k], recv_s.at[2 + k], to_z[k - 1]
        )
        for k in range(1, depth)
    ]

    def small_step(step):
        if step == 0:
            small_first.start()
        elif step == 1:
            small_first.wait_recv()
            sum_core[...] = small[...] + small_core[...]
            small_second.start()
        elif step == 2:
            small_second.wait_recv()
            sum_x[...] = sum_core[...] + small_x[...]
            small_third.start()
        elif step == 3:
            small_third.wait_recv()
            small_z[z] = sum_x[...] + small_y[...]
            for copy in small_last:
                copy.start()
        elif step == 4:
            for copy in small_last:
                copy.wait_recv()
            value = small_z[0]
            for k in range(1, depth):
                value = value + small_z[k]
            out_small[...] = value

    ahead = 2
    for index in range(min(ahead, total)):
        plans[index][0]()
    for step in range(total + 6):
        small_step(step)
        if step + ahead < total:
            plans[step + ahead][0]()
        for stage, delay in ((1, 0), (2, 2), (3, 4), (4, 6)):
            if 0 <= step - delay < total:
                plans[step - delay][stage]()

    narrow_copies = [
        remote(
            out_narrow.at[:, tensor],
            out_narrow.at[:, tensor],
            send_n.at[k - 1],
            recv_n.at[k - 1],
            {"tensor": lax.rem(tensor + k, n_tensor)},
        )
        for k in range(1, n_tensor)
    ]
    for copy in narrow_copies:
        copy.start()
    for copy in narrow_copies:
        copy.wait_recv()
    for entry in plans:
        entry[5]()
    for copy in [small_first, small_second, small_third] + small_last + narrow_copies:
        copy.wait_send()


def reduce_gradients(n_dp, n_tensor, part, state, wide, small):
    layers = len(wide)
    rows = wide[0][0].shape[0] // n_dp
    depth = n_dp // 2
    operands = [
        array.reshape(depth, 2, rows, array.shape[1]) for members in wide for array in members
    ] + [small]
    total = layers * (3 * (part // LANES) + 1)
    scratch = [pltpu.VMEM((2, depth, 2, rows, LANES), BF16)] * total
    for index in range(total):
        shape = (depth, 2, rows, LANES) if index % 2 == 0 else (2, depth, rows, LANES)
        scratch.append(pltpu.VMEM(shape, BF16))
    scratch += [pltpu.VMEM((depth, rows, LANES), BF16)] * total
    scratch += [pltpu.VMEM((depth - 1, rows, LANES), BF16)] * total
    scratch += [pltpu.VMEM(small.shape, F32)] * 3
    scratch += [pltpu.VMEM((depth,) + small.shape, F32)]
    scratch += [pltpu.VMEM(small.shape, F32)] * 2
    pairs = ((total, 2), (total,), (total,), (total, depth - 1), (n_tensor - 1,), (2 + depth,))
    for shape in pairs:
        scratch += [pltpu.SemaphoreType.DMA(shape)] * 2
    return pl.pallas_call(
        partial(reduce_kernel, layers, part, state),
        out_shape=[shaped((layers, rows, part))] * 3
        + [shaped((layers, n_tensor, rows, LANES)), shaped(small.shape)],
        in_specs=[VMEM] * len(operands),
        out_specs=[VMEM] * 5,
        scratch_shapes=scratch,
        compiler_params=pltpu.CompilerParams(
            collective_id=3, has_side_effects=True, vmem_limit_bytes=60 * 1024 * 1024
        ),
        name="reduce_gradients",
    )(*operands)


def gather_steps(n_dp, n_tensor, blocks, wholes, width, sems, x_first):
    send_z, recv_z, send_n, recv_n, own = sems
    dp, tensor = lax.axis_index("dp"), lax.axis_index("tensor")
    core, x = lax.rem(tensor, 2), tensor // 2
    y, z = lax.rem(dp, 2), dp // 2
    depth = n_dp // 2
    block, start, full = width
    to_core = {"tensor": tensor + 1 - 2 * core}
    to_x = {"tensor": lax.rem(tensor + 2, n_tensor)}
    to_y = {"dp": dp + 1 - 2 * y}

    def lanes(side):
        return pl.ds(pl.multiple_of((2 * side + core) * full + start, LANES), block)

    def remote(source, target, send, recv, device):
        return pltpu.make_async_remote_copy(
            src_ref=source,
            dst_ref=target,
            send_sem=send,
            recv_sem=recv,
            device_id=device,
            device_id_type=pl.DeviceIdType.MESH,
        )

    def same(place, slot, device):
        return remote(place, place, send_n.at[slot], recv_n.at[slot], device)

    mine = blocks.at[:, pl.ds(start, block)]
    keep = pltpu.make_async_copy(mine, wholes.at[z, y, :, lanes(x)], own)
    along_z = [
        remote(
            mine,
            wholes.at[z, y, :, lanes(x)],
            send_z.at[k - 1],
            recv_z.at[k - 1],
            {"dp": lax.rem(z + k, depth) * 2 + y},
        )
        for k in range(1, depth)
    ]
    if x_first:
        one = [same(wholes.at[:, y, :, lanes(x)], 0, to_x)]
        two = [same(wholes.at[:, y, :, lanes(side)], 1 + side, to_y) for side in range(2)]
    else:
        one = [same(wholes.at[:, y, :, lanes(x)], 0, to_y)]
        two = [same(wholes.at[:, :, :, lanes(x)], 1, to_x)]
    last = [same(wholes.at[:, :, :, lanes(side)], 3 + side, to_core) for side in range(2)]

    def begin():
        keep.start()
        for copy in along_z:
            copy.start()

    def hand_on(before, after):
        def step():
            for copy in before:
                copy.wait_recv()
            for copy in after:
                copy.start()

        return step

    def first():
        keep.wait()
        hand_on(along_z, one)()

    def finish():
        for copy in last:
            copy.wait_recv()
        for copy in along_z + one + two + last:
            copy.wait_send()

    return [begin, first, hand_on(one, two), hand_on(two, last), finish]


def gather_partners(n_dp, n_tensor):
    dp, tensor = lax.axis_index("dp"), lax.axis_index("tensor")
    core, y, z = lax.rem(tensor, 2), lax.rem(dp, 2), dp // 2
    depth = n_dp // 2
    return [
        {"tensor": tensor + 1 - 2 * core},
        {"tensor": lax.rem(tensor + 2, n_tensor)},
        {"dp": dp + 1 - 2 * y},
    ] + [{"dp": lax.rem(z + k, depth) * 2 + y} for k in range(1, depth)]


def gather_kernel(layers, part, *refs):
    arranged = refs[0]
    blocks = refs[1:5]
    hidden = refs[5]
    wholes = refs[6 : 6 + 4 * layers]
    send_z, recv_z, send_n, recv_n, own, deal_send, deal_recv, deal_own = refs[6 + 4 * layers :]
    n_dp, n_tensor = lax.axis_size("dp"), lax.axis_size("tensor")
    dp, tensor = lax.axis_index("dp"), lax.axis_index("tensor")
    parts = n_dp // n_tensor
    runner = dp // parts

    barrier = pltpu.get_barrier_semaphore()

    def greet(device):
        pl.semaphore_signal(barrier, inc=1, device_id=device, device_id_type=pl.DeviceIdType.MESH)

    partners = gather_partners(n_dp, n_tensor)
    for partner in partners:
        greet(partner)
    for k in range(parts):
        for other in range(n_tensor):
            source = tensor * parts + k

            @pl.when((source != dp) | (other != tensor))
            def _():
                greet({"dp": source, "tensor": other})

    with_self = (runner == tensor).astype(jnp.int32)
    pl.semaphore_wait(barrier, len(partners) + n_dp - with_self)

    deal_keep = pltpu.make_async_copy(
        arranged.at[dp], hidden.at[lax.rem(dp, parts), tensor], deal_own
    )
    deal = [
        pltpu.make_async_remote_copy(
            src_ref=arranged.at[j],
            dst_ref=hidden.at[lax.rem(dp, parts), tensor],
            send_sem=deal_send.at[j],
            recv_sem=deal_recv.at[lax.rem(dp, parts), tensor],
            device_id={"dp": j, "tensor": runner},
            device_id_type=pl.DeviceIdType.MESH,
        )
        for j in range(n_dp)
    ]
    for j in range(n_dp):
        remote_here = (j != dp) | (runner != tensor)

        @pl.when(remote_here)
        def _():
            deal[j].start()

    @pl.when(runner == tensor)
    def _():
        deal_keep.start()

    plans = []
    for layer in range(layers):
        for member in range(4):
            full = LANES if member == 2 else part
            for start in range(0, full, LANES):
                index = len(plans)
                plans.append(
                    gather_steps(
                        n_dp,
                        n_tensor,
                        blocks[member].at[layer],
                        wholes[4 * layer + member],
                        (LANES, start, full),
                        [sem.at[index] for sem in (send_z, recv_z, send_n, recv_n, own)],
                        index % 2 == 0,
                    )
                )
    total = len(plans)
    ahead = 3
    for index in range(min(ahead, total)):
        plans[index][0]()
    for step in range(total + 6):
        if step + ahead < total:
            plans[step + ahead][0]()
        for stage, delay in ((1, 0), (2, 2), (3, 4), (4, 6)):
            if 0 <= step - delay < total:
                plans[step - delay][stage]()

    for k in range(parts):
        for other in range(n_tensor):

            @pl.when((tensor * parts + k != dp) | (other != tensor))
            def _():
                pltpu.make_async_remote_copy(
                    src_ref=arranged.at[0],
                    dst_ref=hidden.at[k, other],
                    send_sem=deal_send.at[0],
                    recv_sem=deal_recv.at[k, other],
                    device_id={"dp": dp, "tensor": lax.rem(tensor + 1, n_tensor)},
                    device_id_type=pl.DeviceIdType.MESH,
                ).wait_recv()

    for j in range(n_dp):
        remote_here = (j != dp) | (runner != tensor)

        @pl.when(remote_here)
        def _():
            deal[j].wait_send()

    @pl.when(runner == tensor)
    def _():
        deal_keep.wait()


def gather_all(n_dp, n_tensor, arranged, blocks):
    layers, rows, part = blocks[0].shape
    piece, width = arranged.shape[1:]
    depth = n_dp // 2
    total = layers * (3 * (part // LANES) + 1)
    wholes = [
        shaped((depth, 2, rows, n_tensor * block.shape[2]), BF16)
        for layer in range(layers)
        for block in blocks
    ]
    results = pl.pallas_call(
        partial(gather_kernel, layers, part),
        out_shape=[shaped((n_dp // n_tensor, n_tensor, piece, width), BF16)] + wholes,
        in_specs=[ANY] * 5,
        out_specs=[ANY] * (1 + len(wholes)),
        scratch_shapes=[
            pltpu.SemaphoreType.DMA((total, depth - 1)),
            pltpu.SemaphoreType.DMA((total, depth - 1)),
            pltpu.SemaphoreType.DMA((total, 5)),
            pltpu.SemaphoreType.DMA((total, 5)),
            pltpu.SemaphoreType.DMA((total,)),
            pltpu.SemaphoreType.DMA((n_dp,)),
            pltpu.SemaphoreType.DMA((n_dp // n_tensor, n_tensor)),
            pltpu.SemaphoreType.DMA,
        ],
        compiler_params=pltpu.CompilerParams(collective_id=4, has_side_effects=True),
        name="gather_all",
    )(arranged, *blocks)
    tokens = n_dp * piece
    return results[0].reshape(tokens, width), [
        [whole.reshape(n_dp * rows, whole.shape[3]) for whole in results[1 + 4 * layer : 5 + 4 * layer]]
        for layer in range(layers)
    ]


def padded_lanes(values):
    return jnp.pad(values, ((0, 0), (0, LANES - values.shape[1])))


def padded_rows(values):
    return jnp.pad(values, ((0, 8 - values.shape[0]), (0, 0)))


def local(
    hidden_in,
    lengths,
    order,
    in_gain,
    w_z,
    w_x,
    w_bc,
    w_dt,
    conv_x,
    conv_bc,
    dt_bias,
    a_log,
    d_skip,
    gated_gain,
    w_out,
    cotangent,
):
    n_dp = lax.axis_size("dp")
    n_tensor = lax.axis_size("tensor")
    dp_index = lax.axis_index("dp")
    tensor_index = lax.axis_index("tensor")
    piece = hidden_in.shape[2]
    width = hidden_in.shape[3]
    tokens = piece * n_dp
    parts = n_dp // n_tensor
    layers = w_z.shape[0]
    inner = gated_gain.shape[1]
    heads = dt_bias.shape[1]
    head_size = inner // heads
    state = conv_bc.shape[2] // 2
    rows_local = w_z.shape[1]
    part = w_z.shape[2]

    def to_run(values):
        swapped = lax.all_to_all(
            values.reshape(n_tensor, parts, piece, width), "tensor", split_axis=0, concat_axis=0
        )
        return swapped.transpose(1, 0, 2, 3).reshape(tokens, width)

    def to_pieces(values):
        swapped = values.reshape(parts, n_tensor, piece, width).transpose(1, 0, 2, 3)
        return lax.all_to_all(swapped, "tensor", split_axis=0, concat_axis=0).reshape(
            n_dp, piece, width
        )

    seq_length = jnp.take(lengths, jnp.take(order, dp_index))
    arranged = jnp.take(hidden_in, order, axis=0)
    direct = rows_local % 16 == 0 and n_tensor == 4 and n_dp % 2 == 0
    quarter = 2 * state // n_tensor
    narrow = jnp.concatenate(
        [lax.dynamic_slice_in_dim(w_bc, tensor_index * quarter, quarter, 2), w_dt], axis=2
    )
    narrow = jnp.pad(narrow, ((0, 0), (0, 0), (0, LANES - narrow.shape[2])))
    blocks = (w_z, w_x, narrow, w_out)
    if direct:
        hidden, weights = gather_all(n_dp, n_tensor, arranged[:, 0], blocks)
    else:
        dealt = lax.all_to_all(arranged, "dp", split_axis=0, concat_axis=1, tiled=True)
        hidden = to_run(dealt[0])

        def whole(stacked):
            gathered = lax.all_gather(stacked, "dp", axis=1, tiled=True)
            return lax.all_gather(gathered, "tensor", axis=2, tiled=True)

        wholes = [whole(block) for block in blocks]
        weights = [[stacked[layer] for stacked in wholes] for layer in range(layers)]
    hidden = hidden.astype(F32)
    positions = tensor_index * tokens + jnp.arange(tokens)
    live = jnp.broadcast_to((positions < seq_length).astype(F32)[:, None], (tokens, LANES))

    head_ids = jnp.arange(inner) // head_size
    one_hot = (head_ids[:, None] == jnp.arange(LANES)[None, :]).astype(BF16)
    spread = jnp.concatenate([one_hot.T, one_hot.T], axis=0)
    source = jnp.arange(n_tensor * LANES)
    place = jnp.where(
        source % LANES < quarter,
        source // LANES * quarter + source % LANES,
        jnp.where(
            source % LANES < quarter + heads // n_tensor,
            2 * state + source // LANES * (heads // n_tensor) + source % LANES - quarter,
            -1,
        ),
    )
    select = (place[:, None] == jnp.arange(2 * state + LANES)[None, :]).astype(BF16)
    small = []
    for layer in range(layers):
        small.append(
            dict(
                gain=padded_rows(in_gain[layer][None]),
                tap_x=padded_rows(conv_x[layer]),
                tap_b=padded_rows(conv_bc[layer]),
                dt_bias=padded_rows(padded_lanes(dt_bias[layer][None])),
                aneg=padded_rows(padded_lanes(-jnp.exp(a_log[layer])[None])),
                skip=padded_rows(jnp.repeat(d_skip[layer], head_size)[None]),
                gate_gain=padded_rows(gated_gain[layer][None]),
                live=live,
                spread=spread,
                select=select,
                collect=one_hot,
            )
        )

    inputs, kept = [], []
    for layer in range(layers):
        inputs.append(hidden)
        results = layer_forward(n_tensor, head_size, state, hidden, small[layer], weights[layer])
        hidden = results[0]
        kept.append(results[1:])
    block_out = to_pieces(hidden.astype(BF16))[None]

    grad = to_run(cotangent[0]).astype(F32)
    wide_terms = [None] * layers
    small_terms = [None] * layers
    for layer in reversed(range(layers)):
        results = layer_backward(
            n_tensor, head_size, state, grad, inputs[layer], small[layer], kept[layer], weights[layer]
        )
        grad = results[0]
        wide_terms[layer] = results[1:5]
        small_terms[layer] = results[5]

    if direct:
        sum_z, sum_x, sum_out, sum_narrow, sum_small = reduce_gradients(
            n_dp, n_tensor, part, state, wide_terms, jnp.stack(small_terms)
        )
    else:

        def scattered(member):
            blocks = jnp.stack([terms[member] for terms in wide_terms]).astype(F32)
            mine = lax.psum_scatter(blocks, "dp", scatter_dimension=1, tiled=True)
            return lax.psum_scatter(mine, "tensor", scatter_dimension=2, tiled=True)

        sum_z, sum_x, sum_out, narrow = (scattered(member) for member in range(4))
        sum_narrow = lax.all_gather(narrow, "tensor", axis=1)
        sum_small = lax.psum(jnp.stack(small_terms), ("dp", "tensor"))
    sum_bc = jnp.concatenate([sum_narrow[:, 0], sum_narrow[:, 1]], axis=2)
    sum_dt = lax.dynamic_slice_in_dim(
        sum_narrow[:, 2], tensor_index * (heads // n_tensor), heads // n_tensor, 2
    )
    at = small_rows(width, inner, state)

    def taken(name, rows, shape):
        return sum_small[:, at[name] : at[name] + rows].reshape((layers,) + shape)

    returned = lax.all_to_all(
        to_pieces(grad.astype(BF16))[None], "dp", split_axis=1, concat_axis=0, tiled=True
    )
    input_grad = jnp.zeros_like(returned).at[order].set(returned)
    tap_rows = WIDTH + 1
    return (
        block_out,
        input_grad,
        taken("gain", width // LANES, (width,)),
        sum_z,
        sum_x,
        sum_bc,
        sum_dt,
        taken("tap_x", tap_rows * (inner // LANES), (tap_rows, inner)),
        taken("tap_b", tap_rows * (2 * state // LANES), (tap_rows, 2 * state)),
        sum_small[:, at["heads"], :heads],
        sum_small[:, at["heads"] + 1, :heads],
        sum_small[:, at["heads"] + 2, :heads],
        taken("gate_gain", inner // LANES, (inner,)),
        sum_out,
    )


def solution(mesh):
    return jax.shard_map(
        local,
        mesh=mesh,
        in_specs=(
            P(None, "dp", "tensor", None),
            P(),
            P(),
            P(),
            P(None, "dp", "tensor"),
            P(None, "dp", "tensor"),
            P(None, "dp", None),
            P(None, "dp", "tensor"),
            P(),
            P(),
            P(),
            P(),
            P(),
            P(),
            P(None, "dp", "tensor"),
            P("dp", None, "tensor", None),
        ),
        out_specs=(
            P("dp", None, "tensor", None),
            P(None, "dp", "tensor", None),
            P(),
            P(None, "dp", "tensor"),
            P(None, "dp", "tensor"),
            P(None, "dp", None),
            P(None, "dp", "tensor"),
            P(),
            P(),
            P(),
            P(),
            P(),
            P(),
            P(None, "dp", "tensor"),
        ),
        check_vma=False,
    )
```

```python
from functools import partial
from types import SimpleNamespace

import jax
import jax.numpy as jnp
from jax import lax
from jax.experimental import pallas as pl
from jax.experimental.pallas import tpu as pltpu
from jax.sharding import PartitionSpec as P

SCAN_BLOCK = 256
HALF = SCAN_BLOCK // 2
EPS = 1e-05
LOG2E = 1.4426950408889634
F32, BF16 = jnp.float32, jnp.bfloat16
LANES = 128
GROUP = 256
PAD = 16
ROWS = 128
WIDTH = 4
NN = (((1,), (0,)), ((), ()))
NT = (((1,), (1,)), ((), ()))
MESH = pl.DeviceIdType.MESH
VMEM = pl.BlockSpec(memory_space=pltpu.VMEM)
SMEM = pl.BlockSpec(memory_space=pltpu.SMEM)
ANY = pl.BlockSpec(memory_space=pl.ANY)
DMA = pltpu.SemaphoreType.DMA
DP, TENSOR = "dp", "tensor"
VMEM_LIMIT = 63 * 1024 * 1024


def mm(left, right, dims=NN):
    return lax.dot_general(left, right, dims, preferred_element_type=F32)


def exact(left, right):
    return lax.dot_general(
        left, right, NN, precision=lax.Precision.HIGHEST, preferred_element_type=F32
    )


def halves(values):
    high = values.astype(BF16)
    return high, (values - high.astype(F32)).astype(BF16)


def beside(values):
    return jnp.concatenate(halves(values), axis=1)


def lanes_of(step, size):
    return pl.ds(pl.multiple_of(step * size, size), size)


def rows_of(step, size, start=0):
    return pl.ds(pl.multiple_of(start + step * size, PAD), size)


def shaped(shape, dtype=F32):
    return jax.ShapeDtypeStruct(shape, dtype)


def vmem(shape, dtype=F32):
    return pltpu.VMEM(shape, dtype)


def call_kernel(body, name, collective_id, ins, outs, scratch):
    names = list(ins) + list(outs) + list(scratch)

    def kernel(*refs):
        body(SimpleNamespace(**dict(zip(names, refs))))

    remote_copies = (
        dict(collective_id=collective_id, has_side_effects=True) if collective_id is not None else {}
    )
    results = pl.pallas_call(
        kernel,
        out_shape=[shape for shape, _ in outs.values()],
        in_specs=[spec for _, spec in ins.values()],
        out_specs=[spec for _, spec in outs.values()],
        scratch_shapes=list(scratch.values()),
        compiler_params=pltpu.CompilerParams(vmem_limit_bytes=VMEM_LIMIT, **remote_copies),
        name=name,
    )(*[array for array, _ in ins.values()])
    return dict(zip(outs, results))


def place():
    dp, tensor = lax.axis_index(DP), lax.axis_index(TENSOR)
    n_dp, n_tensor = lax.axis_size(DP), lax.axis_size(TENSOR)
    return SimpleNamespace(
        dp=dp,
        tensor=tensor,
        n_dp=n_dp,
        n_tensor=n_tensor,
        depth=n_dp // 2,
        core=lax.rem(tensor, 2),
        x=tensor // 2,
        y=lax.rem(dp, 2),
        z=dp // 2,
        parts=n_dp // n_tensor,
    )


def over_core(at):
    return {TENSOR: at.tensor + 1 - 2 * at.core}


def over_x(at):
    return {TENSOR: lax.rem(at.tensor + 2, at.n_tensor)}


def over_y(at):
    return {DP: at.dp + 1 - 2 * at.y}


def over_z(at, k):
    return {DP: lax.rem(at.z + k, at.depth) * 2 + at.y}


def grid_partners(at):
    return [over_core(at), over_x(at), over_y(at)] + [over_z(at, k) for k in range(1, at.depth)]


def tensor_partners(at):
    return [{TENSOR: lax.rem(at.tensor + k, at.n_tensor)} for k in range(1, at.n_tensor)]


def greet(device):
    pl.semaphore_signal(
        pltpu.get_barrier_semaphore(), inc=1, device_id=device, device_id_type=MESH
    )


def greet_all(partners):
    for partner in partners:
        greet(partner)


def met(count):
    pl.semaphore_wait(pltpu.get_barrier_semaphore(), count)


def remote(source, target, send, recv, device):
    return pltpu.make_async_remote_copy(
        src_ref=source,
        dst_ref=target,
        send_sem=send,
        recv_sem=recv,
        device_id=device,
        device_id_type=MESH,
    )


class Rounds:
    def __init__(self):
        self.units = []
        self.next = 0
        self.begun = 0
        self.finished = set()

    def add(self, unit):
        self.units.append(unit)

    def begin(self, count):
        while self.begun < min(count, len(self.units)):
            self.units[self.begun][0]()
            self.begun += 1

    def start(self):
        self.begin(2 * AHEAD)

    def tick(self):
        pairs = -(-len(self.units) // 2)
        if not self.units or self.next >= pairs + STAGES - 1:
            return
        for stage in reversed(range(STAGES)):
            pair = self.next - stage
            if 0 <= pair < pairs:
                for unit in self.units[2 * pair : 2 * pair + 2]:
                    unit[1][stage]()
        self.next += 1
        self.begin(2 * (self.next + AHEAD))

    def ready(self, unit, rounds_ago=0):
        return self.next >= unit // 2 + STAGES + rounds_ago or self.finished.issuperset({unit})

    def finish(self, unit):
        while not self.ready(unit):
            self.tick()
        if unit not in self.finished:
            self.finished.add(unit)
            self.units[unit][2]()

    def drain(self):
        for unit in range(len(self.units)):
            self.finish(unit)


def gather_sems(total, depth):
    return dict(
        gather_z_send=DMA((total, depth - 1)),
        gather_z_recv=DMA((total, depth - 1)),
        gather_send=DMA((total, 5)),
        gather_recv=DMA((total, 5)),
        gather_own=DMA((total,)),
    )


def gather_unit(at, r, index, block, whole, start, full):
    core, x, y, z = at.core, at.x, at.y, at.z

    def lanes(side):
        return pl.ds(pl.multiple_of((2 * side + core) * full + start, LANES), LANES)

    def same(part, slot, device):
        return remote(
            part, part, r.gather_send.at[index, slot], r.gather_recv.at[index, slot], device
        )

    mine = block.at[:, pl.ds(start, LANES)]
    keep = pltpu.make_async_copy(mine, whole.at[z, y, :, lanes(x)], r.gather_own.at[index])
    along_z = [
        remote(
            mine,
            whole.at[z, y, :, lanes(x)],
            r.gather_z_send.at[index, k - 1],
            r.gather_z_recv.at[index, k - 1],
            over_z(at, k),
        )
        for k in range(1, at.depth)
    ]
    if index % 2 == 0:
        one = [same(whole.at[:, y, :, lanes(x)], 0, over_x(at))]
        two = [same(whole.at[:, y, :, lanes(side)], 1 + side, over_y(at)) for side in range(2)]
    else:
        one = [same(whole.at[:, y, :, lanes(x)], 0, over_y(at))]
        two = [same(whole.at[:, :, :, lanes(x)], 1, over_x(at))]
    last = [same(whole.at[:, :, :, lanes(side)], 3 + side, over_core(at)) for side in range(2)]

    def begin():
        keep.start()
        for copy in along_z:
            copy.start()

    def hand_on(before, after):
        def step():
            for copy in before:
                copy.wait_recv()
            for copy in after:
                copy.start()

        return step

    def first():
        keep.wait()
        hand_on(along_z, one)()

    def finish():
        for copy in last:
            copy.wait_recv()
        for copy in along_z + one + two + last:
            copy.wait_send()

    return begin, [first, hand_on(one, two), hand_on(two, last)], finish


def reduce_scratch(total, depth, rows):
    scratch = dict(
        reduce_send=DMA((total, 4)),
        reduce_recv=DMA((total, 4)),
        reduce_z_send=DMA((total, depth - 1)),
        reduce_z_recv=DMA((total, depth - 1)),
    )
    for index in range(total):
        second = (depth, 2, rows, LANES) if index % 2 == 0 else (2, depth, rows, LANES)
        shapes = ((2, depth, 2, rows, LANES), second, (depth, rows, LANES), (depth - 1, rows, LANES))
        for stage, shape in enumerate(shapes):
            scratch[f"sum{stage}_{index}"] = vmem(shape, BF16)
    return scratch


def reduce_unit(at, r, index, source, start, full, put):
    core, x, y, z, depth = at.core, at.x, at.y, at.z, at.depth
    a, b, c, d = (getattr(r, f"sum{stage}_{index}") for stage in range(4))
    send, recv = r.reduce_send, r.reduce_recv
    x_first = index % 2 == 0

    def lanes(side, which):
        return pl.ds(pl.multiple_of((2 * side + which) * full + start, LANES), LANES)

    zero = [
        remote(
            source.at[:, :, :, lanes(side, 1 - core)],
            a.at[side],
            send.at[index, side],
            recv.at[index, side],
            over_core(at),
        )
        for side in range(2)
    ]
    if x_first:
        one = remote(a.at[1 - x], b, send.at[index, 2], recv.at[index, 2], over_x(at))
        two = remote(b.at[:, 1 - y], c, send.at[index, 3], recv.at[index, 3], over_y(at))
    else:
        one = remote(a.at[:, :, 1 - y], b, send.at[index, 2], recv.at[index, 2], over_y(at))
        two = remote(b.at[1 - x], c, send.at[index, 3], recv.at[index, 3], over_x(at))
    three = [
        remote(
            c.at[lax.rem(z + k, depth)],
            d.at[k - 1],
            r.reduce_z_send.at[index, k - 1],
            r.reduce_z_recv.at[index, k - 1],
            over_z(at, k),
        )
        for k in range(1, depth)
    ]

    def plus(left, right):
        return (left.astype(F32) + right.astype(F32)).astype(BF16)

    def begin():
        for copy in zero:
            copy.start()

    def after_core():
        for copy in zero:
            copy.wait_recv()

        @pl.loop(0, 2 * depth)
        def _(step):
            high, low = step // 2, lax.rem(step, 2)
            for side in range(2):
                a[side, high, low] = plus(a[side, high, low], source[high, low, :, lanes(side, core)])

        one.start()

    def after_first():
        one.wait_recv()

        @pl.loop(0, depth)
        def _(high):
            for side in range(2):
                if x_first:
                    b[high, side] = plus(b[high, side], a[x, high, side])
                else:
                    b[side, high] = plus(b[side, high], a[side, high, y])

        two.start()

    def after_second():
        two.wait_recv()

        @pl.loop(0, depth)
        def _(high):
            c[high] = plus(c[high], b[high, y] if x_first else b[x, high])

        for copy in three:
            copy.start()

    def finish():
        value = c[z].astype(F32)
        for k, copy in enumerate(three):
            copy.wait_recv()
            value = value + d[k].astype(F32)
        put(value)
        for copy in zero + [one, two] + three:
            copy.wait_send()

    return begin, [after_core, after_first, after_second], finish


STAGES = 3
AHEAD = 2


def conv_rows(raw, taps, start, columns):
    total = taps(WIDTH, columns)
    for tap in range(WIDTH):
        first = PAD - (WIDTH - 1) + tap + start
        total = total + taps(tap, columns) * raw[pl.ds(first, ROWS), columns]
    return total


def taps_of(ref, layer):
    def taps(tap, columns):
        return ref[tap, pl.ds(layer, 1), columns]

    return taps


def fill_constants(r, at, head_size, state, heads):
    inner = r.spread.shape[1]
    row = lax.broadcasted_iota(jnp.int32, (2 * LANES, inner), 0)
    column = lax.broadcasted_iota(jnp.int32, (2 * LANES, inner), 1)
    r.spread[...] = (lax.rem(row, LANES) == column // head_size).astype(F32).astype(BF16)
    if hasattr(r, "collect"):
        row = lax.broadcasted_iota(jnp.int32, (inner, LANES), 0)
        column = lax.broadcasted_iota(jnp.int32, (inner, LANES), 1)
        r.collect[...] = (row // head_size == column).astype(F32).astype(BF16)
    quarter, own = 2 * state // at.n_tensor, heads // at.n_tensor
    shape = (at.n_tensor * LANES, 2 * state + LANES)
    row = lax.broadcasted_iota(jnp.int32, shape, 0)
    column = lax.broadcasted_iota(jnp.int32, shape, 1)
    block, lane = row // LANES, lax.rem(row, LANES)
    target = jnp.where(
        lane < quarter,
        block * quarter + lane,
        jnp.where(lane < quarter + own, 2 * state + block * own + lane - quarter, -1),
    )
    r.select[...] = (target == column).astype(F32).astype(BF16)


def split_narrow(r, narrow):
    narrow = narrow[...].reshape(r.wbc.shape[0], r.select.shape[0])
    r.wbc[...] = mm(narrow, r.select[:, : r.wbc.shape[1]]).astype(BF16)
    r.wdt[...] = mm(narrow, r.select[:, r.wbc.shape[1] :]).astype(BF16)


def fill_live(r, at):
    tokens = r.live.shape[0]
    length = r.lengths[r.order[at.dp]]
    position = lax.broadcasted_iota(jnp.int32, (tokens, LANES), 0) + at.tensor * tokens
    r.live[...] = (position < length).astype(F32)


def step_terms(r, layer, block):
    rows = pl.ds(block * SCAN_BLOCK, SCAN_BLOCK)
    value = r.dtp[rows, :]
    size = (jnp.maximum(value, 0.0) + jnp.log1p(jnp.exp(-jnp.abs(value)))) * r.live[rows, :]
    r.dt[block] = size
    row_id = lax.broadcasted_iota(jnp.int32, (SCAN_BLOCK, SCAN_BLOCK), 0)
    col_id = lax.broadcasted_iota(jnp.int32, (SCAN_BLOCK, SCAN_BLOCK), 1)
    earlier = (row_id >= col_id).astype(F32)
    running = exact(earlier, size * (r.heads[layer, 1:2, :] * LOG2E))
    r.run[block] = running
    r.run_t[block] = running.T
    total = running[SCAN_BLOCK - 1 : SCAN_BLOCK, :]
    r.step_two[block] = beside(size)
    r.grow_two[block] = beside(jnp.exp2(running))
    r.keep_two[block] = beside(jnp.exp2(total - running))
    whole = jnp.broadcast_to(jnp.exp2(total), (8, LANES))
    r.decay[block] = mm(beside(whole), r.spread[...])


def fill_heads(r):
    heads = r.dt_bias.shape[1]
    row = lax.broadcasted_iota(jnp.int32, (heads, LANES), 0)
    column = lax.broadcasted_iota(jnp.int32, (heads, LANES), 1)
    widen = (row == column).astype(F32)
    for index, values in enumerate((r.dt_bias[...], -jnp.exp(r.a_log[...]), r.d_skip[...])):
        padded = exact(values, widen)
        for layer in range(values.shape[0]):
            r.heads[layer, index : index + 1, :] = padded[layer : layer + 1, :]


def spread_skip(r, layer):
    r.skip[...] = mm(
        beside(jnp.broadcast_to(r.heads[layer, 2:3, :], (8, LANES))), r.spread[...]
    )


def head_row(head, head_size):
    lane = lax.broadcasted_iota(jnp.int32, (1, GROUP), 1)
    return (lane // head_size == head).astype(F32).astype(BF16)


def own_lanes(stacked, per_group, head_size):
    rows = stacked.shape[0] // per_group
    lane = lax.broadcasted_iota(jnp.int32, (1, GROUP), 1) // head_size
    total = stacked[:rows]
    for head in range(1, per_group):
        total = jnp.where(lane == head, stacked[head * rows : (head + 1) * rows], total)
    return total


def columns_of(r, block, group, per_group):
    return pltpu.roll(r.run[block], lax.rem(LANES - per_group * group, LANES), 1)


def common_scratch(param_shapes, width, inner, state, n_blocks, tokens, n_tensor, depth):
    return dict(
        wbc=vmem((width, 2 * state), BF16),
        wdt=vmem((width, LANES), BF16),
        spread=vmem((2 * LANES, inner), BF16),
        select=vmem((n_tensor * LANES, 2 * state + LANES), BF16),
        live=vmem((tokens, LANES)),
        skip=vmem((8, inner)),
        dt=vmem((n_blocks, SCAN_BLOCK, LANES)),
        run=vmem((n_blocks, SCAN_BLOCK, LANES)),
        run_t=vmem((n_blocks, LANES, SCAN_BLOCK)),
        step_two=vmem((n_blocks, SCAN_BLOCK, 2 * LANES), BF16),
        grow_two=vmem((n_blocks, SCAN_BLOCK, 2 * LANES), BF16),
        keep_two=vmem((n_blocks, SCAN_BLOCK, 2 * LANES), BF16),
        decay=vmem((n_blocks, 8, inner)),
        pair=vmem((n_blocks, SCAN_BLOCK, SCAN_BLOCK)),
        states=vmem((n_blocks + 1, state, inner)),
        bc=vmem((tokens, 2 * state), BF16),
        xc=vmem((tokens, inner), BF16),
        dtp=vmem((tokens, LANES)),
        rms=vmem((tokens, LANES)),
        in_gain=vmem(param_shapes[0]),
        conv_x=vmem(param_shapes[1]),
        conv_bc=vmem(param_shapes[2]),
        dt_bias=vmem(param_shapes[3]),
        a_log=vmem(param_shapes[4]),
        d_skip=vmem(param_shapes[5]),
        gated_gain=vmem(param_shapes[6]),
        heads=vmem((param_shapes[3][0], 3, LANES)),
        load_sem=DMA((40,)),
        store_sem=DMA((24,)),
    )


def small_rows(width, inner, state):
    sizes = dict(
        heads=8,
        gain=-(-width // LANES // 8) * 8,
        gate_gain=inner // LANES,
        tap_x=(WIDTH + 1) * (inner // LANES),
        tap_b=(WIDTH + 1) * (2 * state // LANES),
    )
    starts, total = {}, 0
    for name, size in sizes.items():
        starts[name] = total
        total += size
    return SimpleNamespace(all=-(-total // 64) * 64, **starts)


def param_loads(r):
    copies = [
        pltpu.make_async_copy(getattr(r, "p_" + name), getattr(r, name), r.load_sem.at[16 + index])
        for index, name in enumerate(PARAMS)
    ]
    for copy in copies:
        copy.start()
    return copies


def param_inputs(params):
    ins = {"p_" + name: (params[name], ANY) for name in PARAMS}
    return dict(lengths=(params["lengths"], SMEM), order=(params["order"], SMEM), **ins)


def param_shapes(params):
    return [params[name].shape for name in PARAMS]


def row_blocks(whole, target, sems):
    depth, two, rows, _ = whole.shape
    return [
        pltpu.make_async_copy(
            whole.at[index // two, index % two],
            target.at[pl.ds(index * rows, rows), :],
            sems.at[index],
        )
        for index in range(depth * two)
    ]


PARAMS = ("in_gain", "conv_x", "conv_bc", "dt_bias", "a_log", "d_skip", "gated_gain")
TERMS = ("dt", "run", "run_t", "step_two", "grow_two", "keep_two", "decay")
CONSTANTS = ("spread", "collect", "select")
SAVED = ("nx", "gate", "xraw", "braw", "xc", "bc", "dtp", "mixed", "states", "rms")


class Weights:
    def __init__(self, queues, sources):
        self.queues = queues
        self.sources = sources
        self.started = {name: 0 for name in sources}
        self.used = {name: 0 for name in sources}

    def load(self, name, rounds_ago):
        layer = self.started[name]
        if layer == len(self.sources[name]) or self.used[name] != layer:
            return
        queue, units, copies = self.sources[name][layer]
        if all(queue.ready(unit, rounds_ago) for unit in units):
            for unit in units:
                queue.finish(unit)
            for copy in copies:
                copy.start()
            self.started[name] += 1

    def tick(self):
        for queue in self.queues:
            queue.tick()
        for name in self.sources:
            self.load(name, 1)

    def wait(self, name, layer):
        queue, units, copies = self.sources[name][layer]
        while not all(queue.ready(unit) for unit in units):
            self.tick()
        self.load(name, 0)
        for copy in copies:
            copy.wait()

    def done(self, name):
        self.used[name] += 1
        self.load(name, 1)


def deal_start(at, r):
    runner = at.dp // at.parts
    at_home = runner == at.tensor
    piece = r.arranged.shape[1]

    def spot(k, other):
        start = (k * at.n_tensor + other) * piece
        return r.dealt.at[pl.ds(pl.multiple_of(start, PAD), piece), :]

    slot = lax.rem(at.dp, at.parts)
    keep = pltpu.make_async_copy(r.arranged.at[at.dp], spot(slot, at.tensor), r.deal_own)
    deal = [
        remote(
            r.arranged.at[j],
            spot(slot, at.tensor),
            r.deal_send.at[j],
            r.deal_recv.at[slot, at.tensor],
            {DP: j, TENSOR: runner},
        )
        for j in range(at.n_dp)
    ]
    for j in range(at.n_dp):
        pl.when((j != at.dp) | (runner != at.tensor))(deal[j].start)
    pl.when(at_home)(keep.start)

    def arrive():
        for k in range(at.parts):
            for other in range(at.n_tensor):
                arrival = remote(
                    r.arranged.at[0],
                    spot(k, other),
                    r.deal_send.at[0],
                    r.deal_recv.at[k, other],
                    {TENSOR: lax.rem(at.tensor + 1, at.n_tensor)},
                )
                pl.when((at.tensor * at.parts + k != at.dp) | (other != at.tensor))(
                    arrival.wait_recv
                )
        pl.when(at_home)(keep.wait)

    def rest():
        for j in range(at.n_dp):
            pl.when((j != at.dp) | (runner != at.tensor))(deal[j].wait_send)

    return arrive, rest


def forward_body(cfg, r):
    at = place()
    direct = cfg.direct
    width = r.dealt.shape[1]
    small_loads = param_loads(r)
    count = 0
    if direct:
        greet_all(grid_partners(at))
        for source, other in deal_sources(at):

            @pl.when((source != at.dp) | (other != at.tensor))
            def _():
                greet({DP: source, TENSOR: other})

        at_home = (at.dp // at.parts == at.tensor).astype(jnp.int32)
        count = len(grid_partners(at)) + at.n_dp - at_home
    greet_all(tensor_partners(at))
    count = count + len(tensor_partners(at))

    first_queue, queue = Rounds(), Rounds()
    names = ("wn", "wx", "wz", "wo")
    sources = {name: [] for name in names}
    total = 0
    for layer in range(cfg.layers):
        for name in names:
            target = getattr(r, name)
            index = len(sources[name]) * len(names) + names.index(name)
            if direct:
                block, whole = getattr(r, "block_" + name), getattr(r, f"whole_{name}{layer}")
                full = block.shape[2]
                owner = first_queue if layer == 0 and name in names[:2] else queue
                units = []
                for start in range(0, full, LANES):
                    units.append(len(owner.units))
                    owner.add(gather_unit(at, r, total, block.at[layer], whole, start, full))
                    total += 1
                copies = row_blocks(whole, target, r.weight_sem.at[index])
                sources[name].append((owner, units, copies))
            else:
                whole = getattr(r, f"{name}{layer}_in")
                copy = pltpu.make_async_copy(whole, target, r.weight_sem.at[index, 0])
                sources[name].append((queue, [], [copy]))
    weights = Weights((queue,), sources)

    if direct:
        for j in range(at.n_dp):
            r.arranged[j] = r.hidden_in[r.order[j]]
    else:
        first = pltpu.make_async_copy(r.hidden_in, r.dealt, r.deal_own)
        first.start()
    met(count)
    if direct:
        first_queue.start()
        first_queue.tick()
        arrive, rest = deal_start(at, r)
        queue.start()
    fill_constants(r, at, cfg.head_size, cfg.state, cfg.heads)
    fill_live(r, at)
    for copy in small_loads:
        copy.wait()
    fill_heads(r)
    constants = []
    for index, name in enumerate(CONSTANTS):
        copy = pltpu.make_async_copy(getattr(r, name), getattr(r, name + "_out"), r.store_sem.at[20 + index])
        copy.start()
        constants.append(copy)
    if direct:
        first_queue.drain()
        for name in names[:2]:
            weights.load(name, 0)
        weights.tick()
        weights.tick()
        arrive()
        first = pltpu.make_async_copy(r.dealt, r.hidden, r.hidden_sem)
        first.start()
    else:
        first.wait()
    stores = {}
    turned = turn_copies(at, r, False) if direct else []
    for layer in range(cfg.layers):
        forward_layer(cfg, at, r, layer, weights, stores, turned)
    queue.drain()
    for copy in turned:
        copy.wait()
    if direct:
        rest()
        first.wait()
    for store in list(stores.values()) + constants:
        store.wait()


def forward_layer(cfg, at, r, layer, weights, stores, turned):
    me, last = at.tensor, at.n_tensor - 1
    h = r.dealt if layer == 0 else getattr(r, f"h{layer}")
    h_next = getattr(r, f"h{layer + 1}")
    halo = getattr(r, f"halo{layer}")
    tokens, width = h.shape
    inner, state, head_size = cfg.inner, cfg.state, cfg.head_size
    n_blocks = tokens // SCAN_BLOCK
    groups = inner // GROUP
    per_group = GROUP // head_size
    following = {TENSOR: lax.rem(me + 1, at.n_tensor)}

    def clear(*names):
        for name in names:
            if name in stores:
                stores.pop(name).wait()

    def store(name):
        index = (SAVED + TERMS).index(name)
        copy = pltpu.make_async_copy(
            getattr(r, name), getattr(r, f"{name}{layer}_out"), r.store_sem.at[index]
        )
        copy.start()
        stores[name] = copy

    halo_copy = remote(
        h.at[pl.ds(tokens - PAD, PAD), :], halo, r.halo_send.at[layer], r.halo_recv.at[layer], following
    )

    @pl.when(me < last)
    def _():
        halo_copy.start()

    spread_skip(r, layer)
    gain = r.in_gain[layer : layer + 1, :]

    def normalize(values):
        values = values.astype(F32)
        inv = lax.rsqrt(jnp.mean(values * values, axis=-1, keepdims=True) + EPS)
        return (values * inv * gain).astype(BF16)

    clear("nx", "dtp", *TERMS)

    @pl.loop(0, tokens // ROWS)
    def _(step):
        r.nx[rows_of(step, ROWS, PAD), :] = normalize(h[rows_of(step, ROWS), :])

    weights.wait("wn", layer)
    split_narrow(r, r.wn)
    weights.done("wn")
    r.dtp[...] = mm(r.nx[pl.ds(PAD, tokens), :], r.wdt[...]) + r.heads[layer, 0:1, :]
    for block in range(n_blocks):
        step_terms(r, layer, block)

    @pl.when(me > 0)
    def _():
        halo_copy.wait_recv()
        r.nx[0:PAD, :] = normalize(halo[...])

    @pl.when(me == 0)
    def _():
        r.nx[0:PAD, :] = jnp.zeros((PAD, width), BF16)

    store("nx")
    store("dtp")
    for name in TERMS:
        store(name)

    def convolve(projection, taps, raw, out, columns):
        raw[:, columns] = mm(r.nx[...], projection[:, columns])
        for start in range(0, tokens, ROWS):
            before = conv_rows(raw, taps, start, columns)
            out[pl.ds(start, ROWS), columns] = (before * jax.nn.sigmoid(before)).astype(BF16)

    clear("braw", "bc")
    for step in range(2 * state // GROUP):
        convolve(r.wbc, taps_of(r.conv_bc, layer), r.braw, r.bc, pl.ds(step * GROUP, GROUP))
    store("braw")
    store("bc")
    for block in range(n_blocks):
        rows = pl.ds(block * SCAN_BLOCK, SCAN_BLOCK)
        r.b_t[block] = r.bc[rows, :state].astype(F32).T.astype(BF16)
        row_id = lax.broadcasted_iota(jnp.int32, (SCAN_BLOCK, SCAN_BLOCK), 0)
        col_id = lax.broadcasted_iota(jnp.int32, (SCAN_BLOCK, SCAN_BLOCK), 1)
        scores = mm(r.bc[rows, state:], r.bc[rows, :state], NT)
        r.pair[block] = jnp.where(row_id >= col_id, scores, 0.0)

    if layer:
        weights.tick()
    weights.wait("wx", layer)
    clear("xraw", "xc", "states")
    for begin in range(0, groups, groups // 2):
        if begin:
            weights.tick()

        @pl.loop(begin, begin + groups // 2)
        def _(group):
            columns = lanes_of(group, GROUP)
            convolve(r.wx, taps_of(r.conv_x, layer), r.xraw, r.xc, columns)
            for block in range(n_blocks):
                rows = pl.ds(block * SCAN_BLOCK, SCAN_BLOCK)
                sizes = mm(r.step_two[block], r.spread[:, columns])
                keeps = mm(r.keep_two[block], r.spread[:, columns])
                weighted = (r.xc[rows, columns].astype(F32) * sizes * keeps).astype(BF16)
                r.states[block + 1, :, columns] = mm(r.b_t[block], weighted)

    weights.done("wx")
    store("xraw")
    store("xc")

    carry_copies = [
        remote(
            r.carry_out.at[layer, group],
            r.carry_in.at[layer, group],
            r.carry_send.at[layer, group],
            r.carry_recv.at[layer, group],
            following,
        )
        for group in range(groups)
    ]

    def chain():
        for group in range(groups):
            columns = pl.ds(group * GROUP, GROUP)

            @pl.when(me > 0)
            def _():
                carry_copies[group].wait_recv()
                r.states[0, :, columns] = r.carry_in[layer, group].astype(F32)

            @pl.when(me == 0)
            def _():
                r.states[0, :, columns] = jnp.zeros((state, GROUP), F32)

            for block in range(n_blocks):
                r.states[block + 1, :, columns] += (
                    r.states[block, :, columns] * r.decay[block, 0:1, columns]
                )
            r.carry_out[layer, group] = r.states[n_blocks, :, columns].astype(BF16)

            @pl.when(me < last)
            def _():
                carry_copies[group].start()

    pl.when(me == 0)(chain)
    clear("mixed")
    for block in range(n_blocks):
        if block:
            weights.tick()
        rows = pl.ds(block * SCAN_BLOCK, SCAN_BLOCK)

        @pl.loop(0, groups)
        def _(group):
            columns = lanes_of(group, GROUP)
            sizes = mm(r.step_two[block], r.spread[:, columns])
            x_here = r.xc[rows, columns].astype(F32)
            stepped = (x_here * sizes).astype(BF16)
            rolled = columns_of(r, block, group, per_group)
            upper, lower = [], []
            for head in range(per_group):
                along = r.run_t[block, pl.ds(per_group * group + head, 1), :]
                down = rolled[:, head : head + 1]
                factor = jnp.exp2(jnp.minimum(down[:HALF] - along[:, :HALF], 0.0))
                upper.append((r.pair[block, :HALF, :HALF] * factor).astype(BF16))
                factor = jnp.exp2(jnp.minimum(down[HALF:] - along, 0.0))
                lower.append((r.pair[block, HALF:, :] * factor).astype(BF16))
            upper = own_lanes(mm(jnp.concatenate(upper, axis=0), stepped[:HALF]), per_group, head_size)
            lower = own_lanes(mm(jnp.concatenate(lower, axis=0), stepped), per_group, head_size)
            r.mixed[rows, columns] = (
                jnp.concatenate([upper, lower], axis=0) + r.skip[0:1, columns] * x_here
            )

        pl.when(me == block + 1)(chain)

    if layer + 1 == cfg.layers:
        for copy in turned:
            copy.start()
    weights.wait("wz", layer)
    clear("gate")

    @pl.loop(0, groups)
    def _(group):
        columns = lanes_of(group, GROUP)
        r.gate[:, columns] = mm(r.nx[pl.ds(PAD, tokens), :], r.wz[:, columns])

    weights.done("wz")
    store("gate")
    pl.when(me > n_blocks)(chain)
    store("states")
    r.squares[...] = jnp.zeros_like(r.squares)
    for block in range(n_blocks):
        rows = pl.ds(block * SCAN_BLOCK, SCAN_BLOCK)

        @pl.loop(0, groups)
        def _(group):
            columns = lanes_of(group, GROUP)
            grown = mm(r.grow_two[block], r.spread[:, columns])
            total = r.mixed[rows, columns] + grown * mm(
                r.bc[rows, state:], r.states[block, :, columns].astype(BF16)
            )
            r.mixed[rows, columns] = total
            gate_in = r.gate[rows, columns]
            gated = total * gate_in * jax.nn.sigmoid(gate_in)
            r.gm[rows, columns] = gated
            squared = gated * gated
            for lane in range(0, GROUP, LANES):
                r.squares[rows, :] += squared[:, lane : lane + LANES]

        if block == 0:
            weights.tick()

    store("mixed")
    clear("rms")
    r.rms[...] = jnp.broadcast_to(
        lax.rsqrt(jnp.sum(r.squares[...], axis=-1, keepdims=True) / inner + EPS), r.rms.shape
    )
    store("rms")

    @pl.loop(0, groups)
    def _(group):
        columns = lanes_of(group, GROUP)
        for start in range(0, tokens, ROWS):
            rows = pl.ds(start, ROWS)
            r.go[rows, columns] = (
                r.gm[rows, columns] * r.rms[rows, 0:1] * r.gated_gain[layer : layer + 1, columns]
            ).astype(BF16)

    weights.wait("wo", layer)

    @pl.loop(0, width // GROUP)
    def _(step):
        columns = lanes_of(step, GROUP)
        branch = mm(r.go[...], r.wo[columns, :], NT)
        value = (h[:, columns].astype(F32) + branch) * r.live[:, 0:1]
        h_next[:, columns] = value
        if layer + 1 == cfg.layers:
            r.h_low[:, columns] = value.astype(BF16)

    weights.done("wo")
    if layer == 0:
        weights.tick()

    @pl.when(me < last)
    def _():
        halo_copy.wait_send()
        for copy in carry_copies:
            copy.wait_send()


def layers_forward(cfg, at, hidden_in, params, weights, blocks, turn):
    layers, inner, state = cfg.layers, cfg.inner, cfg.state
    width = hidden_in.shape[-1]
    tokens = cfg.tokens
    n_blocks = tokens // SCAN_BLOCK
    depth = at.n_dp // 2
    ins = dict(hidden_in=(hidden_in, VMEM if cfg.direct else ANY), **param_inputs(params))
    saved = dict(
        nx=vmem((PAD + tokens, width), BF16),
        gate=vmem((tokens, inner)),
        xraw=vmem((PAD + tokens, inner)),
        braw=vmem((PAD + tokens, 2 * state)),
        xc=vmem((tokens, inner), BF16),
        bc=vmem((tokens, 2 * state), BF16),
        dtp=vmem((tokens, LANES)),
        mixed=vmem((tokens, inner)),
        states=vmem((n_blocks + 1, state, inner)),
        rms=vmem((tokens, LANES)),
    )
    outs = dict(h_low=(shaped((tokens, width), BF16), VMEM))
    scratch = common_scratch(
        param_shapes(params), width, inner, state, n_blocks, tokens, at.n_tensor, depth
    )
    carry = (layers, inner // GROUP, state, GROUP)
    scratch.update(saved)
    scratch.update(
        dealt=vmem((tokens, width), BF16),
        deal_own=DMA,
        wz=vmem((width, inner), BF16),
        wx=vmem((width, inner), BF16),
        wo=vmem((width, inner), BF16),
        wn=vmem((width, at.n_tensor * LANES), BF16),
        weight_sem=DMA((4 * layers, at.n_dp)),
        halo_send=DMA((layers,)),
        halo_recv=DMA((layers,)),
        carry_out=vmem(carry, BF16),
        carry_in=vmem(carry, BF16),
        carry_send=DMA(carry[:2]),
        carry_recv=DMA(carry[:2]),
        b_t=vmem((n_blocks, state, SCAN_BLOCK), BF16),
        gm=vmem((tokens, inner)),
        go=vmem((tokens, inner), BF16),
        squares=vmem((tokens, LANES)),
    )
    for layer in range(layers):
        scratch[f"halo{layer}"] = vmem((PAD, width), F32 if layer else BF16)
        outs[f"h{layer + 1}"] = (shaped((tokens, width)), VMEM)
        for name in SAVED + TERMS:
            kind = scratch[name]
            outs[f"{name}{layer}_out"] = (shaped(kind.shape, kind.dtype), ANY)
    scratch["collect"] = vmem((inner, LANES), BF16)
    for name in CONSTANTS:
        outs[name + "_out"] = (shaped(scratch[name].shape, BF16), ANY)
    if cfg.direct:
        total = 0
        piece = tokens // at.n_dp
        for name, block in blocks.items():
            ins["block_" + name] = (block, VMEM)
            total += layers * (block.shape[2] // LANES)
            whole = (depth, 2, block.shape[1], at.n_tensor * block.shape[2])
            for layer in range(layers):
                outs[f"whole_{name}{layer}"] = (shaped(whole, BF16), ANY)
        ins["turn_in"] = (turn, VMEM)
        outs["turned"] = (shaped(turn.shape, BF16), ANY)
        outs["hidden"] = (shaped((tokens, width), BF16), ANY)
        scratch.update(turn_sems(at))
        scratch.update(gather_sems(total, depth))
        scratch.update(
            arranged=vmem((at.n_dp, piece, width), BF16),
            deal_send=DMA((at.n_dp,)),
            deal_recv=DMA((at.parts, at.n_tensor)),
            hidden_sem=DMA,
        )
    else:
        for layer in range(layers):
            for name in blocks:
                ins[f"{name}{layer}_in"] = (weights[layer][name], ANY)
    return call_kernel(partial(forward_body, cfg), "layers_forward", 1, ins, outs, scratch)


def turn_sems(at):
    shape = (at.n_tensor - 1, at.parts)
    return dict(turn_send=DMA(shape), turn_recv=DMA(shape), turn_own=DMA((at.parts,)))


def turn_copies(at, r, to_pieces):
    copies = []
    for offset in range(at.n_tensor):
        other = lax.rem(at.tensor + offset, at.n_tensor)
        for k in range(at.parts):
            if to_pieces:
                mine = r.turn_in.at[k * at.n_tensor + other]
                theirs = r.turned.at[at.tensor * at.parts + k]
            else:
                mine = r.turn_in.at[other * at.parts + k]
                theirs = r.turned.at[k * at.n_tensor + at.tensor]
            if offset == 0:
                copies.append(pltpu.make_async_copy(mine, theirs, r.turn_own.at[k]))
            else:
                copies.append(
                    remote(
                        mine,
                        theirs,
                        r.turn_send.at[offset - 1, k],
                        r.turn_recv.at[offset - 1, k],
                        {TENSOR: other},
                    )
                )
    return copies


def backward_body(cfg, r):
    at = place()
    me, last = at.tensor, at.n_tensor - 1
    layer, direct = cfg.layer, cfg.direct
    tokens, width = r.h.shape
    inner, state, head_size = cfg.inner, cfg.state, cfg.head_size
    n_blocks = tokens // SCAN_BLOCK
    groups = inner // GROUP
    per_group = GROUP // head_size
    previous = {TENSOR: lax.rem(me + last, at.n_tensor)}

    def load(name, target, index):
        copy = pltpu.make_async_copy(getattr(r, name + "_in"), target, r.load_sem.at[index])
        copy.start()
        return copy

    next_load = load("h_next", r.gn, 10)
    loads = {
        name: load(name, getattr(r, name), index) for index, name in enumerate(("nx", "rms", "dtp", "bc"))
    }
    for index, name in enumerate(CONSTANTS + TERMS):
        loads[name] = load(name, getattr(r, name), 24 + index)
    small_loads = param_loads(r)

    def stream(group, slot):
        columns = lanes_of(group, GROUP)
        return [
            pltpu.make_async_copy(r.gate_in.at[:, columns], r.gate.at[slot], r.stream_sem.at[0, slot]),
            pltpu.make_async_copy(r.mixed_in.at[:, columns], r.mixed.at[slot], r.stream_sem.at[1, slot]),
        ]

    count = 0
    if direct:
        greet_all(grid_partners(at))
        count = len(grid_partners(at))
        if cfg.closing:
            count = count + greet_back(at)
    greet_all(tensor_partners(at))
    count = count + len(tensor_partners(at))

    earlier, own = Rounds(), Rounds()
    unit_indices = []

    def enqueue(queue, source, full, put):
        for start in range(0, full, LANES):
            index = len(unit_indices)
            unit_indices.append(index)
            queue.add(reduce_unit(at, r, index, source, start, full, partial(put, start)))

    def tick():
        earlier.tick()
        own.tick()

    def put_wide(target):
        def put(start, value):
            target[:, start : start + LANES] = value

        return put

    def put_narrow(target):
        def put(start, value):
            target[...] = value

        return put

    turned = []
    if direct:
        if cfg.more:
            enqueue(earlier, r.g_wx, r.sum_wx.shape[1], put_wide(r.sum_wx))
            enqueue(earlier, r.g_narrow, LANES, put_narrow(r.sum_narrow))
            prior_loads = [load("prior_wx", r.g_wx, 11), load("prior_narrow", r.g_narrow, 12)]
        if cfg.turn:
            turned = turn_copies(at, r, True)

    fill_live(r, at)
    for copy in small_loads:
        copy.wait()
    fill_heads(r)
    for name in CONSTANTS:
        loads[name].wait()
    spread_skip(r, layer)
    loads["nx"].wait()
    loads["rms"].wait()
    next_load.wait()

    @pl.loop(0, tokens // ROWS)
    def _(step):
        rows = rows_of(step, ROWS)
        alive = r.live[rows, 0:1]
        low = (r.gh[rows, :].astype(F32) * alive).astype(BF16)
        r.g_branch[rows, :] = low
        columns = lanes_of(step, ROWS)
        r.g_branch_t[:, columns] = low.T
        r.normed_t[:, columns] = r.nx[rows_of(step, ROWS, PAD), :].T
        branch = r.gn[rows, :] - r.h[rows, :].astype(F32)
        scale = r.rms[rows, 0:1]
        along = jnp.sum(low.astype(F32) * branch, axis=-1, keepdims=True) * (scale * scale / inner)
        r.along[rows, :] = jnp.broadcast_to(along, (ROWS, LANES))

    loads.update(
        {
            name: load(name, getattr(r, name), 4 + index)
            for index, name in enumerate(("wo", "xc", "states", "braw", "wz"))
        }
    )
    for copy in stream(0, 0):
        copy.start()
    met(count)
    if direct and cfg.more:
        for copy in prior_loads:
            copy.wait()
        earlier.start()
    for copy in turned:
        copy.start()
    loads["dtp"].wait()
    for name in TERMS:
        loads[name].wait()
    tick()

    loads["bc"].wait()
    row_id = lax.broadcasted_iota(jnp.int32, (SCAN_BLOCK, SCAN_BLOCK), 0)
    col_id = lax.broadcasted_iota(jnp.int32, (SCAN_BLOCK, SCAN_BLOCK), 1)
    for block in range(n_blocks):
        rows = pl.ds(block * SCAN_BLOCK, SCAN_BLOCK)
        scores = mm(r.bc[rows, :state], r.bc[rows, state:], NT)
        r.pair[block] = jnp.where(row_id <= col_id, scores, 0.0)
        r.c_t[block] = r.bc[rows, state:].astype(F32).T.astype(BF16)
    r.g_run[...] = jnp.zeros_like(r.g_run)
    r.g_heads[...] = jnp.zeros_like(r.g_heads)
    places = small_rows(width, inner, state)

    def put_small(name, row, tile, values):
        for lane in range(0, values.shape[1], LANES):
            r.g_small[pl.ds(name + row + tile + lane // LANES, 1), :] = values[
                :, lane : lane + LANES
            ]

    def put_rows(target, columns, values):
        values = values.astype(BF16)
        if direct:
            target[:, :, :, columns] = values.reshape(target.shape[:3] + values.shape[1:])
        else:
            target[:, columns] = values

    def collected(values, columns):
        rows = values.shape[0]
        both = mm(jnp.concatenate(halves(values), axis=0), r.collect[columns, :])
        return both[:rows] + both[rows:]

    loads["wo"].wait()
    loads["xc"].wait()

    def gate_group(group):
        slot = lax.rem(group, 2)
        columns = lanes_of(group, GROUP)
        for copy in stream(group, slot):
            copy.wait()

        @pl.when(group + 1 < groups)
        def _():
            for copy in stream(group + 1, 1 - slot):
                copy.start()

        gain = r.gated_gain[layer : layer + 1, columns]
        skipped = r.skip[0:1, columns]
        gained = jnp.zeros((1, GROUP), F32)
        skip_sum = jnp.zeros((1, GROUP), F32)
        r.gq[pl.ds(0, tokens), columns] = mm(r.g_branch[...], r.wo[:, columns])
        for start in range(0, tokens, ROWS):
            rows = pl.ds(start, ROWS)
            gate_in = r.gate[slot, rows, :]
            here = r.mixed[slot, rows, :]
            x_here = r.xc[rows, columns].astype(F32)
            scale = r.rms[rows, 0:1]
            sig = jax.nn.sigmoid(gate_in)
            act = gate_in * sig
            gated = here * act
            scaled = gated * scale
            r.go[rows, :] = (scaled * gain).astype(BF16)
            g_gated = r.gq[rows, columns]
            gained = gained + jnp.sum(g_gated * scaled, axis=0, keepdims=True)
            g_mix = scale * gain * g_gated - gated * r.along[rows, 0:1]
            g_out = g_mix * act
            r.gq[rows, columns] = g_out
            r.pz[rows, columns] = (g_mix * here * sig * (1.0 + gate_in * (1.0 - sig))).astype(BF16)
            skip_sum = skip_sum + jnp.sum(g_out * x_here, axis=0, keepdims=True)
            r.g_run[rows, :] += collected(g_out * (here - skipped * x_here), columns)
        put_small(places.gate_gain, 0, group * (GROUP // LANES), gained)
        r.g_heads[2:3, :] += collected(jnp.broadcast_to(skip_sum, (8, GROUP)), columns)[0:1, :]
        put_rows(r.g_wo, columns, mm(r.g_branch_t[...], r.go[...]))
        put_rows(r.g_wz, columns, mm(r.normed_t[...], r.pz[:, columns]))
        for block in range(n_blocks):
            rows = pl.ds(block * SCAN_BLOCK, SCAN_BLOCK)
            grown = mm(r.grow_two[block], r.spread[:, columns])
            r.d_states[block, :, columns] = mm(
                r.c_t[block], (r.gq[rows, columns] * grown).astype(BF16)
            )

    for first in range(0, groups, groups // 2):
        pl.loop(first, first + groups // 2)(gate_group)
        tick()
    wx_load = load("wx", r.wo, 13)

    if direct:
        for source, target in ((r.g_wo, r.sum_wo), (r.g_wz, r.sum_wz)):
            enqueue(own, source, target.shape[1], put_wide(target))
        own.start()

    carry_copies = [
        remote(
            r.carry_out.at[group],
            r.carry_in.at[group],
            r.carry_send.at[group],
            r.carry_recv.at[group],
            previous,
        )
        for group in range(groups)
    ]

    def chain():
        for group in range(groups):
            columns = pl.ds(group * GROUP, GROUP)

            @pl.when(me < last)
            def _():
                carry_copies[group].wait_recv()
                r.d_states[n_blocks, :, columns] = r.carry_in[group].astype(F32)

            @pl.when(me == last)
            def _():
                r.d_states[n_blocks, :, columns] = jnp.zeros((state, GROUP), F32)

            for block in reversed(range(n_blocks)):
                r.d_states[block, :, columns] += (
                    r.d_states[block + 1, :, columns] * r.decay[block, 0:1, columns]
                )
            r.carry_out[group] = r.d_states[0, :, columns].astype(BF16)

            @pl.when(me > 0)
            def _():
                carry_copies[group].start()

    pl.when(me == last)(chain)
    loads["states"].wait()
    r.gb[pl.ds(0, tokens), state:] = jnp.zeros((tokens, state), F32)
    for block in range(n_blocks):
        if block:
            tick()
        rows = pl.ds(block * SCAN_BLOCK, SCAN_BLOCK)
        r.g_pair[...] = jnp.zeros_like(r.g_pair)

        @pl.loop(0, groups)
        def _(group):
            columns = lanes_of(group, GROUP)
            sizes = mm(r.step_two[block], r.spread[:, columns])
            grown = mm(r.grow_two[block], r.spread[:, columns])
            stepped = (r.xc[rows, columns].astype(F32) * sizes).astype(BF16)
            g_out = r.gq[rows, columns]
            g_low = g_out.astype(BF16)
            rolled = columns_of(r, block, group, per_group)
            r.gb[rows, state:] += mm(
                (g_out * grown).astype(BF16), r.states[block, :, columns].astype(BF16), NT
            )
            upper, lower, up_factors, low_factors = [], [], [], []
            for head in range(per_group):
                along = r.run_t[block, pl.ds(per_group * group + head, 1), :]
                down = rolled[:, head : head + 1]
                up_factors.append(jnp.exp2(jnp.minimum(along - down[:HALF], 0.0)))
                upper.append((r.pair[block, :HALF, :] * up_factors[head]).astype(BF16))
                low_factors.append(jnp.exp2(jnp.minimum(along[:, HALF:] - down[HALF:], 0.0)))
                lower.append((r.pair[block, HALF:, HALF:] * low_factors[head]).astype(BF16))
            upper = own_lanes(mm(jnp.concatenate(upper, axis=0), g_low), per_group, head_size)
            lower = own_lanes(mm(jnp.concatenate(lower, axis=0), g_low[HALF:]), per_group, head_size)
            ones = [stepped * head_row(head, head_size) for head in range(per_group)]
            up_pairs = mm(jnp.concatenate([one[:HALF] for one in ones], axis=0), g_low, NT)
            low_pairs = mm(jnp.concatenate([one[HALF:] for one in ones], axis=0), g_low[HALF:], NT)
            pair_upper = up_pairs[:HALF] * up_factors[0]
            pair_lower = low_pairs[:HALF] * low_factors[0]
            for head in range(1, per_group):
                span = slice(head * HALF, (head + 1) * HALF)
                pair_upper = pair_upper + up_pairs[span] * up_factors[head]
                pair_lower = pair_lower + low_pairs[span] * low_factors[head]
            r.gx[rows, columns] = jnp.concatenate([upper, lower], axis=0)
            r.g_pair[:HALF, :] += pair_upper
            r.g_pair[HALF:, HALF:] += pair_lower

        g_scores = jnp.where(row_id <= col_id, r.g_pair[...], 0.0)
        r.gb[rows, :state] = mm(g_scores.astype(BF16), r.bc[rows, state:])
        r.gb[rows, state:] += mm(g_scores.T.astype(BF16), r.bc[rows, :state])
        if block < n_blocks - 1:
            pl.when(me == last - 1)(chain)

    pl.when(me < (last - 1 if n_blocks > 1 else last))(chain)
    r.direct[...] = jnp.zeros_like(r.direct)
    for block in reversed(range(n_blocks)):
        if block == n_blocks - 1:
            tick()
        rows = pl.ds(block * SCAN_BLOCK, SCAN_BLOCK)

        @pl.loop(0, groups)
        def _(group):
            columns = lanes_of(group, GROUP)
            sizes = mm(r.step_two[block], r.spread[:, columns])
            keeps = mm(r.keep_two[block], r.spread[:, columns])
            x_here = r.xc[rows, columns].astype(F32)
            stepped = x_here * sizes
            d_here = r.d_states[block + 1, :, columns].astype(BF16)
            d_x = r.gx[rows, columns] + keeps * mm(r.bc[rows, :state], d_here)
            r.gb[rows, :state] += mm((stepped * keeps).astype(BF16), d_here, NT)
            sums = collected(
                jnp.concatenate([d_x * x_here, d_x * stepped.astype(BF16).astype(F32)], axis=0), columns
            )
            r.direct[rows, :] += sums[:SCAN_BLOCK]
            r.g_run[rows, :] -= sums[SCAN_BLOCK:]
            r.gx[rows, columns] = sizes * d_x + r.skip[0:1, columns] * r.gq[rows, columns]

    raw_load = load("xraw", r.gq, 14)
    for block in range(n_blocks):
        rows = pl.ds(block * SCAN_BLOCK, SCAN_BLOCK)
        end_sum = jnp.broadcast_to(
            jnp.sum(r.d_states[block + 1] * r.states[block + 1], axis=0, keepdims=True), (8, inner)
        )
        at_end = collected(end_sum, slice(None))[0:1, :]
        rate = r.heads[layer, 1:2, :]
        g_rate = exact((row_id <= col_id).astype(F32), r.g_run[rows, :]) + at_end
        g_dt = (rate * g_rate + r.direct[rows, :]) * r.live[rows, :] * jax.nn.sigmoid(r.dtp[rows, :])
        r.pd[rows, :] = g_dt.astype(BF16)
        r.g_heads[0:1, :] += jnp.sum(g_dt, axis=0, keepdims=True)
        r.g_heads[1:2, :] += jnp.sum(g_rate * r.dt[block], axis=0, keepdims=True) * rate
    tick()

    def before_conv(taps, raw, grad, columns):
        for start in range(0, tokens, ROWS):
            rows = pl.ds(start, ROWS)
            before = conv_rows(raw, taps, start, columns)
            sig = jax.nn.sigmoid(before)
            grad[rows, columns] = grad[rows, columns] * (sig * (1.0 + before * (1.0 - sig)))

    def through_conv(taps, raw, grad, columns, name, tile, low):
        sums = [jnp.zeros((1, GROUP), F32) for tap in range(WIDTH + 1)]
        for start in range(0, tokens, ROWS):
            total = jnp.zeros((ROWS, GROUP), F32)
            here = grad[pl.ds(start, ROWS), columns]
            for tap in range(WIDTH):
                shift = WIDTH - 1 - tap
                total = total + taps(tap, columns) * grad[pl.ds(start + shift, ROWS), columns]
                sums[tap] = sums[tap] + jnp.sum(
                    here * raw[pl.ds(PAD - shift + start, ROWS), columns], axis=0, keepdims=True
                )
            sums[WIDTH] = sums[WIDTH] + jnp.sum(here, axis=0, keepdims=True)
            low[pl.ds(start, ROWS), columns] = total.astype(BF16)
        for tap in range(WIDTH + 1):
            put_small(name, tap * (grad.shape[1] // LANES), tile, sums[tap])

    earlier.drain()
    wn_load = load("wn", r.g_narrow, 15)
    loads["braw"].wait()
    for step in range(2 * state // GROUP):
        before_conv(taps_of(r.conv_bc, layer), r.braw, r.gb, pl.ds(step * GROUP, GROUP))
    raw_load.wait()

    @pl.loop(0, groups)
    def _(step):
        before_conv(taps_of(r.conv_x, layer), r.gq, r.gx, lanes_of(step, GROUP))

    halo_copies = [
        remote(
            buffer.at[pl.ds(0, PAD), :],
            buffer.at[pl.ds(tokens, PAD), :],
            r.halo_send.at[index],
            r.halo_recv.at[index],
            previous,
        )
        for index, buffer in enumerate((r.gx, r.gb))
    ]

    @pl.when(me > 0)
    def _():
        for copy in halo_copies:
            copy.start()

    wn_load.wait()
    split_narrow(r, r.g_narrow)
    put_rows(r.g_narrow, pl.ds(2 * state, LANES), mm(r.normed_t[...], r.pd[...]))
    put_rows(r.g_narrow, pl.ds(2 * state + LANES, LANES), jnp.zeros((width, LANES), F32))
    loads["wz"].wait()
    r.g_gain[...] = jnp.zeros_like(r.g_gain)

    @pl.loop(0, width // GROUP)
    def _(step):
        columns = lanes_of(step, GROUP)
        r.gn[:, columns] = mm(r.pz[...], r.wz[columns, :], NT) + mm(r.pd[...], r.wdt[columns, :], NT)

    tick()

    @pl.when(me < last)
    def _():
        for copy in halo_copies:
            copy.wait_recv()

    @pl.when(me == last)
    def _():
        for buffer in (r.gx, r.gb):
            buffer[pl.ds(tokens, PAD), :] = jnp.zeros((PAD, buffer.shape[1]), F32)

    for step in range(2 * state // GROUP):
        columns = pl.ds(step * GROUP, GROUP)
        through_conv(
            taps_of(r.conv_bc, layer), r.braw, r.gb, columns, places.tap_b, step * (GROUP // LANES), r.pb
        )
        put_rows(r.g_narrow, columns, mm(r.normed_t[...], r.pb[:, columns]))
    stores = []

    def store(source, target):
        copy = pltpu.make_async_copy(source, target, r.store_sem.at[len(stores)])
        copy.start()
        stores.append(copy)

    final = Rounds()
    if cfg.closing:
        enqueue(final, r.g_wx, r.close_wx.shape[1], put_wide(r.close_wx))
        enqueue(final, r.g_narrow, LANES, put_narrow(r.close_narrow))
    else:
        store(r.g_narrow, r.g_narrow_out)

    for first in range(0, groups, groups // 2):

        @pl.loop(first, first + groups // 2)
        def _(step):
            columns = lanes_of(step, GROUP)
            through_conv(
                taps_of(r.conv_x, layer), r.gq, r.gx, columns, places.tap_x, step * (GROUP // LANES), r.px
            )
            put_rows(r.g_wx, columns, mm(r.normed_t[...], r.px[:, columns]))

        tick()

    own.drain()
    if cfg.closing:
        final.start()
    else:
        store(r.g_wx, r.g_wx_out)
    wx_load.wait()

    @pl.loop(0, width // GROUP)
    def _(step):
        columns = lanes_of(step, GROUP)
        r.gn[:, columns] += mm(r.px[...], r.wo[columns, :], NT) + mm(r.pb[...], r.wbc[columns, :], NT)

    final.tick()
    r.g_small[pl.ds(places.heads, 8), :] = r.g_heads[...]
    r.g_small[pl.ds(places.gain, 8), :] = jnp.zeros((8, LANES), F32)
    gain = r.in_gain[layer : layer + 1, :]

    @pl.loop(0, tokens // ROWS)
    def _(step):
        rows = rows_of(step, ROWS)
        values = r.h[rows, :].astype(F32)
        inv = lax.rsqrt(jnp.mean(values * values, axis=-1, keepdims=True) + EPS)
        g_normed = r.gn[rows, :]
        r.g_gain[0:1, :] += jnp.sum(g_normed * values * inv, axis=0, keepdims=True)
        scaled = g_normed * gain
        along_h = jnp.mean(scaled * values, axis=-1, keepdims=True)
        r.gh_next[rows, :] = (
            r.gh[rows, :].astype(F32) * r.live[rows, 0:1]
            + inv * scaled
            - values * (inv * inv * inv * along_h)
        ).astype(r.gh_next.dtype)

    put_small(places.gain, 0, 0, r.g_gain[0:1, :])
    if cfg.closing:
        close(cfg, at, r, final)
    for copy in turned:
        copy.wait()
    if not direct:
        store(r.g_wo, r.g_wo_out)
        store(r.g_wz, r.g_wz_out)
    for copy in stores:
        copy.wait()

    @pl.when(me > 0)
    def _():
        for copy in halo_copies + carry_copies:
            copy.wait_send()


def greet_back(at):
    runner = at.dp // at.parts
    for j in range(at.n_dp):

        @pl.when((j != at.dp) | (runner != at.tensor))
        def _():
            greet({DP: j, TENSOR: runner})

    return at.n_dp - (runner == at.tensor).astype(jnp.int32)


def close(cfg, at, r, final):
    runner = at.dp // at.parts
    at_home = runner == at.tensor
    depth = at.depth
    piece = r.returned.shape[1]
    quarter = r.packed.shape[1] // depth
    for layer in range(cfg.layer + 1, cfg.layers):
        r.packed[layer] = getattr(r, f"small{layer}")[...]
    r.packed[cfg.layer] = r.g_small[...]

    def part(index):
        return pl.ds(pl.multiple_of(index * quarter, 8), quarter)

    first = remote(r.packed, r.small_core, r.small_send.at[0], r.small_recv.at[0], over_core(at))
    second = remote(r.sum_core, r.small_x, r.small_send.at[1], r.small_recv.at[1], over_x(at))
    third = remote(r.sum_x, r.small_y, r.small_send.at[2], r.small_recv.at[2], over_y(at))
    fourth = [
        remote(
            r.sum_y.at[:, part(lax.rem(at.z + k, depth))],
            r.small_z.at[k - 1],
            r.small_send.at[2 + k],
            r.small_recv.at[2 + k],
            over_z(at, k),
        )
        for k in range(1, depth)
    ]
    fifth = [
        remote(
            r.small_sum.at[:, part(at.z)],
            r.small_sum.at[:, part(at.z)],
            r.small_send.at[1 + depth + k],
            r.small_recv.at[1 + depth + k],
            over_z(at, k),
        )
        for k in range(1, depth)
    ]
    back = []
    for k in range(at.parts):
        for other in range(at.n_tensor):
            owner = at.tensor * at.parts + k
            copy = remote(
                r.gh_next.at[pl.ds((k * at.n_tensor + other) * piece, piece), :],
                r.returned.at[at.dp],
                r.back_send.at[k, other],
                r.back_recv.at[at.dp],
                {DP: owner, TENSOR: other},
            )
            away = (owner != at.dp) | (other != at.tensor)
            back.append((copy, away))
            pl.when(away)(copy.start)
    own_slot = lax.rem(at.dp, at.parts) * at.n_tensor + at.tensor
    keep = pltpu.make_async_copy(
        r.gh_next.at[pl.ds(pl.multiple_of(own_slot * piece, PAD), piece), :],
        r.returned.at[at.dp],
        r.back_own,
    )
    pl.when(at_home)(keep.start)

    first.start()
    final.tick()
    first.wait_recv()
    r.sum_core[...] = r.packed[...] + r.small_core[...]
    second.start()
    final.tick()
    second.wait_recv()
    r.sum_x[...] = r.sum_core[...] + r.small_x[...]
    third.start()
    final.tick()
    third.wait_recv()
    r.sum_y[...] = r.sum_x[...] + r.small_y[...]
    for copy in fourth:
        copy.start()
    final.finish(len(final.units) - 1)
    r.narrow[cfg.layer, at.tensor] = r.close_narrow[...]
    for layer in range(cfg.layer + 1, cfg.layers):
        r.narrow[layer, at.tensor] = (r.sum_narrow if layer == cfg.layer + 1 else getattr(r, f"narrow{layer}"))[...]
    spread = [
        remote(
            r.narrow.at[:, at.tensor],
            r.narrow.at[:, at.tensor],
            r.narrow_send.at[k - 1],
            r.narrow_recv.at[k - 1],
            {TENSOR: lax.rem(at.tensor + k, at.n_tensor)},
        )
        for k in range(1, at.n_tensor)
    ]
    for copy in spread:
        copy.start()
    value = r.sum_y[:, part(at.z)]
    for k, copy in enumerate(fourth):
        copy.wait_recv()
        value = value + r.small_z[k]
    r.small_sum[:, part(at.z)] = value
    for copy in fifth:
        copy.start()
    final.drain()
    for j in range(at.n_dp):
        arrival = remote(
            r.gh_next.at[pl.ds(0, piece), :],
            r.returned.at[j],
            r.back_send.at[0, 0],
            r.back_recv.at[j],
            {TENSOR: lax.rem(at.tensor + 1, at.n_tensor)},
        )
        pl.when((j != at.dp) | (runner != at.tensor))(arrival.wait_recv)
    pl.when(at_home)(keep.wait)
    for index in range(at.n_dp):
        source = jnp.int32(0)
        for j in range(1, at.n_dp):
            source = jnp.where(r.order[j] == index, j, source)
        r.input_grad[index] = r.returned[source]
    for copy in fifth + spread:
        copy.wait_recv()
    for copy in [first, second, third] + fourth + fifth + spread:
        copy.wait_send()
    for copy, away in back:
        pl.when(away)(copy.wait_send)


def layer_backward(cfg, at, gh, h, h_next, params, saved, weights, prior, turn, others):
    tokens, width = h.shape
    inner, state = cfg.inner, cfg.state
    n_blocks = tokens // SCAN_BLOCK
    depth, rows = at.n_dp // 2, width // at.n_dp
    part = inner // at.n_tensor
    piece = tokens // at.n_dp
    narrow = at.n_tensor * LANES
    small_shape = (small_rows(width, inner, state).all, LANES)

    def blocked(columns):
        return (depth, 2, rows, columns) if cfg.direct else (width, columns)

    ins = dict(gh=(gh, VMEM), h=(h, VMEM), h_next_in=(h_next, ANY), **param_inputs(params))
    for name in SAVED + TERMS + CONSTANTS:
        ins[name + "_in"] = (saved[name], ANY)
    for name in ("wz", "wx", "wo"):
        ins[name + "_in"] = (weights[name], ANY)
    ins["wn_in"] = (weights["wn"].reshape(blocked(narrow)), ANY)
    outs = {}
    scratch = common_scratch(
        param_shapes(params), width, inner, state, n_blocks, tokens, at.n_tensor, depth
    )
    scratch.update(
        carry_out=vmem((inner // GROUP, state, GROUP), BF16),
        carry_in=vmem((inner // GROUP, state, GROUP), BF16),
        carry_send=DMA((inner // GROUP,)),
        carry_recv=DMA((inner // GROUP,)),
        nx=vmem((PAD + tokens, width), BF16),
        wz=vmem((width, inner), BF16),
        wo=vmem((width, inner), BF16),
        collect=vmem((inner, LANES), BF16),
        gate=vmem((2, tokens, GROUP)),
        mixed=vmem((2, tokens, GROUP)),
        stream_sem=DMA((2, 2)),
        braw=vmem((PAD + tokens, 2 * state)),
        g_branch=vmem((tokens, width), BF16),
        g_branch_t=vmem((width, tokens), BF16),
        normed_t=vmem((width, tokens), BF16),
        along=vmem((tokens, LANES)),
        c_t=vmem((n_blocks, state, SCAN_BLOCK), BF16),
        g_run=vmem((tokens, LANES)),
        direct=vmem((tokens, LANES)),
        g_heads=vmem((8, LANES)),
        g_gain=vmem((8, width)),
        go=vmem((tokens, GROUP), BF16),
        gq=vmem((PAD + tokens, inner)),
        gx=vmem((tokens + PAD, inner)),
        gb=vmem((tokens + PAD, 2 * state)),
        pz=vmem((tokens, inner), BF16),
        px=vmem((tokens, inner), BF16),
        pb=vmem((tokens, 2 * state), BF16),
        pd=vmem((tokens, LANES), BF16),
        d_states=vmem((n_blocks + 1, state, inner)),
        g_pair=vmem((SCAN_BLOCK, SCAN_BLOCK)),
        gn=vmem((tokens, width)),
        g_wo=vmem(blocked(inner), BF16),
        g_wz=vmem(blocked(inner), BF16),
        g_wx=vmem(blocked(inner), BF16),
        g_narrow=vmem(blocked(narrow), BF16),
        halo_send=DMA((2,)),
        halo_recv=DMA((2,)),
    )
    small, wide = shaped(small_shape), shaped((rows, part))
    if cfg.closing:
        scratch.update(gh_next=vmem((tokens, width), BF16), g_small=vmem(small_shape))
    else:
        outs.update(
            gh_next=(shaped((tokens, width), F32 if cfg.layer else BF16), VMEM),
            g_small=(small, VMEM),
            g_wx_out=(shaped(blocked(inner), BF16), ANY),
            g_narrow_out=(shaped(blocked(narrow), BF16), ANY),
        )
    if cfg.direct:
        total = 2 * (part // LANES)
        outs.update(sum_wo=(wide, VMEM), sum_wz=(wide, VMEM))
        if cfg.more:
            total += part // LANES + 1
            ins["prior_wx_in"] = (prior["g_wx_out"], ANY)
            ins["prior_narrow_in"] = (prior["g_narrow_out"], ANY)
            outs.update(sum_wx=(wide, VMEM), sum_narrow=(shaped((rows, LANES)), VMEM))
        if cfg.turn:
            ins["turn_in"] = (turn, VMEM)
            outs["turned"] = (shaped(turn.shape, BF16), ANY)
            scratch.update(turn_sems(at))
        if cfg.closing:
            total += part // LANES + 1
            packed = (cfg.layers,) + small_shape
            quarter = (cfg.layers, small_shape[0] // depth, LANES)
            for layer in range(1, cfg.layers):
                ins[f"small{layer}"] = (others[layer]["small"], VMEM)
                if layer > 1:
                    ins[f"narrow{layer}"] = (others[layer]["narrow"], VMEM)
            outs.update(
                close_wx=(wide, VMEM),
                narrow=(shaped((cfg.layers, at.n_tensor, rows, LANES)), VMEM),
                small_sum=(shaped(packed), VMEM),
                input_grad=(shaped((at.n_dp, piece, width), BF16), VMEM),
            )
            scratch.update(
                close_narrow=vmem((rows, LANES)),
                returned=vmem((at.n_dp, piece, width), BF16),
                packed=vmem(packed),
                small_core=vmem(packed),
                small_x=vmem(packed),
                small_y=vmem(packed),
                sum_core=vmem(packed),
                sum_x=vmem(packed),
                sum_y=vmem(packed),
                small_z=vmem((depth - 1,) + quarter),
                small_send=DMA((1 + 2 * depth,)),
                small_recv=DMA((1 + 2 * depth,)),
                back_send=DMA((at.parts, at.n_tensor)),
                back_recv=DMA((at.n_dp,)),
                back_own=DMA,
                narrow_send=DMA((at.n_tensor - 1,)),
                narrow_recv=DMA((at.n_tensor - 1,)),
            )
        scratch.update(reduce_scratch(total, depth, rows))
    else:
        outs.update(
            g_wo_out=(shaped((width, inner), BF16), ANY),
            g_wz_out=(shaped((width, inner), BF16), ANY),
        )
    return call_kernel(
        partial(backward_body, cfg), f"layer_{cfg.layer}_backward", 11 + cfg.layer, ins, outs, scratch
    )


def deal_sources(at):
    return [(at.tensor * at.parts + k, other) for k in range(at.parts) for other in range(at.n_tensor)]


def finish_body(cfg, r):
    tensor = lax.axis_index(TENSOR)
    places = small_rows(cfg.width, cfg.inner, cfg.state)
    own = cfg.heads // r.narrow.shape[1]
    row = lax.broadcasted_iota(jnp.int32, (own, LANES), 0)
    column = lax.broadcasted_iota(jnp.int32, (own, LANES), 1)
    pick = (row + tensor * own == column).astype(F32)
    r.out_block[...] = r.block[...]
    r.out_grad[...] = r.grad[...]

    def lay_out(target, layer, start, rows, tiles):
        for k in range(rows):
            for tile in range(tiles):
                value = r.small_sum[layer, pl.ds(start + k * tiles + tile, 1), :]
                columns = pl.ds(tile * LANES, LANES)
                if len(target.shape) == 3:
                    target[k, pl.ds(layer, 1), columns] = value
                else:
                    target[pl.ds(layer, 1), columns] = value

    for layer in range(cfg.layers):
        for name in ("wz", "wx", "wo"):
            getattr(r, "out_" + name)[layer] = getattr(r, f"{name}{layer}")[...]
        for side in range(2):
            r.out_bc[layer, :, side * LANES : (side + 1) * LANES] = r.narrow[layer, side]
        picked = lax.dot_general(
            pick, r.narrow[layer, 2], NT, precision=lax.Precision.HIGHEST, preferred_element_type=F32
        )
        for k in range(own):
            r.out_dt[k, pl.ds(layer, 1), :] = picked[k : k + 1, :]
        lay_out(r.out_gain, layer, places.gain, 1, cfg.width // LANES)
        lay_out(r.out_gate_gain, layer, places.gate_gain, 1, cfg.inner // LANES)
        lay_out(r.out_tap_x, layer, places.tap_x, WIDTH + 1, cfg.inner // LANES)
        lay_out(r.out_tap_b, layer, places.tap_b, WIDTH + 1, 2 * cfg.state // LANES)
        for index, target in enumerate((r.out_bias, r.out_alog, r.out_skip)):
            target[pl.ds(layer, 1), :] = r.small_sum[
                layer, pl.ds(places.heads + index, 1), : cfg.heads
            ]


def finish(cfg, block, grad, sums, narrow, small_sum):
    layers, tensor, rows, _ = narrow.shape
    part = cfg.inner // tensor
    ins = dict(
        block=(block, VMEM), grad=(grad, VMEM), narrow=(narrow, VMEM), small_sum=(small_sum, VMEM)
    )
    for layer in range(layers):
        for name in ("wz", "wx", "wo"):
            ins[f"{name}{layer}"] = (sums[layer][name], VMEM)
    wide = (shaped((layers, rows, part)), VMEM)
    per_head = (shaped((layers, cfg.heads)), VMEM)
    outs = dict(
        out_block=(shaped(block.shape, BF16), VMEM),
        out_grad=(shaped(grad.shape, BF16), VMEM),
        out_gain=(shaped((layers, cfg.width)), VMEM),
        out_wz=wide,
        out_wx=wide,
        out_bc=(shaped((layers, rows, 2 * cfg.state)), VMEM),
        out_dt=(shaped((cfg.heads // tensor, layers, rows)), VMEM),
        out_tap_x=(shaped((WIDTH + 1, layers, cfg.inner)), VMEM),
        out_tap_b=(shaped((WIDTH + 1, layers, 2 * cfg.state)), VMEM),
        out_bias=per_head,
        out_alog=per_head,
        out_skip=per_head,
        out_gate_gain=(shaped((layers, cfg.inner)), VMEM),
        out_wo=wide,
    )
    results = call_kernel(partial(finish_body, cfg), "finish", None, ins, outs, {})
    for name, order in (("out_dt", (1, 2, 0)), ("out_tap_x", (1, 0, 2)), ("out_tap_b", (1, 0, 2))):
        results[name] = results[name].transpose(order)
    return tuple(results.values())


def local(
    hidden_in,
    lengths,
    order,
    in_gain,
    w_z,
    w_x,
    w_bc,
    w_dt,
    conv_x,
    conv_bc,
    dt_bias,
    a_log,
    d_skip,
    gated_gain,
    w_out,
    cotangent,
):
    at = place()
    n_dp, n_tensor = at.n_dp, at.n_tensor
    piece = hidden_in.shape[2]
    width = hidden_in.shape[3]
    tokens = piece * n_dp
    layers = w_z.shape[0]
    inner = gated_gain.shape[1]
    heads = dt_bias.shape[1]
    state = conv_bc.shape[2] // 2
    rows_local = w_z.shape[1]
    part = w_z.shape[2]
    direct = rows_local % 16 == 0 and piece % 16 == 0 and n_tensor == 4 and n_dp % 2 == 0

    quarter = 2 * state // n_tensor
    narrow = jnp.concatenate(
        [lax.dynamic_slice_in_dim(w_bc, at.tensor * quarter, quarter, 2), w_dt], axis=2
    )
    narrow = jnp.pad(narrow, ((0, 0), (0, 0), (0, LANES - narrow.shape[2])))
    blocks = dict(wz=w_z, wx=w_x, wn=narrow, wo=w_out)
    params = dict(
        lengths=lengths,
        order=order,
        in_gain=in_gain,
        conv_x=conv_x.transpose(1, 0, 2),
        conv_bc=conv_bc.transpose(1, 0, 2),
        dt_bias=dt_bias,
        a_log=a_log,
        d_skip=d_skip,
        gated_gain=gated_gain,
    )

    def to_run(values):
        swapped = lax.all_to_all(
            values.reshape(n_tensor, at.parts, piece, width), TENSOR, split_axis=0, concat_axis=0
        )
        return swapped.transpose(1, 0, 2, 3).reshape(tokens, width)

    def to_pieces(values):
        swapped = values.reshape(at.parts, n_tensor, piece, width).transpose(1, 0, 2, 3)
        return lax.all_to_all(swapped, TENSOR, split_axis=0, concat_axis=0).reshape(
            n_dp, piece, width
        )

    def config(layer):
        return SimpleNamespace(
            layer=layer,
            layers=layers,
            direct=direct,
            more=layer + 1 < layers,
            turn=layer + 1 == layers,
            closing=direct and layer == 0,
            tokens=tokens,
            width=width,
            inner=inner,
            state=state,
            heads=heads,
            head_size=inner // heads,
        )

    weights = [{} for layer in range(layers)]
    if direct:
        hidden = hidden_in[:, 0]
    else:
        arranged = jnp.take(hidden_in, order, axis=0)
        dealt = lax.all_to_all(arranged, DP, split_axis=0, concat_axis=1, tiled=True)
        hidden = to_run(dealt[0])

        def whole(stacked):
            gathered = lax.all_gather(stacked, DP, axis=1, tiled=True)
            return lax.all_gather(gathered, TENSOR, axis=2, tiled=True)

        for name, block in blocks.items():
            stacked = whole(block)
            for layer in range(layers):
                weights[layer][name] = stacked[layer]
    forward = layers_forward(config(0), at, hidden, params, weights, blocks, cotangent[0])
    if direct:
        hidden = forward["hidden"]
        for layer in range(layers):
            for name in blocks:
                weights[layer][name] = forward[f"whole_{name}{layer}"].reshape(width, -1)
        grad = forward["turned"].reshape(tokens, width)
    else:
        grad = to_run(cotangent[0])
    inputs = [hidden] + [forward[f"h{layer + 1}"] for layer in range(layers)]
    kept = [
        {name: forward[f"{name}{layer}_out"] for name in SAVED + TERMS} for layer in range(layers)
    ]
    for saved in kept:
        saved.update({name: forward[name + "_out"] for name in CONSTANTS})
    h_low = forward["h_low"]
    sums = [{} for layer in range(layers)]
    results = None
    for layer in reversed(range(layers)):
        results = layer_backward(
            config(layer),
            at,
            grad,
            inputs[layer],
            inputs[layer + 1],
            params,
            kept[layer],
            weights[layer],
            results,
            h_low.reshape(n_dp, piece, width),
            sums,
        )
        if direct:
            sums[layer].update(wo=results["sum_wo"], wz=results["sum_wz"])
            if layer + 1 < layers:
                sums[layer + 1].update(wx=results["sum_wx"], narrow=results["sum_narrow"])
            if layer + 1 == layers:
                block_out = results["turned"]
            if layer:
                grad, sums[layer]["small"] = results["gh_next"], results["g_small"]
        else:
            grad, sums[layer]["small"] = results["gh_next"], results["g_small"]
            for name in ("wo", "wz", "wx", "narrow"):
                sums[layer][name] = results[f"g_{name}_out"]

    if direct:
        sums[0]["wx"] = results["close_wx"]
        input_grad = results["input_grad"][:, None]
        narrow_sum, small_sum = results["narrow"], results["small_sum"]
    else:
        block_out = to_pieces(h_low)
        returned = lax.all_to_all(
            to_pieces(grad)[None], DP, split_axis=1, concat_axis=0, tiled=True
        )
        input_grad = jnp.zeros_like(returned).at[order].set(returned)

        def scattered(name):
            terms = jnp.stack([entry[name] for entry in sums]).astype(F32)
            mine = lax.psum_scatter(terms, DP, scatter_dimension=1, tiled=True)
            return lax.psum_scatter(mine, TENSOR, scatter_dimension=2, tiled=True)

        for name in ("wz", "wx", "wo"):
            total = scattered(name)
            for layer in range(layers):
                sums[layer][name] = total[layer]
        narrow_sum = lax.all_gather(scattered("narrow"), TENSOR, axis=1)
        small_sum = lax.psum(jnp.stack([entry["small"] for entry in sums]), (DP, TENSOR))
    return finish(config(0), block_out[None], input_grad, sums, narrow_sum, small_sum)


def solution(mesh):
    return jax.shard_map(
        local,
        mesh=mesh,
        in_specs=(
            P(None, DP, TENSOR, None),
            P(),
            P(),
            P(),
            P(None, DP, TENSOR),
            P(None, DP, TENSOR),
            P(None, DP, None),
            P(None, DP, TENSOR),
            P(),
            P(),
            P(),
            P(),
            P(),
            P(),
            P(None, DP, TENSOR),
            P(DP, None, TENSOR, None),
        ),
        out_specs=(
            P(DP, None, TENSOR, None),
            P(None, DP, TENSOR, None),
            P(),
            P(None, DP, TENSOR),
            P(None, DP, TENSOR),
            P(None, DP, None),
            P(None, DP, TENSOR),
            P(),
            P(),
            P(),
            P(),
            P(),
            P(),
            P(None, DP, TENSOR),
        ),
        check_vma=False,
    )
```

```python
from functools import partial
from types import SimpleNamespace

import jax
import jax.numpy as jnp
from jax import lax
from jax.experimental import pallas as pl
from jax.experimental.pallas import tpu as pltpu
from jax.sharding import PartitionSpec as P

SCAN_BLOCK = 256
HALF = SCAN_BLOCK // 2
EPS = 1e-05
LOG2E = 1.4426950408889634
F32, BF16 = jnp.float32, jnp.bfloat16
LANES = 128
GROUP = 256
PAD = 16
ROWS = 128
WIDTH = 4
NN = (((1,), (0,)), ((), ()))
NT = (((1,), (1,)), ((), ()))
MESH = pl.DeviceIdType.MESH
VMEM = pl.BlockSpec(memory_space=pltpu.VMEM)
SMEM = pl.BlockSpec(memory_space=pltpu.SMEM)
ANY = pl.BlockSpec(memory_space=pl.ANY)
DMA = pltpu.SemaphoreType.DMA
DP, TENSOR = "dp", "tensor"
VMEM_LIMIT = 63 * 1024 * 1024


def mm(left, right, dims=NN):
    return lax.dot_general(left, right, dims, preferred_element_type=F32)


def exact(left, right):
    return lax.dot_general(
        left, right, NN, precision=lax.Precision.HIGHEST, preferred_element_type=F32
    )


def halves(values):
    high = values.astype(BF16)
    return high, (values - high.astype(F32)).astype(BF16)


def beside(values):
    return jnp.concatenate(halves(values), axis=1)


def lanes_of(step, size):
    return pl.ds(pl.multiple_of(step * size, size), size)


def rows_of(step, size, start=0):
    return pl.ds(pl.multiple_of(start + step * size, PAD), size)


def shaped(shape, dtype=F32):
    return jax.ShapeDtypeStruct(shape, dtype)


def vmem(shape, dtype=F32):
    return pltpu.VMEM(shape, dtype)


def call_kernel(body, name, collective_id, ins, outs, scratch):
    names = list(ins) + list(outs) + list(scratch)

    def kernel(*refs):
        body(SimpleNamespace(**dict(zip(names, refs))))

    remote_copies = (
        dict(collective_id=collective_id, has_side_effects=True) if collective_id is not None else {}
    )
    results = pl.pallas_call(
        kernel,
        out_shape=[shape for shape, _ in outs.values()],
        in_specs=[spec for _, spec in ins.values()],
        out_specs=[spec for _, spec in outs.values()],
        scratch_shapes=list(scratch.values()),
        compiler_params=pltpu.CompilerParams(vmem_limit_bytes=VMEM_LIMIT, **remote_copies),
        name=name,
    )(*[array for array, _ in ins.values()])
    return dict(zip(outs, results))


def place():
    dp, tensor = lax.axis_index(DP), lax.axis_index(TENSOR)
    n_dp, n_tensor = lax.axis_size(DP), lax.axis_size(TENSOR)
    return SimpleNamespace(
        dp=dp,
        tensor=tensor,
        n_dp=n_dp,
        n_tensor=n_tensor,
        depth=n_dp // 2,
        core=lax.rem(tensor, 2),
        x=tensor // 2,
        y=lax.rem(dp, 2),
        z=dp // 2,
        parts=n_dp // n_tensor,
    )


def over_core(at):
    return {TENSOR: at.tensor + 1 - 2 * at.core}


def over_x(at):
    return {TENSOR: lax.rem(at.tensor + 2, at.n_tensor)}


def over_y(at):
    return {DP: at.dp + 1 - 2 * at.y}


def over_z(at, k):
    return {DP: lax.rem(at.z + k, at.depth) * 2 + at.y}


def grid_partners(at):
    return [over_core(at), over_x(at), over_y(at)] + [over_z(at, k) for k in range(1, at.depth)]


def tensor_partners(at):
    return [{TENSOR: lax.rem(at.tensor + k, at.n_tensor)} for k in range(1, at.n_tensor)]


def greet(device):
    pl.semaphore_signal(
        pltpu.get_barrier_semaphore(), inc=1, device_id=device, device_id_type=MESH
    )


def greet_all(partners):
    for partner in partners:
        greet(partner)


def met(count):
    pl.semaphore_wait(pltpu.get_barrier_semaphore(), count)


def remote(source, target, send, recv, device):
    return pltpu.make_async_remote_copy(
        src_ref=source,
        dst_ref=target,
        send_sem=send,
        recv_sem=recv,
        device_id=device,
        device_id_type=MESH,
    )


class Rounds:
    def __init__(self):
        self.units = []
        self.next = 0
        self.begun = 0
        self.finished = set()

    def add(self, unit):
        self.units.append(unit)

    def begin(self, count):
        while self.begun < min(count, len(self.units)):
            self.units[self.begun][0]()
            self.begun += 1

    def start(self):
        self.begin(2 * AHEAD)

    def tick(self):
        pairs = -(-len(self.units) // 2)
        if not self.units or self.next >= pairs + STAGES - 1:
            return
        for stage in reversed(range(STAGES)):
            pair = self.next - stage
            if 0 <= pair < pairs:
                for unit in self.units[2 * pair : 2 * pair + 2]:
                    unit[1][stage]()
        self.next += 1
        self.begin(2 * (self.next + AHEAD))

    def ready(self, unit, rounds_ago=0):
        return self.next >= unit // 2 + STAGES + rounds_ago or self.finished.issuperset({unit})

    def finish(self, unit):
        while not self.ready(unit):
            self.tick()
        if unit not in self.finished:
            self.finished.add(unit)
            self.units[unit][2]()

    def drain(self):
        for unit in range(len(self.units)):
            self.finish(unit)


def gather_sems(total, depth):
    return dict(
        gather_z_send=DMA((total, depth - 1)),
        gather_z_recv=DMA((total, depth - 1)),
        gather_send=DMA((total, 5)),
        gather_recv=DMA((total, 5)),
        gather_own=DMA((total,)),
    )


def gather_unit(at, r, index, block, whole, start, full):
    core, x, y, z = at.core, at.x, at.y, at.z

    def lanes(side):
        return pl.ds(pl.multiple_of((2 * side + core) * full + start, LANES), LANES)

    def same(part, slot, device):
        return remote(
            part, part, r.gather_send.at[index, slot], r.gather_recv.at[index, slot], device
        )

    mine = block.at[:, pl.ds(start, LANES)]
    keep = pltpu.make_async_copy(mine, whole.at[z, y, :, lanes(x)], r.gather_own.at[index])
    along_z = [
        remote(
            mine,
            whole.at[z, y, :, lanes(x)],
            r.gather_z_send.at[index, k - 1],
            r.gather_z_recv.at[index, k - 1],
            over_z(at, k),
        )
        for k in range(1, at.depth)
    ]
    if index % 2 == 0:
        one = [same(whole.at[:, y, :, lanes(x)], 0, over_x(at))]
        two = [same(whole.at[:, y, :, lanes(side)], 1 + side, over_y(at)) for side in range(2)]
    else:
        one = [same(whole.at[:, y, :, lanes(x)], 0, over_y(at))]
        two = [same(whole.at[:, :, :, lanes(x)], 1, over_x(at))]
    last = [same(whole.at[:, :, :, lanes(side)], 3 + side, over_core(at)) for side in range(2)]

    def begin():
        keep.start()
        for copy in along_z:
            copy.start()

    def hand_on(before, after):
        def step():
            for copy in before:
                copy.wait_recv()
            for copy in after:
                copy.start()

        return step

    def first():
        keep.wait()
        hand_on(along_z, one)()

    def finish():
        for copy in last:
            copy.wait_recv()
        for copy in along_z + one + two + last:
            copy.wait_send()

    return begin, [first, hand_on(one, two), hand_on(two, last)], finish


def reduce_scratch(total, depth, rows):
    scratch = dict(
        reduce_send=DMA((total, 4)),
        reduce_recv=DMA((total, 4)),
        reduce_z_send=DMA((total, depth - 1)),
        reduce_z_recv=DMA((total, depth - 1)),
    )
    for index in range(total):
        second = (depth, 2, rows, LANES) if index % 2 == 0 else (2, depth, rows, LANES)
        shapes = ((2, depth, 2, rows, LANES), second, (depth, rows, LANES), (depth - 1, rows, LANES))
        for stage, shape in enumerate(shapes):
            scratch[f"sum{stage}_{index}"] = vmem(shape, BF16)
    return scratch


def reduce_unit(at, r, index, source, start, full, put):
    core, x, y, z, depth = at.core, at.x, at.y, at.z, at.depth
    a, b, c, d = (getattr(r, f"sum{stage}_{index}") for stage in range(4))
    send, recv = r.reduce_send, r.reduce_recv
    x_first = index % 2 == 0

    def lanes(side, which):
        return pl.ds(pl.multiple_of((2 * side + which) * full + start, LANES), LANES)

    zero = [
        remote(
            source.at[:, :, :, lanes(side, 1 - core)],
            a.at[side],
            send.at[index, side],
            recv.at[index, side],
            over_core(at),
        )
        for side in range(2)
    ]
    if x_first:
        one = remote(a.at[1 - x], b, send.at[index, 2], recv.at[index, 2], over_x(at))
        two = remote(b.at[:, 1 - y], c, send.at[index, 3], recv.at[index, 3], over_y(at))
    else:
        one = remote(a.at[:, :, 1 - y], b, send.at[index, 2], recv.at[index, 2], over_y(at))
        two = remote(b.at[1 - x], c, send.at[index, 3], recv.at[index, 3], over_x(at))
    three = [
        remote(
            c.at[lax.rem(z + k, depth)],
            d.at[k - 1],
            r.reduce_z_send.at[index, k - 1],
            r.reduce_z_recv.at[index, k - 1],
            over_z(at, k),
        )
        for k in range(1, depth)
    ]

    def plus(left, right):
        return (left.astype(F32) + right.astype(F32)).astype(BF16)

    def begin():
        for copy in zero:
            copy.start()

    def after_core():
        for copy in zero:
            copy.wait_recv()

        @pl.loop(0, 2 * depth)
        def _(step):
            high, low = step // 2, lax.rem(step, 2)
            for side in range(2):
                a[side, high, low] = plus(a[side, high, low], source[high, low, :, lanes(side, core)])

        one.start()

    def after_first():
        one.wait_recv()

        @pl.loop(0, depth)
        def _(high):
            for side in range(2):
                if x_first:
                    b[high, side] = plus(b[high, side], a[x, high, side])
                else:
                    b[side, high] = plus(b[side, high], a[side, high, y])

        two.start()

    def after_second():
        two.wait_recv()

        @pl.loop(0, depth)
        def _(high):
            c[high] = plus(c[high], b[high, y] if x_first else b[x, high])

        for copy in three:
            copy.start()

    def finish():
        value = c[z].astype(F32)
        for k, copy in enumerate(three):
            copy.wait_recv()
            value = value + d[k].astype(F32)
        put(value)
        for copy in zero + [one, two] + three:
            copy.wait_send()

    return begin, [after_core, after_first, after_second], finish


STAGES = 3
AHEAD = 2


def conv_rows(raw, taps, start, columns):
    total = taps(WIDTH, columns)
    for tap in range(WIDTH):
        first = PAD - (WIDTH - 1) + tap + start
        total = total + taps(tap, columns) * raw[pl.ds(first, ROWS), columns]
    return total


def taps_of(ref, layer):
    def taps(tap, columns):
        return ref[tap, pl.ds(layer, 1), columns]

    return taps


def fill_constants(r, at, head_size, state, heads):
    inner = r.spread.shape[1]
    row = lax.broadcasted_iota(jnp.int32, (2 * LANES, inner), 0)
    column = lax.broadcasted_iota(jnp.int32, (2 * LANES, inner), 1)
    r.spread[...] = (lax.rem(row, LANES) == column // head_size).astype(F32).astype(BF16)
    if hasattr(r, "collect"):
        row = lax.broadcasted_iota(jnp.int32, (inner, LANES), 0)
        column = lax.broadcasted_iota(jnp.int32, (inner, LANES), 1)
        r.collect[...] = (row // head_size == column).astype(F32).astype(BF16)
    quarter, own = 2 * state // at.n_tensor, heads // at.n_tensor
    shape = (at.n_tensor * LANES, 2 * state + LANES)
    row = lax.broadcasted_iota(jnp.int32, shape, 0)
    column = lax.broadcasted_iota(jnp.int32, shape, 1)
    block, lane = row // LANES, lax.rem(row, LANES)
    target = jnp.where(
        lane < quarter,
        block * quarter + lane,
        jnp.where(lane < quarter + own, 2 * state + block * own + lane - quarter, -1),
    )
    r.select[...] = (target == column).astype(F32).astype(BF16)


def split_narrow(r, narrow):
    narrow = narrow[...].reshape(r.wbc.shape[0], r.select.shape[0])
    r.wbc[...] = mm(narrow, r.select[:, : r.wbc.shape[1]]).astype(BF16)
    r.wdt[...] = mm(narrow, r.select[:, r.wbc.shape[1] :]).astype(BF16)


def fill_live(r, at):
    tokens = r.live.shape[0]
    length = r.lengths[r.order[at.dp]]
    position = lax.broadcasted_iota(jnp.int32, (tokens, LANES), 0) + at.tensor * tokens
    r.live[...] = (position < length).astype(F32)


def step_terms(r, layer, block):
    rows = pl.ds(block * SCAN_BLOCK, SCAN_BLOCK)
    value = r.dtp[rows, :]
    size = (jnp.maximum(value, 0.0) + jnp.log1p(jnp.exp(-jnp.abs(value)))) * r.live[rows, :]
    r.dt[block] = size
    row_id = lax.broadcasted_iota(jnp.int32, (SCAN_BLOCK, SCAN_BLOCK), 0)
    col_id = lax.broadcasted_iota(jnp.int32, (SCAN_BLOCK, SCAN_BLOCK), 1)
    earlier = (row_id >= col_id).astype(F32)
    running = exact(earlier, size * (r.heads[layer, 1:2, :] * LOG2E))
    r.run[block] = running
    r.run_t[block] = running.T
    total = running[SCAN_BLOCK - 1 : SCAN_BLOCK, :]
    r.step_two[block] = beside(size)
    r.grow_two[block] = beside(jnp.exp2(running))
    r.keep_two[block] = beside(jnp.exp2(total - running))
    whole = jnp.broadcast_to(jnp.exp2(total), (8, LANES))
    r.decay[block] = mm(beside(whole), r.spread[...])


def fill_heads(r):
    heads = r.dt_bias.shape[1]
    row = lax.broadcasted_iota(jnp.int32, (heads, LANES), 0)
    column = lax.broadcasted_iota(jnp.int32, (heads, LANES), 1)
    widen = (row == column).astype(F32)
    for index, values in enumerate((r.dt_bias[...], -jnp.exp(r.a_log[...]), r.d_skip[...])):
        padded = exact(values, widen)
        for layer in range(values.shape[0]):
            r.heads[layer, index : index + 1, :] = padded[layer : layer + 1, :]


def spread_skip(r, layer):
    r.skip[...] = mm(
        beside(jnp.broadcast_to(r.heads[layer, 2:3, :], (8, LANES))), r.spread[...]
    )


def head_row(head, head_size):
    lane = lax.broadcasted_iota(jnp.int32, (1, GROUP), 1)
    return (lane // head_size == head).astype(F32).astype(BF16)


def own_lanes(stacked, per_group, head_size):
    rows = stacked.shape[0] // per_group
    lane = lax.broadcasted_iota(jnp.int32, (1, GROUP), 1) // head_size
    total = stacked[:rows]
    for head in range(1, per_group):
        total = jnp.where(lane == head, stacked[head * rows : (head + 1) * rows], total)
    return total


def columns_of(r, block, group, per_group):
    return pltpu.roll(r.run[block], lax.rem(LANES - per_group * group, LANES), 1)


def common_scratch(param_shapes, width, inner, state, n_blocks, tokens, n_tensor, depth):
    return dict(
        wbc=vmem((width, 2 * state), BF16),
        wdt=vmem((width, LANES), BF16),
        spread=vmem((2 * LANES, inner), BF16),
        select=vmem((n_tensor * LANES, 2 * state + LANES), BF16),
        live=vmem((tokens, LANES)),
        skip=vmem((8, inner)),
        dt=vmem((n_blocks, SCAN_BLOCK, LANES)),
        run=vmem((n_blocks, SCAN_BLOCK, LANES)),
        run_t=vmem((n_blocks, LANES, SCAN_BLOCK)),
        step_two=vmem((n_blocks, SCAN_BLOCK, 2 * LANES), BF16),
        grow_two=vmem((n_blocks, SCAN_BLOCK, 2 * LANES), BF16),
        keep_two=vmem((n_blocks, SCAN_BLOCK, 2 * LANES), BF16),
        decay=vmem((n_blocks, 8, inner)),
        pair=vmem((n_blocks, SCAN_BLOCK, SCAN_BLOCK)),
        states=vmem((n_blocks + 1, state, inner)),
        bc=vmem((tokens, 2 * state), BF16),
        xc=vmem((tokens, inner), BF16),
        dtp=vmem((tokens, LANES)),
        rms=vmem((tokens, LANES)),
        in_gain=vmem(param_shapes[0]),
        conv_x=vmem(param_shapes[1]),
        conv_bc=vmem(param_shapes[2]),
        dt_bias=vmem(param_shapes[3]),
        a_log=vmem(param_shapes[4]),
        d_skip=vmem(param_shapes[5]),
        gated_gain=vmem(param_shapes[6]),
        heads=vmem((param_shapes[3][0], 3, LANES)),
        load_sem=DMA((40,)),
        store_sem=DMA((24,)),
    )


def small_rows(width, inner, state):
    sizes = dict(
        heads=8,
        gain=-(-width // LANES // 8) * 8,
        gate_gain=inner // LANES,
        tap_x=(WIDTH + 1) * (inner // LANES),
        tap_b=(WIDTH + 1) * (2 * state // LANES),
    )
    starts, total = {}, 0
    for name, size in sizes.items():
        starts[name] = total
        total += size
    return SimpleNamespace(all=-(-total // 64) * 64, **starts)


def param_loads(r):
    copies = [
        pltpu.make_async_copy(getattr(r, "p_" + name), getattr(r, name), r.load_sem.at[16 + index])
        for index, name in enumerate(PARAMS)
    ]
    for copy in copies:
        copy.start()
    return copies


def param_inputs(params):
    ins = {"p_" + name: (params[name], ANY) for name in PARAMS}
    return dict(lengths=(params["lengths"], SMEM), order=(params["order"], SMEM), **ins)


def param_shapes(params):
    return [params[name].shape for name in PARAMS]


def row_blocks(whole, target, sems):
    depth, two, rows, _ = whole.shape
    return [
        pltpu.make_async_copy(
            whole.at[index // two, index % two],
            target.at[pl.ds(index * rows, rows), :],
            sems.at[index],
        )
        for index in range(depth * two)
    ]


PARAMS = ("in_gain", "conv_x", "conv_bc", "dt_bias", "a_log", "d_skip", "gated_gain")
TERMS = ("dt", "run", "run_t", "step_two", "grow_two", "keep_two", "decay")
CONSTANTS = ("spread", "collect", "select")
SAVED = ("nx", "gate", "xraw", "braw", "xc", "bc", "dtp", "mixed", "states", "rms")


class Weights:
    def __init__(self, queues, sources):
        self.queues = queues
        self.sources = sources
        self.started = {name: 0 for name in sources}
        self.used = {name: 0 for name in sources}

    def load(self, name, rounds_ago):
        layer = self.started[name]
        if layer == len(self.sources[name]) or self.used[name] != layer:
            return
        queue, units, copies = self.sources[name][layer]
        if all(queue.ready(unit, rounds_ago) for unit in units):
            for unit in units:
                queue.finish(unit)
            for copy in copies:
                copy.start()
            self.started[name] += 1

    def tick(self):
        for queue in self.queues:
            queue.tick()
        for name in self.sources:
            self.load(name, 1)

    def wait(self, name, layer):
        queue, units, copies = self.sources[name][layer]
        while not all(queue.ready(unit) for unit in units):
            self.tick()
        self.load(name, 0)
        for copy in copies:
            copy.wait()

    def done(self, name):
        self.used[name] += 1
        self.load(name, 1)


def deal_start(at, r):
    runner = at.dp // at.parts
    at_home = runner == at.tensor
    piece = r.arranged.shape[1]

    def spot(k, other):
        start = (k * at.n_tensor + other) * piece
        return r.dealt.at[pl.ds(pl.multiple_of(start, PAD), piece), :]

    slot = lax.rem(at.dp, at.parts)
    keep = pltpu.make_async_copy(r.arranged.at[at.dp], spot(slot, at.tensor), r.deal_own)
    deal = [
        remote(
            r.arranged.at[j],
            spot(slot, at.tensor),
            r.deal_send.at[j],
            r.deal_recv.at[slot, at.tensor],
            {DP: j, TENSOR: runner},
        )
        for j in range(at.n_dp)
    ]
    for j in range(at.n_dp):
        pl.when((j != at.dp) | (runner != at.tensor))(deal[j].start)
    pl.when(at_home)(keep.start)

    def arrive():
        for k in range(at.parts):
            for other in range(at.n_tensor):
                arrival = remote(
                    r.arranged.at[0],
                    spot(k, other),
                    r.deal_send.at[0],
                    r.deal_recv.at[k, other],
                    {TENSOR: lax.rem(at.tensor + 1, at.n_tensor)},
                )
                pl.when((at.tensor * at.parts + k != at.dp) | (other != at.tensor))(
                    arrival.wait_recv
                )
        pl.when(at_home)(keep.wait)

    def rest():
        for j in range(at.n_dp):
            pl.when((j != at.dp) | (runner != at.tensor))(deal[j].wait_send)

    return arrive, rest


def forward_body(cfg, r):
    at = place()
    direct = cfg.direct
    width = r.dealt.shape[1]
    small_loads = param_loads(r)
    count = 0
    if direct:
        greet_all(grid_partners(at))
        for source, other in deal_sources(at):

            @pl.when((source != at.dp) | (other != at.tensor))
            def _():
                greet({DP: source, TENSOR: other})

        at_home = (at.dp // at.parts == at.tensor).astype(jnp.int32)
        count = len(grid_partners(at)) + at.n_dp - at_home
    greet_all(tensor_partners(at))
    count = count + len(tensor_partners(at))

    first_queue, queue = Rounds(), Rounds()
    names = ("wn", "wx", "wz", "wo")
    sources = {name: [] for name in names}
    total = 0
    for layer in range(cfg.layers):
        for name in names:
            target = getattr(r, name)
            index = len(sources[name]) * len(names) + names.index(name)
            if direct:
                block, whole = getattr(r, "block_" + name), getattr(r, f"whole_{name}{layer}")
                full = block.shape[2]
                owner = first_queue if layer == 0 and name in names[:2] else queue
                units = []
                for start in range(0, full, LANES):
                    units.append(len(owner.units))
                    owner.add(gather_unit(at, r, total, block.at[layer], whole, start, full))
                    total += 1
                copies = row_blocks(whole, target, r.weight_sem.at[index])
                sources[name].append((owner, units, copies))
            else:
                whole = getattr(r, f"{name}{layer}_in")
                copy = pltpu.make_async_copy(whole, target, r.weight_sem.at[index, 0])
                sources[name].append((queue, [], [copy]))
    weights = Weights((queue,), sources)

    if direct:
        for j in range(at.n_dp):
            r.arranged[j] = r.hidden_in[r.order[j]]
    else:
        first = pltpu.make_async_copy(r.hidden_in, r.dealt, r.deal_own)
        first.start()
    met(count)
    if direct:
        first_queue.start()
        arrive, rest = deal_start(at, r)
        first_queue.tick()
        queue.start()
    fill_constants(r, at, cfg.head_size, cfg.state, cfg.heads)
    fill_live(r, at)
    for copy in small_loads:
        copy.wait()
    fill_heads(r)
    constants = []
    for index, name in enumerate(CONSTANTS):
        copy = pltpu.make_async_copy(getattr(r, name), getattr(r, name + "_out"), r.store_sem.at[20 + index])
        copy.start()
        constants.append(copy)
    if direct:
        first_queue.drain()
        for name in names[:2]:
            weights.load(name, 0)
        weights.tick()
        weights.tick()
        arrive()
        first = pltpu.make_async_copy(r.dealt, r.hidden, r.hidden_sem)
        first.start()
    else:
        first.wait()
    stores = {}
    turned = turn_copies(at, r, False) if direct else []
    for layer in range(cfg.layers):
        forward_layer(cfg, at, r, layer, weights, stores, turned)
    queue.drain()
    for copy in turned:
        copy.wait()
    if direct:
        rest()
        first.wait()
    for store in list(stores.values()) + constants:
        store.wait()


def forward_layer(cfg, at, r, layer, weights, stores, turned):
    me, last = at.tensor, at.n_tensor - 1
    h = r.dealt if layer == 0 else getattr(r, f"h{layer}")
    h_next = getattr(r, f"h{layer + 1}")
    halo = getattr(r, f"halo{layer}")
    tokens, width = h.shape
    inner, state, head_size = cfg.inner, cfg.state, cfg.head_size
    n_blocks = tokens // SCAN_BLOCK
    groups = inner // GROUP
    per_group = GROUP // head_size
    following = {TENSOR: lax.rem(me + 1, at.n_tensor)}

    def clear(*names):
        for name in names:
            if name in stores:
                stores.pop(name).wait()

    def store(name):
        index = (SAVED + TERMS).index(name)
        copy = pltpu.make_async_copy(
            getattr(r, name), getattr(r, f"{name}{layer}_out"), r.store_sem.at[index]
        )
        copy.start()
        stores[name] = copy

    halo_copy = remote(
        h.at[pl.ds(tokens - PAD, PAD), :], halo, r.halo_send.at[layer], r.halo_recv.at[layer], following
    )

    @pl.when(me < last)
    def _():
        halo_copy.start()

    spread_skip(r, layer)
    gain = r.in_gain[layer : layer + 1, :]

    def normalize(values):
        values = values.astype(F32)
        inv = lax.rsqrt(jnp.mean(values * values, axis=-1, keepdims=True) + EPS)
        return (values * inv * gain).astype(BF16)

    clear("nx", "dtp", *TERMS)

    @pl.loop(0, tokens // ROWS)
    def _(step):
        r.nx[rows_of(step, ROWS, PAD), :] = normalize(h[rows_of(step, ROWS), :])

    weights.wait("wn", layer)
    split_narrow(r, r.wn)
    weights.done("wn")
    r.dtp[...] = mm(r.nx[pl.ds(PAD, tokens), :], r.wdt[...]) + r.heads[layer, 0:1, :]
    for block in range(n_blocks):
        step_terms(r, layer, block)

    @pl.when(me > 0)
    def _():
        halo_copy.wait_recv()
        r.nx[0:PAD, :] = normalize(halo[...])

    @pl.when(me == 0)
    def _():
        r.nx[0:PAD, :] = jnp.zeros((PAD, width), BF16)

    store("nx")
    store("dtp")
    for name in TERMS:
        store(name)

    def convolve(projection, taps, raw, out, columns):
        raw[:, columns] = mm(r.nx[...], projection[:, columns])
        for start in range(0, tokens, ROWS):
            before = conv_rows(raw, taps, start, columns)
            out[pl.ds(start, ROWS), columns] = (before * jax.nn.sigmoid(before)).astype(BF16)

    clear("braw", "bc")
    for step in range(2 * state // GROUP):
        convolve(r.wbc, taps_of(r.conv_bc, layer), r.braw, r.bc, pl.ds(step * GROUP, GROUP))
    store("braw")
    store("bc")
    for block in range(n_blocks):
        rows = pl.ds(block * SCAN_BLOCK, SCAN_BLOCK)
        r.b_t[block] = r.bc[rows, :state].astype(F32).T.astype(BF16)
        row_id = lax.broadcasted_iota(jnp.int32, (SCAN_BLOCK, SCAN_BLOCK), 0)
        col_id = lax.broadcasted_iota(jnp.int32, (SCAN_BLOCK, SCAN_BLOCK), 1)
        scores = mm(r.bc[rows, state:], r.bc[rows, :state], NT)
        r.pair[block] = jnp.where(row_id >= col_id, scores, 0.0)

    if layer:
        weights.tick()
    weights.wait("wx", layer)
    clear("xraw", "xc", "states")
    @pl.loop(0, groups)
    def _(group):
        columns = lanes_of(group, GROUP)
        convolve(r.wx, taps_of(r.conv_x, layer), r.xraw, r.xc, columns)
        for block in range(n_blocks):
            rows = pl.ds(block * SCAN_BLOCK, SCAN_BLOCK)
            sizes = mm(r.step_two[block], r.spread[:, columns])
            keeps = mm(r.keep_two[block], r.spread[:, columns])
            weighted = (r.xc[rows, columns].astype(F32) * sizes * keeps).astype(BF16)
            r.states[block + 1, :, columns] = mm(r.b_t[block], weighted)
        pl.when(group == groups // 2 - 1)(weights.tick)

    weights.done("wx")
    store("xraw")
    store("xc")

    carry_copies = [
        remote(
            r.carry_out.at[layer, group],
            r.carry_in.at[layer, group],
            r.carry_send.at[layer, group],
            r.carry_recv.at[layer, group],
            following,
        )
        for group in range(groups)
    ]

    def chain():
        for group in range(groups):
            columns = pl.ds(group * GROUP, GROUP)

            @pl.when(me > 0)
            def _():
                carry_copies[group].wait_recv()
                r.states[0, :, columns] = r.carry_in[layer, group].astype(F32)

            @pl.when(me == 0)
            def _():
                r.states[0, :, columns] = jnp.zeros((state, GROUP), F32)

            for block in range(n_blocks):
                r.states[block + 1, :, columns] += (
                    r.states[block, :, columns] * r.decay[block, 0:1, columns]
                )
            r.carry_out[layer, group] = r.states[n_blocks, :, columns].astype(BF16)

            @pl.when(me < last)
            def _():
                carry_copies[group].start()

    pl.when(me == 0)(chain)
    clear("mixed")
    @pl.loop(0, n_blocks)
    def _(block):
        pl.when(block == 1)(weights.tick)
        rows = lanes_of(block, SCAN_BLOCK)

        @pl.loop(0, groups)
        def _(group):
            columns = lanes_of(group, GROUP)
            sizes = mm(r.step_two[block], r.spread[:, columns])
            x_here = r.xc[rows, columns].astype(F32)
            stepped = (x_here * sizes).astype(BF16)
            rolled = columns_of(r, block, group, per_group)
            upper, lower = [], []
            for head in range(per_group):
                along = r.run_t[block, pl.ds(per_group * group + head, 1), :]
                down = rolled[:, head : head + 1]
                factor = jnp.exp2(jnp.minimum(down[:HALF] - along[:, :HALF], 0.0))
                upper.append((r.pair[block, :HALF, :HALF] * factor).astype(BF16))
                factor = jnp.exp2(jnp.minimum(down[HALF:] - along, 0.0))
                lower.append((r.pair[block, HALF:, :] * factor).astype(BF16))
            upper = own_lanes(mm(jnp.concatenate(upper, axis=0), stepped[:HALF]), per_group, head_size)
            lower = own_lanes(mm(jnp.concatenate(lower, axis=0), stepped), per_group, head_size)
            r.mixed[rows, columns] = (
                jnp.concatenate([upper, lower], axis=0) + r.skip[0:1, columns] * x_here
            )

        pl.when(me == block + 1)(chain)

    if layer + 1 == cfg.layers:
        for copy in turned:
            copy.start()
    weights.wait("wz", layer)
    clear("gate")

    @pl.loop(0, groups)
    def _(group):
        columns = lanes_of(group, GROUP)
        r.gate[:, columns] = mm(r.nx[pl.ds(PAD, tokens), :], r.wz[:, columns])

    weights.done("wz")
    store("gate")
    pl.when(me > n_blocks)(chain)
    store("states")
    r.squares[...] = jnp.zeros_like(r.squares)
    @pl.loop(0, n_blocks)
    def _(block):
        rows = lanes_of(block, SCAN_BLOCK)

        @pl.loop(0, groups)
        def _(group):
            columns = lanes_of(group, GROUP)
            grown = mm(r.grow_two[block], r.spread[:, columns])
            total = r.mixed[rows, columns] + grown * mm(
                r.bc[rows, state:], r.states[block, :, columns].astype(BF16)
            )
            r.mixed[rows, columns] = total
            gate_in = r.gate[rows, columns]
            gated = total * gate_in * jax.nn.sigmoid(gate_in)
            r.gm[rows, columns] = gated
            squared = gated * gated
            for lane in range(0, GROUP, LANES):
                r.squares[rows, :] += squared[:, lane : lane + LANES]

        pl.when(block == 0)(weights.tick)

    store("mixed")
    clear("rms")
    r.rms[...] = jnp.broadcast_to(
        lax.rsqrt(jnp.sum(r.squares[...], axis=-1, keepdims=True) / inner + EPS), r.rms.shape
    )
    store("rms")

    @pl.loop(0, groups)
    def _(group):
        columns = lanes_of(group, GROUP)
        for start in range(0, tokens, ROWS):
            rows = pl.ds(start, ROWS)
            r.go[rows, columns] = (
                r.gm[rows, columns] * r.rms[rows, 0:1] * r.gated_gain[layer : layer + 1, columns]
            ).astype(BF16)

    weights.wait("wo", layer)

    @pl.loop(0, width // GROUP)
    def _(step):
        columns = lanes_of(step, GROUP)
        branch = mm(r.go[...], r.wo[columns, :], NT)
        value = (h[:, columns].astype(F32) + branch) * r.live[:, 0:1]
        h_next[:, columns] = value
        if layer + 1 == cfg.layers:
            r.h_low[:, columns] = value.astype(BF16)

    weights.done("wo")
    if layer == 0:
        weights.tick()

    @pl.when(me < last)
    def _():
        halo_copy.wait_send()
        for copy in carry_copies:
            copy.wait_send()


def layers_forward(cfg, at, hidden_in, params, weights, blocks, turn):
    layers, inner, state = cfg.layers, cfg.inner, cfg.state
    width = hidden_in.shape[-1]
    tokens = cfg.tokens
    n_blocks = tokens // SCAN_BLOCK
    depth = at.n_dp // 2
    ins = dict(hidden_in=(hidden_in, VMEM if cfg.direct else ANY), **param_inputs(params))
    saved = dict(
        nx=vmem((PAD + tokens, width), BF16),
        gate=vmem((tokens, inner)),
        xraw=vmem((PAD + tokens, inner)),
        braw=vmem((PAD + tokens, 2 * state)),
        xc=vmem((tokens, inner), BF16),
        bc=vmem((tokens, 2 * state), BF16),
        dtp=vmem((tokens, LANES)),
        mixed=vmem((tokens, inner)),
        states=vmem((n_blocks + 1, state, inner)),
        rms=vmem((tokens, LANES)),
    )
    outs = dict(h_low=(shaped((tokens, width), BF16), VMEM))
    scratch = common_scratch(
        param_shapes(params), width, inner, state, n_blocks, tokens, at.n_tensor, depth
    )
    carry = (layers, inner // GROUP, state, GROUP)
    scratch.update(saved)
    scratch.update(
        dealt=vmem((tokens, width), BF16),
        deal_own=DMA,
        wz=vmem((width, inner), BF16),
        wx=vmem((width, inner), BF16),
        wo=vmem((width, inner), BF16),
        wn=vmem((width, at.n_tensor * LANES), BF16),
        weight_sem=DMA((4 * layers, at.n_dp)),
        halo_send=DMA((layers,)),
        halo_recv=DMA((layers,)),
        carry_out=vmem(carry, BF16),
        carry_in=vmem(carry, BF16),
        carry_send=DMA(carry[:2]),
        carry_recv=DMA(carry[:2]),
        b_t=vmem((n_blocks, state, SCAN_BLOCK), BF16),
        gm=vmem((tokens, inner)),
        go=vmem((tokens, inner), BF16),
        squares=vmem((tokens, LANES)),
    )
    for layer in range(layers):
        scratch[f"halo{layer}"] = vmem((PAD, width), F32 if layer else BF16)
        outs[f"h{layer + 1}"] = (shaped((tokens, width)), VMEM)
        for name in SAVED + TERMS:
            kind = scratch[name]
            outs[f"{name}{layer}_out"] = (shaped(kind.shape, kind.dtype), ANY)
    scratch["collect"] = vmem((inner, LANES), BF16)
    for name in CONSTANTS:
        outs[name + "_out"] = (shaped(scratch[name].shape, BF16), ANY)
    if cfg.direct:
        total = 0
        piece = tokens // at.n_dp
        for name, block in blocks.items():
            ins["block_" + name] = (block, VMEM)
            total += layers * (block.shape[2] // LANES)
            whole = (depth, 2, block.shape[1], at.n_tensor * block.shape[2])
            for layer in range(layers):
                outs[f"whole_{name}{layer}"] = (shaped(whole, BF16), ANY)
        ins["turn_in"] = (turn, VMEM)
        outs["turned"] = (shaped(turn.shape, BF16), ANY)
        outs["hidden"] = (shaped((tokens, width), BF16), ANY)
        scratch.update(turn_sems(at))
        scratch.update(gather_sems(total, depth))
        scratch.update(
            arranged=vmem((at.n_dp, piece, width), BF16),
            deal_send=DMA((at.n_dp,)),
            deal_recv=DMA((at.parts, at.n_tensor)),
            hidden_sem=DMA,
        )
    else:
        for layer in range(layers):
            for name in blocks:
                ins[f"{name}{layer}_in"] = (weights[layer][name], ANY)
    return call_kernel(partial(forward_body, cfg), "layers_forward", 1, ins, outs, scratch)


def turn_sems(at):
    shape = (at.n_tensor - 1, at.parts)
    return dict(turn_send=DMA(shape), turn_recv=DMA(shape), turn_own=DMA((at.parts,)))


def turn_copies(at, r, to_pieces):
    copies = []
    for offset in range(at.n_tensor):
        other = lax.rem(at.tensor + offset, at.n_tensor)
        for k in range(at.parts):
            if to_pieces:
                mine = r.turn_in.at[k * at.n_tensor + other]
                theirs = r.turned.at[at.tensor * at.parts + k]
            else:
                mine = r.turn_in.at[other * at.parts + k]
                theirs = r.turned.at[k * at.n_tensor + at.tensor]
            if offset == 0:
                copies.append(pltpu.make_async_copy(mine, theirs, r.turn_own.at[k]))
            else:
                copies.append(
                    remote(
                        mine,
                        theirs,
                        r.turn_send.at[offset - 1, k],
                        r.turn_recv.at[offset - 1, k],
                        {TENSOR: other},
                    )
                )
    return copies


def backward_body(cfg, r):
    at = place()
    me, last = at.tensor, at.n_tensor - 1
    layer, direct = cfg.layer, cfg.direct
    tokens, width = r.h.shape
    inner, state, head_size = cfg.inner, cfg.state, cfg.head_size
    n_blocks = tokens // SCAN_BLOCK
    groups = inner // GROUP
    per_group = GROUP // head_size
    previous = {TENSOR: lax.rem(me + last, at.n_tensor)}

    def load(name, target, index):
        copy = pltpu.make_async_copy(getattr(r, name + "_in"), target, r.load_sem.at[index])
        copy.start()
        return copy

    next_load = load("h_next", r.gn, 10)
    loads = {
        name: load(name, getattr(r, name), index) for index, name in enumerate(("nx", "rms", "dtp", "bc"))
    }
    for index, name in enumerate(CONSTANTS + TERMS):
        loads[name] = load(name, getattr(r, name), 24 + index)
    small_loads = param_loads(r)

    def stream(group, slot):
        columns = lanes_of(group, GROUP)
        return [
            pltpu.make_async_copy(r.gate_in.at[:, columns], r.gate.at[slot], r.stream_sem.at[0, slot]),
            pltpu.make_async_copy(r.mixed_in.at[:, columns], r.mixed.at[slot], r.stream_sem.at[1, slot]),
        ]

    count = 0
    if direct:
        greet_all(grid_partners(at))
        count = len(grid_partners(at))
        if cfg.closing:
            greet_all(corner_partners(at))
            count = count + len(corner_partners(at))
    greet_all(tensor_partners(at))
    count = count + len(tensor_partners(at))

    earlier, own = Rounds(), Rounds()
    unit_indices = []

    def enqueue(queue, source, full, put):
        for start in range(0, full, LANES):
            index = len(unit_indices)
            unit_indices.append(index)
            queue.add(reduce_unit(at, r, index, source, start, full, partial(put, start)))

    side = []

    def tick():
        earlier.tick()
        own.tick()
        if side:
            side.pop(0)()

    def put_wide(target):
        def put(start, value):
            target[:, start : start + LANES] = value

        return put

    def put_narrow(target):
        def put(start, value):
            target[...] = value

        return put

    turned = []
    if direct:
        if cfg.more:
            enqueue(earlier, r.g_wx, r.sum_wx.shape[1], put_wide(r.sum_wx))
            enqueue(earlier, r.g_narrow, LANES, put_narrow(r.sum_narrow))
            prior_loads = [load("prior_wx", r.g_wx, 11), load("prior_narrow", r.g_narrow, 12)]
        if cfg.turn:
            turned = turn_copies(at, r, True)

    fill_live(r, at)
    for copy in small_loads:
        copy.wait()
    fill_heads(r)
    for name in CONSTANTS:
        loads[name].wait()
    spread_skip(r, layer)
    loads["nx"].wait()
    loads["rms"].wait()
    next_load.wait()

    @pl.loop(0, tokens // ROWS)
    def _(step):
        rows = rows_of(step, ROWS)
        alive = r.live[rows, 0:1]
        low = (r.gh[rows, :].astype(F32) * alive).astype(BF16)
        r.g_branch[rows, :] = low
        columns = lanes_of(step, ROWS)
        r.g_branch_t[:, columns] = low.T
        r.normed_t[:, columns] = r.nx[rows_of(step, ROWS, PAD), :].T
        branch = r.gn[rows, :] - r.h[rows, :].astype(F32)
        scale = r.rms[rows, 0:1]
        along = jnp.sum(low.astype(F32) * branch, axis=-1, keepdims=True) * (scale * scale / inner)
        r.along[rows, :] = jnp.broadcast_to(along, (ROWS, LANES))

    loads.update(
        {
            name: load(name, getattr(r, name), 4 + index)
            for index, name in enumerate(("wo", "xc", "states", "braw", "wz"))
        }
    )
    for copy in stream(0, 0):
        copy.start()
    met(count)
    if direct and cfg.more:
        for copy in prior_loads:
            copy.wait()
        earlier.start()
    if cfg.closing:
        for other in range(layer + 1, cfg.layers):
            r.packed[other] = getattr(r, f"small{other}")[...]
            side.extend(small_steps(at, r, other))
    for copy in turned:
        copy.start()
    loads["dtp"].wait()
    for name in TERMS:
        loads[name].wait()
    tick()

    loads["bc"].wait()
    row_id = lax.broadcasted_iota(jnp.int32, (SCAN_BLOCK, SCAN_BLOCK), 0)
    col_id = lax.broadcasted_iota(jnp.int32, (SCAN_BLOCK, SCAN_BLOCK), 1)
    for block in range(n_blocks):
        rows = pl.ds(block * SCAN_BLOCK, SCAN_BLOCK)
        scores = mm(r.bc[rows, :state], r.bc[rows, state:], NT)
        r.pair[block] = jnp.where(row_id <= col_id, scores, 0.0)
        r.c_t[block] = r.bc[rows, state:].astype(F32).T.astype(BF16)
    r.g_run[...] = jnp.zeros_like(r.g_run)
    r.g_heads[...] = jnp.zeros_like(r.g_heads)
    places = small_rows(width, inner, state)

    def put_small(name, row, tile, values):
        for lane in range(0, values.shape[1], LANES):
            r.g_small[pl.ds(name + row + tile + lane // LANES, 1), :] = values[
                :, lane : lane + LANES
            ]

    def put_rows(target, columns, values):
        values = values.astype(BF16)
        if direct:
            target[:, :, :, columns] = values.reshape(target.shape[:3] + values.shape[1:])
        else:
            target[:, columns] = values

    def collected(values, columns):
        rows = values.shape[0]
        both = mm(jnp.concatenate(halves(values), axis=0), r.collect[columns, :])
        return both[:rows] + both[rows:]

    loads["wo"].wait()
    loads["xc"].wait()

    def gate_group(group):
        slot = lax.rem(group, 2)
        columns = lanes_of(group, GROUP)
        for copy in stream(group, slot):
            copy.wait()

        @pl.when(group + 1 < groups)
        def _():
            for copy in stream(group + 1, 1 - slot):
                copy.start()

        gain = r.gated_gain[layer : layer + 1, columns]
        skipped = r.skip[0:1, columns]
        gained = jnp.zeros((1, GROUP), F32)
        skip_sum = jnp.zeros((1, GROUP), F32)
        r.gq[pl.ds(0, tokens), columns] = mm(r.g_branch[...], r.wo[:, columns])
        for start in range(0, tokens, ROWS):
            rows = pl.ds(start, ROWS)
            gate_in = r.gate[slot, rows, :]
            here = r.mixed[slot, rows, :]
            x_here = r.xc[rows, columns].astype(F32)
            scale = r.rms[rows, 0:1]
            sig = jax.nn.sigmoid(gate_in)
            act = gate_in * sig
            gated = here * act
            scaled = gated * scale
            r.go[rows, :] = (scaled * gain).astype(BF16)
            g_gated = r.gq[rows, columns]
            gained = gained + jnp.sum(g_gated * scaled, axis=0, keepdims=True)
            g_mix = scale * gain * g_gated - gated * r.along[rows, 0:1]
            g_out = g_mix * act
            r.gq[rows, columns] = g_out
            r.pz[rows, columns] = (g_mix * here * sig * (1.0 + gate_in * (1.0 - sig))).astype(BF16)
            skip_sum = skip_sum + jnp.sum(g_out * x_here, axis=0, keepdims=True)
            r.g_run[rows, :] += collected(g_out * (here - skipped * x_here), columns)
        pl.when(group == groups // 2 - 1)(tick)
        put_small(places.gate_gain, 0, group * (GROUP // LANES), gained)
        r.g_heads[2:3, :] += collected(jnp.broadcast_to(skip_sum, (8, GROUP)), columns)[0:1, :]
        put_rows(r.g_wo, columns, mm(r.g_branch_t[...], r.go[...]))
        put_rows(r.g_wz, columns, mm(r.normed_t[...], r.pz[:, columns]))
        for block in range(n_blocks):
            rows = pl.ds(block * SCAN_BLOCK, SCAN_BLOCK)
            grown = mm(r.grow_two[block], r.spread[:, columns])
            r.d_states[block, :, columns] = mm(
                r.c_t[block], (r.gq[rows, columns] * grown).astype(BF16)
            )

    pl.loop(0, groups)(gate_group)
    tick()
    wx_load = load("wx", r.wo, 13)

    if direct:
        for source, target in ((r.g_wo, r.sum_wo), (r.g_wz, r.sum_wz)):
            enqueue(own, source, target.shape[1], put_wide(target))
        own.start()

    carry_copies = [
        remote(
            r.carry_out.at[group],
            r.carry_in.at[group],
            r.carry_send.at[group],
            r.carry_recv.at[group],
            previous,
        )
        for group in range(groups)
    ]

    def chain():
        for group in range(groups):
            columns = pl.ds(group * GROUP, GROUP)

            @pl.when(me < last)
            def _():
                carry_copies[group].wait_recv()
                r.d_states[n_blocks, :, columns] = r.carry_in[group].astype(F32)

            @pl.when(me == last)
            def _():
                r.d_states[n_blocks, :, columns] = jnp.zeros((state, GROUP), F32)

            for block in reversed(range(n_blocks)):
                r.d_states[block, :, columns] += (
                    r.d_states[block + 1, :, columns] * r.decay[block, 0:1, columns]
                )
            r.carry_out[group] = r.d_states[0, :, columns].astype(BF16)

            @pl.when(me > 0)
            def _():
                carry_copies[group].start()

    pl.when(me == last)(chain)
    loads["states"].wait()
    r.gb[pl.ds(0, tokens), state:] = jnp.zeros((tokens, state), F32)
    for block in range(n_blocks):
        if block:
            tick()
        rows = pl.ds(block * SCAN_BLOCK, SCAN_BLOCK)
        r.g_pair[...] = jnp.zeros_like(r.g_pair)

        @pl.loop(0, groups)
        def _(group):
            columns = lanes_of(group, GROUP)
            sizes = mm(r.step_two[block], r.spread[:, columns])
            grown = mm(r.grow_two[block], r.spread[:, columns])
            stepped = (r.xc[rows, columns].astype(F32) * sizes).astype(BF16)
            g_out = r.gq[rows, columns]
            g_low = g_out.astype(BF16)
            rolled = columns_of(r, block, group, per_group)
            r.gb[rows, state:] += mm(
                (g_out * grown).astype(BF16), r.states[block, :, columns].astype(BF16), NT
            )
            upper, lower, up_factors, low_factors = [], [], [], []
            for head in range(per_group):
                along = r.run_t[block, pl.ds(per_group * group + head, 1), :]
                down = rolled[:, head : head + 1]
                up_factors.append(jnp.exp2(jnp.minimum(along - down[:HALF], 0.0)))
                upper.append((r.pair[block, :HALF, :] * up_factors[head]).astype(BF16))
                low_factors.append(jnp.exp2(jnp.minimum(along[:, HALF:] - down[HALF:], 0.0)))
                lower.append((r.pair[block, HALF:, HALF:] * low_factors[head]).astype(BF16))
            upper = own_lanes(mm(jnp.concatenate(upper, axis=0), g_low), per_group, head_size)
            lower = own_lanes(mm(jnp.concatenate(lower, axis=0), g_low[HALF:]), per_group, head_size)
            ones = [stepped * head_row(head, head_size) for head in range(per_group)]
            up_pairs = mm(jnp.concatenate([one[:HALF] for one in ones], axis=0), g_low, NT)
            low_pairs = mm(jnp.concatenate([one[HALF:] for one in ones], axis=0), g_low[HALF:], NT)
            pair_upper = up_pairs[:HALF] * up_factors[0]
            pair_lower = low_pairs[:HALF] * low_factors[0]
            for head in range(1, per_group):
                span = slice(head * HALF, (head + 1) * HALF)
                pair_upper = pair_upper + up_pairs[span] * up_factors[head]
                pair_lower = pair_lower + low_pairs[span] * low_factors[head]
            r.gx[rows, columns] = jnp.concatenate([upper, lower], axis=0)
            r.g_pair[:HALF, :] += pair_upper
            r.g_pair[HALF:, HALF:] += pair_lower

        g_scores = jnp.where(row_id <= col_id, r.g_pair[...], 0.0)
        r.gb[rows, :state] = mm(g_scores.astype(BF16), r.bc[rows, state:])
        r.gb[rows, state:] += mm(g_scores.T.astype(BF16), r.bc[rows, :state])
        if block < n_blocks - 1:
            pl.when(me == last - 1)(chain)

    pl.when(me < (last - 1 if n_blocks > 1 else last))(chain)
    r.direct[...] = jnp.zeros_like(r.direct)
    for block in reversed(range(n_blocks)):
        if block == n_blocks - 1:
            tick()
        rows = pl.ds(block * SCAN_BLOCK, SCAN_BLOCK)

        @pl.loop(0, groups)
        def _(group):
            columns = lanes_of(group, GROUP)
            sizes = mm(r.step_two[block], r.spread[:, columns])
            keeps = mm(r.keep_two[block], r.spread[:, columns])
            x_here = r.xc[rows, columns].astype(F32)
            stepped = x_here * sizes
            d_here = r.d_states[block + 1, :, columns].astype(BF16)
            d_x = r.gx[rows, columns] + keeps * mm(r.bc[rows, :state], d_here)
            r.gb[rows, :state] += mm((stepped * keeps).astype(BF16), d_here, NT)
            sums = collected(
                jnp.concatenate([d_x * x_here, d_x * stepped.astype(BF16).astype(F32)], axis=0), columns
            )
            r.direct[rows, :] += sums[:SCAN_BLOCK]
            r.g_run[rows, :] -= sums[SCAN_BLOCK:]
            r.gx[rows, columns] = sizes * d_x + r.skip[0:1, columns] * r.gq[rows, columns]

    raw_load = load("xraw", r.gq, 14)
    for block in range(n_blocks):
        rows = pl.ds(block * SCAN_BLOCK, SCAN_BLOCK)
        end_sum = jnp.broadcast_to(
            jnp.sum(r.d_states[block + 1] * r.states[block + 1], axis=0, keepdims=True), (8, inner)
        )
        at_end = collected(end_sum, slice(None))[0:1, :]
        rate = r.heads[layer, 1:2, :]
        g_rate = exact((row_id <= col_id).astype(F32), r.g_run[rows, :]) + at_end
        g_dt = (rate * g_rate + r.direct[rows, :]) * r.live[rows, :] * jax.nn.sigmoid(r.dtp[rows, :])
        r.pd[rows, :] = g_dt.astype(BF16)
        r.g_heads[0:1, :] += jnp.sum(g_dt, axis=0, keepdims=True)
        r.g_heads[1:2, :] += jnp.sum(g_rate * r.dt[block], axis=0, keepdims=True) * rate
    tick()

    def before_conv(taps, raw, grad, columns):
        for start in range(0, tokens, ROWS):
            rows = pl.ds(start, ROWS)
            before = conv_rows(raw, taps, start, columns)
            sig = jax.nn.sigmoid(before)
            grad[rows, columns] = grad[rows, columns] * (sig * (1.0 + before * (1.0 - sig)))

    def through_conv(taps, raw, grad, columns, name, tile, low):
        sums = [jnp.zeros((1, GROUP), F32) for tap in range(WIDTH + 1)]
        for start in range(0, tokens, ROWS):
            total = jnp.zeros((ROWS, GROUP), F32)
            here = grad[pl.ds(start, ROWS), columns]
            for tap in range(WIDTH):
                shift = WIDTH - 1 - tap
                total = total + taps(tap, columns) * grad[pl.ds(start + shift, ROWS), columns]
                sums[tap] = sums[tap] + jnp.sum(
                    here * raw[pl.ds(PAD - shift + start, ROWS), columns], axis=0, keepdims=True
                )
            sums[WIDTH] = sums[WIDTH] + jnp.sum(here, axis=0, keepdims=True)
            low[pl.ds(start, ROWS), columns] = total.astype(BF16)
        for tap in range(WIDTH + 1):
            put_small(name, tap * (grad.shape[1] // LANES), tile, sums[tap])

    earlier.drain()
    wn_load = load("wn", r.g_narrow, 15)
    loads["braw"].wait()
    for step in range(2 * state // GROUP):
        before_conv(taps_of(r.conv_bc, layer), r.braw, r.gb, pl.ds(step * GROUP, GROUP))
    raw_load.wait()

    @pl.loop(0, groups)
    def _(step):
        before_conv(taps_of(r.conv_x, layer), r.gq, r.gx, lanes_of(step, GROUP))

    halo_copies = [
        remote(
            buffer.at[pl.ds(0, PAD), :],
            buffer.at[pl.ds(tokens, PAD), :],
            r.halo_send.at[index],
            r.halo_recv.at[index],
            previous,
        )
        for index, buffer in enumerate((r.gx, r.gb))
    ]

    @pl.when(me > 0)
    def _():
        for copy in halo_copies:
            copy.start()

    wn_load.wait()
    split_narrow(r, r.g_narrow)
    put_rows(r.g_narrow, pl.ds(2 * state, LANES), mm(r.normed_t[...], r.pd[...]))
    put_rows(r.g_narrow, pl.ds(2 * state + LANES, LANES), jnp.zeros((width, LANES), F32))
    loads["wz"].wait()
    r.g_gain[...] = jnp.zeros_like(r.g_gain)

    @pl.loop(0, width // GROUP)
    def _(step):
        columns = lanes_of(step, GROUP)
        r.gn[:, columns] = mm(r.pz[...], r.wz[columns, :], NT) + mm(r.pd[...], r.wdt[columns, :], NT)

    tick()

    @pl.when(me < last)
    def _():
        for copy in halo_copies:
            copy.wait_recv()

    @pl.when(me == last)
    def _():
        for buffer in (r.gx, r.gb):
            buffer[pl.ds(tokens, PAD), :] = jnp.zeros((PAD, buffer.shape[1]), F32)

    for step in range(2 * state // GROUP):
        columns = pl.ds(step * GROUP, GROUP)
        through_conv(
            taps_of(r.conv_bc, layer), r.braw, r.gb, columns, places.tap_b, step * (GROUP // LANES), r.pb
        )
        put_rows(r.g_narrow, columns, mm(r.normed_t[...], r.pb[:, columns]))
    stores = []

    def store(source, target):
        copy = pltpu.make_async_copy(source, target, r.store_sem.at[len(stores)])
        copy.start()
        stores.append(copy)

    final = Rounds()
    if cfg.closing:
        enqueue(final, r.g_wx, r.close_wx.shape[1], put_wide(r.close_wx))
        enqueue(final, r.g_narrow, LANES, put_narrow(r.close_narrow))
    else:
        store(r.g_narrow, r.g_narrow_out)

    for first in range(0, groups, groups // 2):

        @pl.loop(first, first + groups // 2)
        def _(step):
            columns = lanes_of(step, GROUP)
            through_conv(
                taps_of(r.conv_x, layer), r.gq, r.gx, columns, places.tap_x, step * (GROUP // LANES), r.px
            )
            put_rows(r.g_wx, columns, mm(r.normed_t[...], r.px[:, columns]))

        tick()

    own.drain()
    while side:
        side.pop(0)()
    if cfg.closing:
        final.start()
    else:
        store(r.g_wx, r.g_wx_out)
    wx_load.wait()

    @pl.loop(0, width // GROUP)
    def _(step):
        columns = lanes_of(step, GROUP)
        r.gn[:, columns] += mm(r.px[...], r.wo[columns, :], NT) + mm(r.pb[...], r.wbc[columns, :], NT)

    final.tick()
    r.g_small[pl.ds(places.heads, 8), :] = r.g_heads[...]
    r.g_small[pl.ds(places.gain, 8), :] = jnp.zeros((8, LANES), F32)
    gain = r.in_gain[layer : layer + 1, :]

    @pl.loop(0, tokens // ROWS)
    def _(step):
        rows = rows_of(step, ROWS)
        values = r.h[rows, :].astype(F32)
        inv = lax.rsqrt(jnp.mean(values * values, axis=-1, keepdims=True) + EPS)
        g_normed = r.gn[rows, :]
        r.g_gain[0:1, :] += jnp.sum(g_normed * values * inv, axis=0, keepdims=True)
        scaled = g_normed * gain
        along_h = jnp.mean(scaled * values, axis=-1, keepdims=True)
        r.gh_next[rows, :] = (
            r.gh[rows, :].astype(F32) * r.live[rows, 0:1]
            + inv * scaled
            - values * (inv * inv * inv * along_h)
        ).astype(r.gh_next.dtype)

    put_small(places.gain, 0, 0, r.g_gain[0:1, :])
    if cfg.closing:
        close(cfg, at, r, final)
    for copy in turned:
        copy.wait()
    if not direct:
        store(r.g_wo, r.g_wo_out)
        store(r.g_wz, r.g_wz_out)
    for copy in stores:
        copy.wait()

    @pl.when(me > 0)
    def _():
        for copy in halo_copies + carry_copies:
            copy.wait_send()


def corner_partners(at):
    return [
        {DP: at.dp + 1 - 2 * at.y, TENSOR: lax.rem(at.tensor + k, at.n_tensor)}
        for k in range(1, at.n_tensor)
    ]


def small_steps(at, r, layer):
    depth = at.depth
    quarter = r.packed.shape[1] // depth
    send, recv = r.small_send, r.small_recv

    def part(index):
        return pl.ds(pl.multiple_of(index * quarter, 8), quarter)

    def hop(index, source, target, device):
        return remote(source, target, send.at[layer, index], recv.at[layer, index], device)

    hops = [
        hop(0, r.packed.at[layer], r.small_core.at[layer], over_core(at)),
        hop(1, r.sum_core.at[layer], r.small_x.at[layer], over_x(at)),
        hop(2, r.sum_x.at[layer], r.small_y.at[layer], over_y(at)),
    ]
    scatter = [
        hop(
            2 + k,
            r.sum_y.at[layer, part(lax.rem(at.z + k, depth))],
            r.small_z.at[layer, k - 1],
            over_z(at, k),
        )
        for k in range(1, depth)
    ]
    total = r.small_sum.at[layer, part(at.z)]
    gather = [hop(1 + depth + k, total, total, over_z(at, k)) for k in range(1, depth)]

    def begin():
        hops[0].start()

    def add(index, own, other, result):
        def step():
            hops[index].wait_recv()
            result[layer] = own[layer] + other[layer]
            for copy in [hops[index + 1]] if index < 2 else scatter:
                copy.start()

        return step

    def turn():
        value = r.sum_y[layer, part(at.z)]
        for k, copy in enumerate(scatter):
            copy.wait_recv()
            value = value + r.small_z[layer, k]
        r.small_sum[layer, part(at.z)] = value
        for copy in gather:
            copy.start()

    def end():
        for copy in gather:
            copy.wait_recv()
        for copy in hops + scatter + gather:
            copy.wait_send()

    return [
        begin,
        add(0, r.packed, r.small_core, r.sum_core),
        add(1, r.sum_core, r.small_x, r.sum_x),
        add(2, r.sum_x, r.small_y, r.sum_y),
        turn,
        end,
    ]


def close(cfg, at, r, final):
    piece = r.returned.shape[1]
    middle = r.input_grad
    r.packed[cfg.layer] = r.g_small[...]
    smalls = small_steps(at, r, cfg.layer)
    mine = 2 * at.tensor + at.y

    def run(k, other):
        return r.gh_next.at[pl.ds(pl.multiple_of((k * at.n_tensor + other) * piece, PAD), piece), :]

    stay = pltpu.make_async_copy(run(at.y, at.tensor), middle.at[mine], r.back_own.at[0])
    stay.start()
    out = []
    for k in range(2):
        for offset in range(at.n_tensor):
            other = lax.rem(at.tensor + offset, at.n_tensor)
            copy = remote(
                run(k, other),
                middle.at[mine],
                r.back_send.at[k, offset],
                r.back_recv.at[mine],
                {DP: at.z * 2 + k, TENSOR: other},
            )
            out.append((copy, at.y != k if offset == 0 else at.y >= 0))
    for copy, away in out:
        pl.when(away)(copy.start)
    smalls[0]()
    final.tick()
    smalls[1]()

    stay.wait()
    keep = pltpu.make_async_copy(
        middle.at[pl.ds(2 * at.z, 2)], r.returned.at[pl.ds(2 * at.z, 2)], r.back_own.at[1]
    )
    through = []
    for owner in range(at.n_tensor):
        for slot in (2 * owner, 2 * owner + 1):
            arrival = remote(
                run(0, 0), middle.at[slot], r.back_send.at[0, 0], r.back_recv.at[slot], over_core(at)
            )
            pl.when(mine != slot)(arrival.wait_recv)
        copy = remote(
            middle.at[pl.ds(2 * owner, 2)],
            r.returned.at[pl.ds(2 * at.z, 2)],
            r.through_send.at[owner],
            r.through_recv.at[at.z],
            {DP: owner * 2 + at.y},
        )
        through.append(copy)
        pl.when(at.z != owner)(copy.start)
    keep.start()
    final.tick()
    smalls[2]()
    final.tick()
    smalls[3]()
    final.finish(len(final.units) - 1)

    r.narrow[cfg.layer, at.tensor] = r.close_narrow[...]
    for layer in range(cfg.layer + 1, cfg.layers):
        source = r.sum_narrow if layer == cfg.layer + 1 else getattr(r, f"narrow{layer}")
        r.narrow[layer, at.tensor] = source[...]
    spread = [
        remote(
            r.narrow.at[:, at.tensor],
            r.narrow.at[:, at.tensor],
            r.narrow_send.at[k - 1],
            r.narrow_recv.at[k - 1],
            {TENSOR: lax.rem(at.tensor + k, at.n_tensor)},
        )
        for k in range(1, at.n_tensor)
    ]
    for copy in spread:
        copy.start()
    smalls[4]()
    final.drain()

    keep.wait()
    for owner in range(at.n_tensor):
        arrival = remote(
            middle.at[pl.ds(0, 2)],
            r.returned.at[pl.ds(2 * owner, 2)],
            r.through_send.at[owner],
            r.through_recv.at[owner],
            over_core(at),
        )
        pl.when(at.z != owner)(arrival.wait_recv)
        pl.when(at.z != owner)(through[owner].wait_send)
    for copy, away in out:
        pl.when(away)(copy.wait_send)
    for index in range(at.n_dp):
        source = jnp.int32(0)
        for j in range(1, at.n_dp):
            source = jnp.where(r.order[j] == index, j, source)
        r.input_grad[index] = r.returned[source]
    smalls[5]()
    for copy in spread:
        copy.wait()


def layer_backward(cfg, at, gh, h, h_next, params, saved, weights, prior, turn, others):
    tokens, width = h.shape
    inner, state = cfg.inner, cfg.state
    n_blocks = tokens // SCAN_BLOCK
    depth, rows = at.n_dp // 2, width // at.n_dp
    part = inner // at.n_tensor
    piece = tokens // at.n_dp
    narrow = at.n_tensor * LANES
    small_shape = (small_rows(width, inner, state).all, LANES)

    def blocked(columns):
        return (depth, 2, rows, columns) if cfg.direct else (width, columns)

    ins = dict(gh=(gh, VMEM), h=(h, VMEM), h_next_in=(h_next, ANY), **param_inputs(params))
    for name in SAVED + TERMS + CONSTANTS:
        ins[name + "_in"] = (saved[name], ANY)
    for name in ("wz", "wx", "wo"):
        ins[name + "_in"] = (weights[name], ANY)
    ins["wn_in"] = (weights["wn"].reshape(blocked(narrow)), ANY)
    outs = {}
    scratch = common_scratch(
        param_shapes(params), width, inner, state, n_blocks, tokens, at.n_tensor, depth
    )
    scratch.update(
        carry_out=vmem((inner // GROUP, state, GROUP), BF16),
        carry_in=vmem((inner // GROUP, state, GROUP), BF16),
        carry_send=DMA((inner // GROUP,)),
        carry_recv=DMA((inner // GROUP,)),
        nx=vmem((PAD + tokens, width), BF16),
        wz=vmem((width, inner), BF16),
        wo=vmem((width, inner), BF16),
        collect=vmem((inner, LANES), BF16),
        gate=vmem((2, tokens, GROUP)),
        mixed=vmem((2, tokens, GROUP)),
        stream_sem=DMA((2, 2)),
        braw=vmem((PAD + tokens, 2 * state)),
        g_branch=vmem((tokens, width), BF16),
        g_branch_t=vmem((width, tokens), BF16),
        normed_t=vmem((width, tokens), BF16),
        along=vmem((tokens, LANES)),
        c_t=vmem((n_blocks, state, SCAN_BLOCK), BF16),
        g_run=vmem((tokens, LANES)),
        direct=vmem((tokens, LANES)),
        g_heads=vmem((8, LANES)),
        g_gain=vmem((8, width)),
        go=vmem((tokens, GROUP), BF16),
        gq=vmem((PAD + tokens, inner)),
        gx=vmem((tokens + PAD, inner)),
        gb=vmem((tokens + PAD, 2 * state)),
        pz=vmem((tokens, inner), BF16),
        px=vmem((tokens, inner), BF16),
        pb=vmem((tokens, 2 * state), BF16),
        pd=vmem((tokens, LANES), BF16),
        d_states=vmem((n_blocks + 1, state, inner)),
        g_pair=vmem((SCAN_BLOCK, SCAN_BLOCK)),
        gn=vmem((tokens, width)),
        g_wo=vmem(blocked(inner), BF16),
        g_wz=vmem(blocked(inner), BF16),
        g_wx=vmem(blocked(inner), BF16),
        g_narrow=vmem(blocked(narrow), BF16),
        halo_send=DMA((2,)),
        halo_recv=DMA((2,)),
    )
    small, wide = shaped(small_shape), shaped((rows, part))
    if cfg.closing:
        scratch.update(gh_next=vmem((tokens, width), BF16), g_small=vmem(small_shape))
    else:
        outs.update(
            gh_next=(shaped((tokens, width), F32 if cfg.layer else BF16), VMEM),
            g_small=(small, VMEM),
            g_wx_out=(shaped(blocked(inner), BF16), ANY),
            g_narrow_out=(shaped(blocked(narrow), BF16), ANY),
        )
    if cfg.direct:
        total = 2 * (part // LANES)
        outs.update(sum_wo=(wide, VMEM), sum_wz=(wide, VMEM))
        if cfg.more:
            total += part // LANES + 1
            ins["prior_wx_in"] = (prior["g_wx_out"], ANY)
            ins["prior_narrow_in"] = (prior["g_narrow_out"], ANY)
            outs.update(sum_wx=(wide, VMEM), sum_narrow=(shaped((rows, LANES)), VMEM))
        if cfg.turn:
            ins["turn_in"] = (turn, VMEM)
            outs["turned"] = (shaped(turn.shape, BF16), ANY)
            scratch.update(turn_sems(at))
        if cfg.closing:
            total += part // LANES + 1
            packed = (cfg.layers,) + small_shape
            quarter = (small_shape[0] // depth, LANES)
            for layer in range(1, cfg.layers):
                ins[f"small{layer}"] = (others[layer]["small"], VMEM)
                if layer > 1:
                    ins[f"narrow{layer}"] = (others[layer]["narrow"], VMEM)
            outs.update(
                close_wx=(wide, VMEM),
                narrow=(shaped((cfg.layers, at.n_tensor, rows, LANES)), VMEM),
                small_sum=(shaped(packed), VMEM),
                input_grad=(shaped((at.n_dp, piece, width), BF16), VMEM),
            )
            scratch.update(
                close_narrow=vmem((rows, LANES)),
                returned=vmem((at.n_dp, piece, width), BF16),
                packed=vmem(packed),
                small_core=vmem(packed),
                through_send=DMA((depth,)),
                through_recv=DMA((depth,)),
                small_x=vmem(packed),
                small_y=vmem(packed),
                sum_core=vmem(packed),
                sum_x=vmem(packed),
                sum_y=vmem(packed),
                small_z=vmem((cfg.layers, depth - 1) + quarter),
                small_send=DMA((cfg.layers, 1 + 2 * depth)),
                small_recv=DMA((cfg.layers, 1 + 2 * depth)),
                back_send=DMA((at.parts, at.n_tensor)),
                back_recv=DMA((at.n_dp,)),
                back_own=DMA((2,)),
                narrow_send=DMA((at.n_tensor - 1,)),
                narrow_recv=DMA((at.n_tensor - 1,)),
            )
        scratch.update(reduce_scratch(total, depth, rows))
    else:
        outs.update(
            g_wo_out=(shaped((width, inner), BF16), ANY),
            g_wz_out=(shaped((width, inner), BF16), ANY),
        )
    return call_kernel(
        partial(backward_body, cfg), f"layer_{cfg.layer}_backward", 11 + cfg.layer, ins, outs, scratch
    )


def deal_sources(at):
    return [(at.tensor * at.parts + k, other) for k in range(at.parts) for other in range(at.n_tensor)]


def finish_body(cfg, r):
    tensor = lax.axis_index(TENSOR)
    places = small_rows(cfg.width, cfg.inner, cfg.state)
    own = cfg.heads // r.narrow.shape[1]
    row = lax.broadcasted_iota(jnp.int32, (own, LANES), 0)
    column = lax.broadcasted_iota(jnp.int32, (own, LANES), 1)
    pick = (row + tensor * own == column).astype(F32)
    r.out_block[...] = r.block[...]
    r.out_grad[...] = r.grad[...]

    def lay_out(target, layer, start, rows, tiles):
        for k in range(rows):
            for tile in range(tiles):
                value = r.small_sum[layer, pl.ds(start + k * tiles + tile, 1), :]
                columns = pl.ds(tile * LANES, LANES)
                if len(target.shape) == 3:
                    target[k, pl.ds(layer, 1), columns] = value
                else:
                    target[pl.ds(layer, 1), columns] = value

    for layer in range(cfg.layers):
        for name in ("wz", "wx", "wo"):
            getattr(r, "out_" + name)[layer] = getattr(r, f"{name}{layer}")[...]
        for side in range(2):
            r.out_bc[layer, :, side * LANES : (side + 1) * LANES] = r.narrow[layer, side]
        picked = lax.dot_general(
            pick, r.narrow[layer, 2], NT, precision=lax.Precision.HIGHEST, preferred_element_type=F32
        )
        for k in range(own):
            r.out_dt[k, pl.ds(layer, 1), :] = picked[k : k + 1, :]
        lay_out(r.out_gain, layer, places.gain, 1, cfg.width // LANES)
        lay_out(r.out_gate_gain, layer, places.gate_gain, 1, cfg.inner // LANES)
        lay_out(r.out_tap_x, layer, places.tap_x, WIDTH + 1, cfg.inner // LANES)
        lay_out(r.out_tap_b, layer, places.tap_b, WIDTH + 1, 2 * cfg.state // LANES)
        for index, target in enumerate((r.out_bias, r.out_alog, r.out_skip)):
            target[pl.ds(layer, 1), :] = r.small_sum[
                layer, pl.ds(places.heads + index, 1), : cfg.heads
            ]


def finish(cfg, block, grad, sums, narrow, small_sum):
    layers, tensor, rows, _ = narrow.shape
    part = cfg.inner // tensor
    ins = dict(
        block=(block, VMEM), grad=(grad, VMEM), narrow=(narrow, VMEM), small_sum=(small_sum, VMEM)
    )
    for layer in range(layers):
        for name in ("wz", "wx", "wo"):
            ins[f"{name}{layer}"] = (sums[layer][name], VMEM)
    wide = (shaped((layers, rows, part)), VMEM)
    per_head = (shaped((layers, cfg.heads)), VMEM)
    outs = dict(
        out_block=(shaped(block.shape, BF16), VMEM),
        out_grad=(shaped(grad.shape, BF16), VMEM),
        out_gain=(shaped((layers, cfg.width)), VMEM),
        out_wz=wide,
        out_wx=wide,
        out_bc=(shaped((layers, rows, 2 * cfg.state)), VMEM),
        out_dt=(shaped((cfg.heads // tensor, layers, rows)), VMEM),
        out_tap_x=(shaped((WIDTH + 1, layers, cfg.inner)), VMEM),
        out_tap_b=(shaped((WIDTH + 1, layers, 2 * cfg.state)), VMEM),
        out_bias=per_head,
        out_alog=per_head,
        out_skip=per_head,
        out_gate_gain=(shaped((layers, cfg.inner)), VMEM),
        out_wo=wide,
    )
    results = call_kernel(partial(finish_body, cfg), "finish", None, ins, outs, {})
    for name, order in (("out_dt", (1, 2, 0)), ("out_tap_x", (1, 0, 2)), ("out_tap_b", (1, 0, 2))):
        results[name] = results[name].transpose(order)
    return tuple(results.values())


def local(
    hidden_in,
    lengths,
    order,
    in_gain,
    w_z,
    w_x,
    w_bc,
    w_dt,
    conv_x,
    conv_bc,
    dt_bias,
    a_log,
    d_skip,
    gated_gain,
    w_out,
    cotangent,
):
    at = place()
    n_dp, n_tensor = at.n_dp, at.n_tensor
    piece = hidden_in.shape[2]
    width = hidden_in.shape[3]
    tokens = piece * n_dp
    layers = w_z.shape[0]
    inner = gated_gain.shape[1]
    heads = dt_bias.shape[1]
    state = conv_bc.shape[2] // 2
    rows_local = w_z.shape[1]
    part = w_z.shape[2]
    direct = rows_local % 16 == 0 and piece % 16 == 0 and n_tensor == 4 and n_dp == 2 * n_tensor

    quarter = 2 * state // n_tensor
    narrow = jnp.concatenate(
        [lax.dynamic_slice_in_dim(w_bc, at.tensor * quarter, quarter, 2), w_dt], axis=2
    )
    narrow = jnp.pad(narrow, ((0, 0), (0, 0), (0, LANES - narrow.shape[2])))
    blocks = dict(wz=w_z, wx=w_x, wn=narrow, wo=w_out)
    params = dict(
        lengths=lengths,
        order=order,
        in_gain=in_gain,
        conv_x=conv_x.transpose(1, 0, 2),
        conv_bc=conv_bc.transpose(1, 0, 2),
        dt_bias=dt_bias,
        a_log=a_log,
        d_skip=d_skip,
        gated_gain=gated_gain,
    )

    def to_run(values):
        swapped = lax.all_to_all(
            values.reshape(n_tensor, at.parts, piece, width), TENSOR, split_axis=0, concat_axis=0
        )
        return swapped.transpose(1, 0, 2, 3).reshape(tokens, width)

    def to_pieces(values):
        swapped = values.reshape(at.parts, n_tensor, piece, width).transpose(1, 0, 2, 3)
        return lax.all_to_all(swapped, TENSOR, split_axis=0, concat_axis=0).reshape(
            n_dp, piece, width
        )

    def config(layer):
        return SimpleNamespace(
            layer=layer,
            layers=layers,
            direct=direct,
            more=layer + 1 < layers,
            turn=layer + 1 == layers,
            closing=direct and layer == 0,
            tokens=tokens,
            width=width,
            inner=inner,
            state=state,
            heads=heads,
            head_size=inner // heads,
        )

    weights = [{} for layer in range(layers)]
    if direct:
        hidden = hidden_in[:, 0]
    else:
        arranged = jnp.take(hidden_in, order, axis=0)
        dealt = lax.all_to_all(arranged, DP, split_axis=0, concat_axis=1, tiled=True)
        hidden = to_run(dealt[0])

        def whole(stacked):
            gathered = lax.all_gather(stacked, DP, axis=1, tiled=True)
            return lax.all_gather(gathered, TENSOR, axis=2, tiled=True)

        for name, block in blocks.items():
            stacked = whole(block)
            for layer in range(layers):
                weights[layer][name] = stacked[layer]
    forward = layers_forward(config(0), at, hidden, params, weights, blocks, cotangent[0])
    if direct:
        hidden = forward["hidden"]
        for layer in range(layers):
            for name in blocks:
                weights[layer][name] = forward[f"whole_{name}{layer}"].reshape(width, -1)
        grad = forward["turned"].reshape(tokens, width)
    else:
        grad = to_run(cotangent[0])
    inputs = [hidden] + [forward[f"h{layer + 1}"] for layer in range(layers)]
    kept = [
        {name: forward[f"{name}{layer}_out"] for name in SAVED + TERMS} for layer in range(layers)
    ]
    for saved in kept:
        saved.update({name: forward[name + "_out"] for name in CONSTANTS})
    h_low = forward["h_low"]
    sums = [{} for layer in range(layers)]
    results = None
    for layer in reversed(range(layers)):
        results = layer_backward(
            config(layer),
            at,
            grad,
            inputs[layer],
            inputs[layer + 1],
            params,
            kept[layer],
            weights[layer],
            results,
            h_low.reshape(n_dp, piece, width),
            sums,
        )
        if direct:
            sums[layer].update(wo=results["sum_wo"], wz=results["sum_wz"])
            if layer + 1 < layers:
                sums[layer + 1].update(wx=results["sum_wx"], narrow=results["sum_narrow"])
            if layer + 1 == layers:
                block_out = results["turned"]
            if layer:
                grad, sums[layer]["small"] = results["gh_next"], results["g_small"]
        else:
            grad, sums[layer]["small"] = results["gh_next"], results["g_small"]
            for name in ("wo", "wz", "wx", "narrow"):
                sums[layer][name] = results[f"g_{name}_out"]

    if direct:
        sums[0]["wx"] = results["close_wx"]
        input_grad = results["input_grad"][:, None]
        narrow_sum, small_sum = results["narrow"], results["small_sum"]
    else:
        block_out = to_pieces(h_low)
        returned = lax.all_to_all(
            to_pieces(grad)[None], DP, split_axis=1, concat_axis=0, tiled=True
        )
        input_grad = jnp.zeros_like(returned).at[order].set(returned)

        def scattered(name):
            terms = jnp.stack([entry[name] for entry in sums]).astype(F32)
            mine = lax.psum_scatter(terms, DP, scatter_dimension=1, tiled=True)
            return lax.psum_scatter(mine, TENSOR, scatter_dimension=2, tiled=True)

        for name in ("wz", "wx", "wo"):
            total = scattered(name)
            for layer in range(layers):
                sums[layer][name] = total[layer]
        narrow_sum = lax.all_gather(scattered("narrow"), TENSOR, axis=1)
        small_sum = lax.psum(jnp.stack([entry["small"] for entry in sums]), (DP, TENSOR))
    return finish(config(0), block_out[None], input_grad, sums, narrow_sum, small_sum)


def solution(mesh):
    return jax.shard_map(
        local,
        mesh=mesh,
        in_specs=(
            P(None, DP, TENSOR, None),
            P(),
            P(),
            P(),
            P(None, DP, TENSOR),
            P(None, DP, TENSOR),
            P(None, DP, None),
            P(None, DP, TENSOR),
            P(),
            P(),
            P(),
            P(),
            P(),
            P(),
            P(None, DP, TENSOR),
            P(DP, None, TENSOR, None),
        ),
        out_specs=(
            P(DP, None, TENSOR, None),
            P(None, DP, TENSOR, None),
            P(),
            P(None, DP, TENSOR),
            P(None, DP, TENSOR),
            P(None, DP, None),
            P(None, DP, TENSOR),
            P(),
            P(),
            P(),
            P(),
            P(),
            P(),
            P(None, DP, TENSOR),
        ),
        check_vma=False,
    )
```

```python
from functools import partial
from types import SimpleNamespace

import jax
import jax.numpy as jnp
from jax import lax
from jax.experimental import pallas as pl
from jax.experimental.pallas import tpu as pltpu
from jax.sharding import PartitionSpec as P

SCAN_BLOCK = 256
HALF = SCAN_BLOCK // 2
EPS = 1e-05
LOG2E = 1.4426950408889634
F32, BF16 = jnp.float32, jnp.bfloat16
LANES = 128
GROUP = 256
PAD = 16
ROWS = 128
WIDTH = 4
NN = (((1,), (0,)), ((), ()))
NT = (((1,), (1,)), ((), ()))
MESH = pl.DeviceIdType.MESH
VMEM = pl.BlockSpec(memory_space=pltpu.VMEM)
SMEM = pl.BlockSpec(memory_space=pltpu.SMEM)
ANY = pl.BlockSpec(memory_space=pl.ANY)
DMA = pltpu.SemaphoreType.DMA
DP, TENSOR = "dp", "tensor"
VMEM_LIMIT = 63 * 1024 * 1024


def mm(left, right, dims=NN):
    return lax.dot_general(left, right, dims, preferred_element_type=F32)


def exact(left, right):
    return lax.dot_general(
        left, right, NN, precision=lax.Precision.HIGHEST, preferred_element_type=F32
    )


def sigmoid(values):
    return 0.5 * jnp.tanh(0.5 * values) + 0.5


def halves(values):
    high = values.astype(BF16)
    return high, (values - high.astype(F32)).astype(BF16)


def beside(values):
    return jnp.concatenate(halves(values), axis=1)


def lanes_of(step, size):
    return pl.ds(pl.multiple_of(step * size, size), size)


def rows_of(step, size, start=0):
    return pl.ds(pl.multiple_of(start + step * size, PAD), size)


def shaped(shape, dtype=F32):
    return jax.ShapeDtypeStruct(shape, dtype)


def vmem(shape, dtype=F32):
    return pltpu.VMEM(shape, dtype)


def call_kernel(body, name, collective_id, ins, outs, scratch):
    names = list(ins) + list(outs) + list(scratch)

    def kernel(*refs):
        body(SimpleNamespace(**dict(zip(names, refs))))

    remote_copies = (
        dict(collective_id=collective_id, has_side_effects=True) if collective_id is not None else {}
    )
    results = pl.pallas_call(
        kernel,
        out_shape=[shape for shape, _ in outs.values()],
        in_specs=[spec for _, spec in ins.values()],
        out_specs=[spec for _, spec in outs.values()],
        scratch_shapes=list(scratch.values()),
        compiler_params=pltpu.CompilerParams(vmem_limit_bytes=VMEM_LIMIT, **remote_copies),
        name=name,
    )(*[array for array, _ in ins.values()])
    return dict(zip(outs, results))


def place():
    dp, tensor = lax.axis_index(DP), lax.axis_index(TENSOR)
    n_dp, n_tensor = lax.axis_size(DP), lax.axis_size(TENSOR)
    return SimpleNamespace(
        dp=dp,
        tensor=tensor,
        n_dp=n_dp,
        n_tensor=n_tensor,
        depth=n_dp // 2,
        core=lax.rem(tensor, 2),
        x=tensor // 2,
        y=lax.rem(dp, 2),
        z=dp // 2,
        parts=n_dp // n_tensor,
    )


def over_core(at):
    return {TENSOR: at.tensor + 1 - 2 * at.core}


def over_x(at):
    return {TENSOR: lax.rem(at.tensor + 2, at.n_tensor)}


def over_y(at):
    return {DP: at.dp + 1 - 2 * at.y}


def over_z(at, k):
    return {DP: lax.rem(at.z + k, at.depth) * 2 + at.y}


def grid_partners(at):
    return [over_core(at), over_x(at), over_y(at)] + [over_z(at, k) for k in range(1, at.depth)]


def tensor_partners(at):
    return [{TENSOR: lax.rem(at.tensor + k, at.n_tensor)} for k in range(1, at.n_tensor)]


def greet(device):
    pl.semaphore_signal(
        pltpu.get_barrier_semaphore(), inc=1, device_id=device, device_id_type=MESH
    )


def greet_all(partners):
    for partner in partners:
        greet(partner)


def met(count):
    pl.semaphore_wait(pltpu.get_barrier_semaphore(), count)


def remote(source, target, send, recv, device):
    return pltpu.make_async_remote_copy(
        src_ref=source,
        dst_ref=target,
        send_sem=send,
        recv_sem=recv,
        device_id=device,
        device_id_type=MESH,
    )


class Rounds:
    def __init__(self):
        self.units = []
        self.next = 0
        self.begun = 0
        self.finished = set()

    def add(self, unit):
        self.units.append(unit)

    def begin(self, count):
        while self.begun < min(count, len(self.units)):
            self.units[self.begun][0]()
            self.begun += 1

    def start(self):
        self.begin(2 * AHEAD)

    def tick(self):
        pairs = -(-len(self.units) // 2)
        if not self.units or self.next >= pairs + STAGES - 1:
            return
        for stage in reversed(range(STAGES)):
            pair = self.next - stage
            if 0 <= pair < pairs:
                for unit in self.units[2 * pair : 2 * pair + 2]:
                    unit[1][stage]()
        self.next += 1
        self.begin(2 * (self.next + AHEAD))

    def ready(self, unit, rounds_ago=0):
        return self.next >= unit // 2 + STAGES + rounds_ago or self.finished.issuperset({unit})

    def finish(self, unit):
        while not self.ready(unit):
            self.tick()
        if unit not in self.finished:
            self.finished.add(unit)
            self.units[unit][2]()

    def drain(self):
        for unit in range(len(self.units)):
            self.finish(unit)


def gather_sems(total, depth):
    return dict(
        gather_z_send=DMA((total, depth - 1)),
        gather_z_recv=DMA((total, depth - 1)),
        gather_send=DMA((total, 5)),
        gather_recv=DMA((total, 5)),
        gather_own=DMA((total,)),
    )


def gather_unit(at, r, index, block, whole, start, full):
    core, x, y, z = at.core, at.x, at.y, at.z

    def lanes(side):
        return pl.ds(pl.multiple_of((2 * side + core) * full + start, LANES), LANES)

    def same(part, slot, device):
        return remote(
            part, part, r.gather_send.at[index, slot], r.gather_recv.at[index, slot], device
        )

    mine = block.at[:, pl.ds(start, LANES)]
    keep = pltpu.make_async_copy(mine, whole.at[z, y, :, lanes(x)], r.gather_own.at[index])
    along_z = [
        remote(
            mine,
            whole.at[z, y, :, lanes(x)],
            r.gather_z_send.at[index, k - 1],
            r.gather_z_recv.at[index, k - 1],
            over_z(at, k),
        )
        for k in range(1, at.depth)
    ]
    if index % 2 == 0:
        one = [same(whole.at[:, y, :, lanes(x)], 0, over_x(at))]
        two = [same(whole.at[:, y, :, lanes(side)], 1 + side, over_y(at)) for side in range(2)]
    else:
        one = [same(whole.at[:, y, :, lanes(x)], 0, over_y(at))]
        two = [same(whole.at[:, :, :, lanes(x)], 1, over_x(at))]
    last = [same(whole.at[:, :, :, lanes(side)], 3 + side, over_core(at)) for side in range(2)]

    def begin():
        keep.start()
        for copy in along_z:
            copy.start()

    def hand_on(before, after):
        def step():
            for copy in before:
                copy.wait_recv()
            for copy in after:
                copy.start()

        return step

    def first():
        keep.wait()
        hand_on(along_z, one)()

    def finish():
        for copy in last:
            copy.wait_recv()
        for copy in along_z + one + two + last:
            copy.wait_send()

    return begin, [first, hand_on(one, two), hand_on(two, last)], finish


def reduce_scratch(total, depth, rows):
    scratch = dict(
        reduce_send=DMA((total, 4)),
        reduce_recv=DMA((total, 4)),
        reduce_z_send=DMA((total, depth - 1)),
        reduce_z_recv=DMA((total, depth - 1)),
    )
    for index in range(total):
        second = (depth, 2, rows, LANES) if index % 2 == 0 else (2, depth, rows, LANES)
        shapes = ((2, depth, 2, rows, LANES), second, (depth, rows, LANES), (depth - 1, rows, LANES))
        for stage, shape in enumerate(shapes):
            scratch[f"sum{stage}_{index}"] = vmem(shape, BF16)
    return scratch


def reduce_unit(at, r, index, source, start, full, put):
    core, x, y, z, depth = at.core, at.x, at.y, at.z, at.depth
    a, b, c, d = (getattr(r, f"sum{stage}_{index}") for stage in range(4))
    send, recv = r.reduce_send, r.reduce_recv
    x_first = index % 2 == 0

    def lanes(side, which):
        return pl.ds(pl.multiple_of((2 * side + which) * full + start, LANES), LANES)

    zero = [
        remote(
            source.at[:, :, :, lanes(side, 1 - core)],
            a.at[side],
            send.at[index, side],
            recv.at[index, side],
            over_core(at),
        )
        for side in range(2)
    ]
    if x_first:
        one = remote(a.at[1 - x], b, send.at[index, 2], recv.at[index, 2], over_x(at))
        two = remote(b.at[:, 1 - y], c, send.at[index, 3], recv.at[index, 3], over_y(at))
    else:
        one = remote(a.at[:, :, 1 - y], b, send.at[index, 2], recv.at[index, 2], over_y(at))
        two = remote(b.at[1 - x], c, send.at[index, 3], recv.at[index, 3], over_x(at))
    three = [
        remote(
            c.at[lax.rem(z + k, depth)],
            d.at[k - 1],
            r.reduce_z_send.at[index, k - 1],
            r.reduce_z_recv.at[index, k - 1],
            over_z(at, k),
        )
        for k in range(1, depth)
    ]

    def plus(left, right):
        return (left.astype(F32) + right.astype(F32)).astype(BF16)

    def begin():
        for copy in zero:
            copy.start()

    def after_core():
        for copy in zero:
            copy.wait_recv()

        @pl.loop(0, 2 * depth)
        def _(step):
            high, low = step // 2, lax.rem(step, 2)
            for side in range(2):
                a[side, high, low] = plus(a[side, high, low], source[high, low, :, lanes(side, core)])

        one.start()

    def after_first():
        one.wait_recv()

        @pl.loop(0, depth)
        def _(high):
            for side in range(2):
                if x_first:
                    b[high, side] = plus(b[high, side], a[x, high, side])
                else:
                    b[side, high] = plus(b[side, high], a[side, high, y])

        two.start()

    def after_second():
        two.wait_recv()

        @pl.loop(0, depth)
        def _(high):
            c[high] = plus(c[high], b[high, y] if x_first else b[x, high])

        for copy in three:
            copy.start()

    def finish():
        value = c[z].astype(F32)
        for k, copy in enumerate(three):
            copy.wait_recv()
            value = value + d[k].astype(F32)
        put(value)
        for copy in zero + [one, two] + three:
            copy.wait_send()

    return begin, [after_core, after_first, after_second], finish


STAGES = 3
AHEAD = 2


def conv_rows(raw, taps, start, columns):
    total = taps(WIDTH, columns)
    for tap in range(WIDTH):
        first = PAD - (WIDTH - 1) + tap + start
        total = total + taps(tap, columns) * raw[pl.ds(first, ROWS), columns]
    return total


def taps_of(ref, layer):
    def taps(tap, columns):
        return ref[tap, pl.ds(layer, 1), columns]

    return taps


def fill_constants(r, at, head_size, state, heads):
    inner = r.spread.shape[1]
    row = lax.broadcasted_iota(jnp.int32, (2 * LANES, inner), 0)
    column = lax.broadcasted_iota(jnp.int32, (2 * LANES, inner), 1)
    r.spread[...] = (lax.rem(row, LANES) == column // head_size).astype(F32).astype(BF16)
    if hasattr(r, "collect"):
        row = lax.broadcasted_iota(jnp.int32, (inner, LANES), 0)
        column = lax.broadcasted_iota(jnp.int32, (inner, LANES), 1)
        r.collect[...] = (row // head_size == column).astype(F32).astype(BF16)
    quarter, own = 2 * state // at.n_tensor, heads // at.n_tensor
    shape = (at.n_tensor * LANES, 2 * state + LANES)
    row = lax.broadcasted_iota(jnp.int32, shape, 0)
    column = lax.broadcasted_iota(jnp.int32, shape, 1)
    block, lane = row // LANES, lax.rem(row, LANES)
    target = jnp.where(
        lane < quarter,
        block * quarter + lane,
        jnp.where(lane < quarter + own, 2 * state + block * own + lane - quarter, -1),
    )
    r.select[...] = (target == column).astype(F32).astype(BF16)


def split_narrow(r, narrow):
    narrow = narrow[...].reshape(r.wbc.shape[0], r.select.shape[0])
    r.wbc[...] = mm(narrow, r.select[:, : r.wbc.shape[1]]).astype(BF16)
    r.wdt[...] = mm(narrow, r.select[:, r.wbc.shape[1] :]).astype(BF16)


def fill_live(r, at):
    tokens = r.live.shape[0]
    length = r.lengths[r.order[at.dp]]
    position = lax.broadcasted_iota(jnp.int32, (tokens, LANES), 0) + at.tensor * tokens
    r.live[...] = (position < length).astype(F32)


def step_terms(r, layer, block):
    rows = pl.ds(block * SCAN_BLOCK, SCAN_BLOCK)
    value = r.dtp[rows, :]
    size = (jnp.maximum(value, 0.0) + jnp.log1p(jnp.exp(-jnp.abs(value)))) * r.live[rows, :]
    r.dt[block] = size
    row_id = lax.broadcasted_iota(jnp.int32, (SCAN_BLOCK, SCAN_BLOCK), 0)
    col_id = lax.broadcasted_iota(jnp.int32, (SCAN_BLOCK, SCAN_BLOCK), 1)
    earlier = (row_id >= col_id).astype(F32)
    running = exact(earlier, size * (r.heads[layer, 1:2, :] * LOG2E))
    r.run[block] = running
    r.run_t[block] = running.T
    total = running[SCAN_BLOCK - 1 : SCAN_BLOCK, :]
    r.step_two[block] = beside(size)
    r.grow_two[block] = beside(jnp.exp2(running))
    r.keep_two[block] = beside(jnp.exp2(total - running))
    whole = jnp.broadcast_to(jnp.exp2(total), (8, LANES))
    r.decay[block] = mm(beside(whole), r.spread[...])


def fill_heads(r):
    heads = r.dt_bias.shape[1]
    row = lax.broadcasted_iota(jnp.int32, (heads, LANES), 0)
    column = lax.broadcasted_iota(jnp.int32, (heads, LANES), 1)
    widen = (row == column).astype(F32)
    for index, values in enumerate((r.dt_bias[...], -jnp.exp(r.a_log[...]), r.d_skip[...])):
        padded = exact(values, widen)
        for layer in range(values.shape[0]):
            r.heads[layer, index : index + 1, :] = padded[layer : layer + 1, :]


def spread_skip(r, layer):
    r.skip[...] = mm(
        beside(jnp.broadcast_to(r.heads[layer, 2:3, :], (8, LANES))), r.spread[...]
    )


def head_row(head, head_size):
    lane = lax.broadcasted_iota(jnp.int32, (1, GROUP), 1)
    return (lane // head_size == head).astype(F32).astype(BF16)


def own_lanes(stacked, per_group, head_size):
    rows = stacked.shape[0] // per_group
    lane = lax.broadcasted_iota(jnp.int32, (1, GROUP), 1) // head_size
    total = stacked[:rows]
    for head in range(1, per_group):
        total = jnp.where(lane == head, stacked[head * rows : (head + 1) * rows], total)
    return total


def columns_of(r, block, group, per_group):
    return pltpu.roll(r.run[block], lax.rem(LANES - per_group * group, LANES), 1)


def common_scratch(param_shapes, width, inner, state, n_blocks, tokens, n_tensor, depth):
    return dict(
        wbc=vmem((width, 2 * state), BF16),
        wdt=vmem((width, LANES), BF16),
        spread=vmem((2 * LANES, inner), BF16),
        select=vmem((n_tensor * LANES, 2 * state + LANES), BF16),
        live=vmem((tokens, LANES)),
        skip=vmem((8, inner)),
        dt=vmem((n_blocks, SCAN_BLOCK, LANES)),
        run=vmem((n_blocks, SCAN_BLOCK, LANES)),
        run_t=vmem((n_blocks, LANES, SCAN_BLOCK)),
        step_two=vmem((n_blocks, SCAN_BLOCK, 2 * LANES), BF16),
        grow_two=vmem((n_blocks, SCAN_BLOCK, 2 * LANES), BF16),
        keep_two=vmem((n_blocks, SCAN_BLOCK, 2 * LANES), BF16),
        decay=vmem((n_blocks, 8, inner)),
        pair=vmem((n_blocks, SCAN_BLOCK, SCAN_BLOCK)),
        states=vmem((n_blocks + 1, state, inner)),
        bc=vmem((tokens, 2 * state), BF16),
        xc=vmem((tokens, inner), BF16),
        dtp=vmem((tokens, LANES)),
        rms=vmem((tokens, LANES)),
        in_gain=vmem(param_shapes[0]),
        conv_x=vmem(param_shapes[1]),
        conv_bc=vmem(param_shapes[2]),
        dt_bias=vmem(param_shapes[3]),
        a_log=vmem(param_shapes[4]),
        d_skip=vmem(param_shapes[5]),
        gated_gain=vmem(param_shapes[6]),
        heads=vmem((param_shapes[3][0], 3, LANES)),
        load_sem=DMA((40,)),
        store_sem=DMA((24,)),
    )


def small_rows(width, inner, state):
    sizes = dict(
        heads=8,
        gain=-(-width // LANES // 8) * 8,
        gate_gain=inner // LANES,
        tap_x=(WIDTH + 1) * (inner // LANES),
        tap_b=(WIDTH + 1) * (2 * state // LANES),
    )
    starts, total = {}, 0
    for name, size in sizes.items():
        starts[name] = total
        total += size
    return SimpleNamespace(all=-(-total // 64) * 64, **starts)


def param_loads(r):
    copies = [
        pltpu.make_async_copy(getattr(r, "p_" + name), getattr(r, name), r.load_sem.at[16 + index])
        for index, name in enumerate(PARAMS)
    ]
    for copy in copies:
        copy.start()
    return copies


def param_inputs(params):
    ins = {"p_" + name: (params[name], ANY) for name in PARAMS}
    return dict(lengths=(params["lengths"], SMEM), order=(params["order"], SMEM), **ins)


def param_shapes(params):
    return [params[name].shape for name in PARAMS]


def row_blocks(whole, target, sems):
    depth, two, rows, _ = whole.shape
    return [
        pltpu.make_async_copy(
            whole.at[index // two, index % two],
            target.at[pl.ds(index * rows, rows), :],
            sems.at[index],
        )
        for index in range(depth * two)
    ]


PARAMS = ("in_gain", "conv_x", "conv_bc", "dt_bias", "a_log", "d_skip", "gated_gain")
TERMS = ("dt", "run", "run_t", "step_two", "grow_two", "keep_two", "decay")
CONSTANTS = ("spread", "collect", "select")
SAVED = ("nx", "gate", "xraw", "braw", "xc", "bc", "dtp", "mixed", "states", "rms")


class Weights:
    def __init__(self, queues, sources):
        self.queues = queues
        self.sources = sources
        self.started = {name: 0 for name in sources}
        self.used = {name: 0 for name in sources}

    def load(self, name, rounds_ago):
        layer = self.started[name]
        if layer == len(self.sources[name]) or self.used[name] != layer:
            return
        queue, units, copies = self.sources[name][layer]
        if all(queue.ready(unit, rounds_ago) for unit in units):
            for unit in units:
                queue.finish(unit)
            for copy in copies:
                copy.start()
            self.started[name] += 1

    def tick(self):
        for queue in self.queues:
            queue.tick()
        for name in self.sources:
            self.load(name, 1)

    def wait(self, name, layer):
        queue, units, copies = self.sources[name][layer]
        while not all(queue.ready(unit) for unit in units):
            self.tick()
        self.load(name, 0)
        for copy in copies:
            copy.wait()

    def done(self, name):
        self.used[name] += 1
        self.load(name, 1)


def deal_start(at, r):
    runner = at.dp // at.parts
    at_home = runner == at.tensor
    piece = r.arranged.shape[1]

    def spot(k, other):
        start = (k * at.n_tensor + other) * piece
        return r.dealt.at[pl.ds(pl.multiple_of(start, PAD), piece), :]

    slot = lax.rem(at.dp, at.parts)
    keep = pltpu.make_async_copy(r.arranged.at[at.dp], spot(slot, at.tensor), r.deal_own)
    deal = [
        remote(
            r.arranged.at[j],
            spot(slot, at.tensor),
            r.deal_send.at[j],
            r.deal_recv.at[slot, at.tensor],
            {DP: j, TENSOR: runner},
        )
        for j in range(at.n_dp)
    ]
    for j in range(at.n_dp):
        pl.when((j != at.dp) | (runner != at.tensor))(deal[j].start)
    pl.when(at_home)(keep.start)

    def arrive():
        for k in range(at.parts):
            for other in range(at.n_tensor):
                arrival = remote(
                    r.arranged.at[0],
                    spot(k, other),
                    r.deal_send.at[0],
                    r.deal_recv.at[k, other],
                    {TENSOR: lax.rem(at.tensor + 1, at.n_tensor)},
                )
                pl.when((at.tensor * at.parts + k != at.dp) | (other != at.tensor))(
                    arrival.wait_recv
                )
        pl.when(at_home)(keep.wait)

    def rest():
        for j in range(at.n_dp):
            pl.when((j != at.dp) | (runner != at.tensor))(deal[j].wait_send)

    return arrive, rest


def forward_body(cfg, r):
    at = place()
    direct = cfg.direct
    width = r.dealt.shape[1]
    small_loads = param_loads(r)
    count = 0
    if direct:
        greet_all(grid_partners(at))
        for source, other in deal_sources(at):

            @pl.when((source != at.dp) | (other != at.tensor))
            def _():
                greet({DP: source, TENSOR: other})

        at_home = (at.dp // at.parts == at.tensor).astype(jnp.int32)
        count = len(grid_partners(at)) + at.n_dp - at_home
    greet_all(tensor_partners(at))
    count = count + len(tensor_partners(at))

    first_queue, queue = Rounds(), Rounds()
    names = ("wn", "wx", "wz", "wo")
    sources = {name: [] for name in names}
    total = 0
    for layer in range(cfg.layers):
        for name in names:
            target = getattr(r, name)
            index = len(sources[name]) * len(names) + names.index(name)
            if direct:
                block, whole = getattr(r, "block_" + name), getattr(r, f"whole_{name}{layer}")
                full = block.shape[2]
                owner = first_queue if layer == 0 and name in names[:2] else queue
                units = []
                for start in range(0, full, LANES):
                    units.append(len(owner.units))
                    owner.add(gather_unit(at, r, total, block.at[layer], whole, start, full))
                    total += 1
                copies = row_blocks(whole, target, r.weight_sem.at[index])
                sources[name].append((owner, units, copies))
            else:
                whole = getattr(r, f"{name}{layer}_in")
                copy = pltpu.make_async_copy(whole, target, r.weight_sem.at[index, 0])
                sources[name].append((queue, [], [copy]))
    weights = Weights((queue,), sources)

    if direct:
        for j in range(at.n_dp):
            r.arranged[j] = r.hidden_in[r.order[j]]
    else:
        first = pltpu.make_async_copy(r.hidden_in, r.dealt, r.deal_own)
        first.start()
    met(count)
    if direct:
        first_queue.start()
        arrive, rest = deal_start(at, r)
        first_queue.tick()
        queue.start()
    fill_constants(r, at, cfg.head_size, cfg.state, cfg.heads)
    fill_live(r, at)
    for copy in small_loads:
        copy.wait()
    fill_heads(r)
    constants = []
    for index, name in enumerate(CONSTANTS):
        copy = pltpu.make_async_copy(getattr(r, name), getattr(r, name + "_out"), r.store_sem.at[20 + index])
        copy.start()
        constants.append(copy)
    if direct:
        first_queue.drain()
        for name in names[:2]:
            weights.load(name, 0)
        weights.tick()
        weights.tick()
        arrive()
        first = pltpu.make_async_copy(r.dealt, r.hidden, r.hidden_sem)
        first.start()
    else:
        first.wait()
    stores = {}
    turned = turn_copies(at, r, False) if direct else []
    for layer in range(cfg.layers):
        forward_layer(cfg, at, r, layer, weights, stores, turned)
    queue.drain()
    for copy in turned:
        copy.wait()
    if direct:
        rest()
        first.wait()
    for store in list(stores.values()) + constants:
        store.wait()


def forward_layer(cfg, at, r, layer, weights, stores, turned):
    me, last = at.tensor, at.n_tensor - 1
    h = r.dealt if layer == 0 else getattr(r, f"h{layer}")
    h_next = getattr(r, f"h{layer + 1}")
    halo = getattr(r, f"halo{layer}")
    tokens, width = h.shape
    inner, state, head_size = cfg.inner, cfg.state, cfg.head_size
    n_blocks = tokens // SCAN_BLOCK
    groups = inner // GROUP
    per_group = GROUP // head_size
    following = {TENSOR: lax.rem(me + 1, at.n_tensor)}

    def clear(*names):
        for name in names:
            if name in stores:
                stores.pop(name).wait()

    def store(name):
        index = (SAVED + TERMS).index(name)
        copy = pltpu.make_async_copy(
            getattr(r, name), getattr(r, f"{name}{layer}_out"), r.store_sem.at[index]
        )
        copy.start()
        stores[name] = copy

    halo_copy = remote(
        h.at[pl.ds(tokens - PAD, PAD), :], halo, r.halo_send.at[layer], r.halo_recv.at[layer], following
    )

    @pl.when(me < last)
    def _():
        halo_copy.start()

    spread_skip(r, layer)
    gain = r.in_gain[layer : layer + 1, :]

    def normalize(values):
        values = values.astype(F32)
        inv = lax.rsqrt(jnp.mean(values * values, axis=-1, keepdims=True) + EPS)
        return (values * inv * gain).astype(BF16)

    clear("nx", "dtp", *TERMS)

    @pl.loop(0, tokens // ROWS)
    def _(step):
        r.nx[rows_of(step, ROWS, PAD), :] = normalize(h[rows_of(step, ROWS), :])

    weights.wait("wn", layer)
    split_narrow(r, r.wn)
    weights.done("wn")
    r.dtp[...] = mm(r.nx[pl.ds(PAD, tokens), :], r.wdt[...]) + r.heads[layer, 0:1, :]
    for block in range(n_blocks):
        step_terms(r, layer, block)

    @pl.when(me > 0)
    def _():
        halo_copy.wait_recv()
        r.nx[0:PAD, :] = normalize(halo[...])

    @pl.when(me == 0)
    def _():
        r.nx[0:PAD, :] = jnp.zeros((PAD, width), BF16)

    store("nx")
    store("dtp")
    for name in TERMS:
        store(name)

    def convolve(projection, taps, raw, out, columns):
        raw[:, columns] = mm(r.nx[...], projection[:, columns])
        for start in range(0, tokens, ROWS):
            before = conv_rows(raw, taps, start, columns)
            out[pl.ds(start, ROWS), columns] = (before * sigmoid(before)).astype(BF16)

    clear("braw", "bc")
    for step in range(2 * state // GROUP):
        convolve(r.wbc, taps_of(r.conv_bc, layer), r.braw, r.bc, pl.ds(step * GROUP, GROUP))
    store("braw")
    store("bc")
    for block in range(n_blocks):
        rows = pl.ds(block * SCAN_BLOCK, SCAN_BLOCK)
        r.b_t[block] = r.bc[rows, :state].astype(F32).T.astype(BF16)
        row_id = lax.broadcasted_iota(jnp.int32, (SCAN_BLOCK, SCAN_BLOCK), 0)
        col_id = lax.broadcasted_iota(jnp.int32, (SCAN_BLOCK, SCAN_BLOCK), 1)
        scores = mm(r.bc[rows, state:], r.bc[rows, :state], NT)
        r.pair[block] = jnp.where(row_id >= col_id, scores, 0.0)

    if layer:
        weights.tick()
    weights.wait("wx", layer)
    clear("xraw", "xc", "states")
    @pl.loop(0, groups)
    def _(group):
        columns = lanes_of(group, GROUP)
        convolve(r.wx, taps_of(r.conv_x, layer), r.xraw, r.xc, columns)
        for block in range(n_blocks):
            rows = pl.ds(block * SCAN_BLOCK, SCAN_BLOCK)
            sizes = mm(r.step_two[block], r.spread[:, columns])
            keeps = mm(r.keep_two[block], r.spread[:, columns])
            weighted = (r.xc[rows, columns].astype(F32) * sizes * keeps).astype(BF16)
            r.states[block + 1, :, columns] = mm(r.b_t[block], weighted)
        pl.when(group == groups // 2 - 1)(weights.tick)

    weights.done("wx")
    store("xraw")
    store("xc")

    carry_copies = [
        remote(
            r.carry_out.at[layer, group],
            r.carry_in.at[layer, group],
            r.carry_send.at[layer, group],
            r.carry_recv.at[layer, group],
            following,
        )
        for group in range(groups)
    ]

    def chain():
        for group in range(groups):
            columns = pl.ds(group * GROUP, GROUP)

            @pl.when(me > 0)
            def _():
                carry_copies[group].wait_recv()
                r.states[0, :, columns] = r.carry_in[layer, group].astype(F32)

            @pl.when(me == 0)
            def _():
                r.states[0, :, columns] = jnp.zeros((state, GROUP), F32)

            for block in range(n_blocks):
                r.states[block + 1, :, columns] += (
                    r.states[block, :, columns] * r.decay[block, 0:1, columns]
                )
            r.carry_out[layer, group] = r.states[n_blocks, :, columns].astype(BF16)

            @pl.when(me < last)
            def _():
                carry_copies[group].start()

    pl.when(me == 0)(chain)
    clear("mixed")
    @pl.loop(0, n_blocks)
    def _(block):
        pl.when(block == 1)(weights.tick)
        rows = lanes_of(block, SCAN_BLOCK)

        @pl.loop(0, groups)
        def _(group):
            columns = lanes_of(group, GROUP)
            sizes = mm(r.step_two[block], r.spread[:, columns])
            x_here = r.xc[rows, columns].astype(F32)
            stepped = (x_here * sizes).astype(BF16)
            rolled = columns_of(r, block, group, per_group)
            upper, lower = [], []
            for head in range(per_group):
                along = r.run_t[block, pl.ds(per_group * group + head, 1), :]
                down = rolled[:, head : head + 1]
                factor = jnp.exp2(jnp.minimum(down[:HALF] - along[:, :HALF], 0.0))
                upper.append((r.pair[block, :HALF, :HALF] * factor).astype(BF16))
                factor = jnp.exp2(jnp.minimum(down[HALF:] - along, 0.0))
                lower.append((r.pair[block, HALF:, :] * factor).astype(BF16))
            upper = own_lanes(mm(jnp.concatenate(upper, axis=0), stepped[:HALF]), per_group, head_size)
            lower = own_lanes(mm(jnp.concatenate(lower, axis=0), stepped), per_group, head_size)
            r.mixed[rows, columns] = (
                jnp.concatenate([upper, lower], axis=0) + r.skip[0:1, columns] * x_here
            )

        pl.when(me == block + 1)(chain)

    if layer + 1 == cfg.layers:
        for copy in turned:
            copy.start()
    weights.wait("wz", layer)
    clear("gate")

    @pl.loop(0, groups)
    def _(group):
        columns = lanes_of(group, GROUP)
        r.gate[:, columns] = mm(r.nx[pl.ds(PAD, tokens), :], r.wz[:, columns])

    weights.done("wz")
    store("gate")
    pl.when(me > n_blocks)(chain)
    store("states")
    r.squares[...] = jnp.zeros_like(r.squares)
    @pl.loop(0, n_blocks)
    def _(block):
        rows = lanes_of(block, SCAN_BLOCK)

        @pl.loop(0, groups)
        def _(group):
            columns = lanes_of(group, GROUP)
            grown = mm(r.grow_two[block], r.spread[:, columns])
            total = r.mixed[rows, columns] + grown * mm(
                r.bc[rows, state:], r.states[block, :, columns].astype(BF16)
            )
            r.mixed[rows, columns] = total
            gate_in = r.gate[rows, columns]
            gated = total * gate_in * sigmoid(gate_in)
            r.gm[rows, columns] = gated
            squared = gated * gated
            for lane in range(0, GROUP, LANES):
                r.squares[rows, :] += squared[:, lane : lane + LANES]

        pl.when(block == 0)(weights.tick)

    store("mixed")
    clear("rms")
    r.rms[...] = jnp.broadcast_to(
        lax.rsqrt(jnp.sum(r.squares[...], axis=-1, keepdims=True) / inner + EPS), r.rms.shape
    )
    store("rms")

    @pl.loop(0, groups)
    def _(group):
        columns = lanes_of(group, GROUP)
        for start in range(0, tokens, ROWS):
            rows = pl.ds(start, ROWS)
            r.go[rows, columns] = (
                r.gm[rows, columns] * r.rms[rows, 0:1] * r.gated_gain[layer : layer + 1, columns]
            ).astype(BF16)

    weights.wait("wo", layer)

    @pl.loop(0, width // GROUP)
    def _(step):
        columns = lanes_of(step, GROUP)
        branch = mm(r.go[...], r.wo[columns, :], NT)
        value = (h[:, columns].astype(F32) + branch) * r.live[:, 0:1]
        h_next[:, columns] = value
        if layer + 1 == cfg.layers:
            r.h_low[:, columns] = value.astype(BF16)

    weights.done("wo")
    if layer == 0:
        weights.tick()

    @pl.when(me < last)
    def _():
        halo_copy.wait_send()
        for copy in carry_copies:
            copy.wait_send()


def layers_forward(cfg, at, hidden_in, params, weights, blocks, turn):
    layers, inner, state = cfg.layers, cfg.inner, cfg.state
    width = hidden_in.shape[-1]
    tokens = cfg.tokens
    n_blocks = tokens // SCAN_BLOCK
    depth = at.n_dp // 2
    ins = dict(hidden_in=(hidden_in, VMEM if cfg.direct else ANY), **param_inputs(params))
    saved = dict(
        nx=vmem((PAD + tokens, width), BF16),
        gate=vmem((tokens, inner)),
        xraw=vmem((PAD + tokens, inner)),
        braw=vmem((PAD + tokens, 2 * state)),
        xc=vmem((tokens, inner), BF16),
        bc=vmem((tokens, 2 * state), BF16),
        dtp=vmem((tokens, LANES)),
        mixed=vmem((tokens, inner)),
        states=vmem((n_blocks + 1, state, inner)),
        rms=vmem((tokens, LANES)),
    )
    outs = dict(h_low=(shaped((tokens, width), BF16), VMEM))
    scratch = common_scratch(
        param_shapes(params), width, inner, state, n_blocks, tokens, at.n_tensor, depth
    )
    carry = (layers, inner // GROUP, state, GROUP)
    scratch.update(saved)
    scratch.update(
        dealt=vmem((tokens, width), BF16),
        deal_own=DMA,
        wz=vmem((width, inner), BF16),
        wx=vmem((width, inner), BF16),
        wo=vmem((width, inner), BF16),
        wn=vmem((width, at.n_tensor * LANES), BF16),
        weight_sem=DMA((4 * layers, at.n_dp)),
        halo_send=DMA((layers,)),
        halo_recv=DMA((layers,)),
        carry_out=vmem(carry, BF16),
        carry_in=vmem(carry, BF16),
        carry_send=DMA(carry[:2]),
        carry_recv=DMA(carry[:2]),
        b_t=vmem((n_blocks, state, SCAN_BLOCK), BF16),
        gm=vmem((tokens, inner)),
        go=vmem((tokens, inner), BF16),
        squares=vmem((tokens, LANES)),
    )
    for layer in range(layers):
        scratch[f"halo{layer}"] = vmem((PAD, width), F32 if layer else BF16)
        outs[f"h{layer + 1}"] = (shaped((tokens, width)), VMEM)
        for name in SAVED + TERMS:
            kind = scratch[name]
            outs[f"{name}{layer}_out"] = (shaped(kind.shape, kind.dtype), ANY)
    scratch["collect"] = vmem((inner, LANES), BF16)
    for name in CONSTANTS:
        outs[name + "_out"] = (shaped(scratch[name].shape, BF16), ANY)
    if cfg.direct:
        total = 0
        piece = tokens // at.n_dp
        for name, block in blocks.items():
            ins["block_" + name] = (block, VMEM)
            total += layers * (block.shape[2] // LANES)
            whole = (depth, 2, block.shape[1], at.n_tensor * block.shape[2])
            for layer in range(layers):
                outs[f"whole_{name}{layer}"] = (shaped(whole, BF16), ANY)
        ins["turn_in"] = (turn, VMEM)
        outs["turned"] = (shaped(turn.shape, BF16), ANY)
        outs["hidden"] = (shaped((tokens, width), BF16), ANY)
        scratch.update(turn_sems(at))
        scratch.update(gather_sems(total, depth))
        scratch.update(
            arranged=vmem((at.n_dp, piece, width), BF16),
            deal_send=DMA((at.n_dp,)),
            deal_recv=DMA((at.parts, at.n_tensor)),
            hidden_sem=DMA,
        )
    else:
        for layer in range(layers):
            for name in blocks:
                ins[f"{name}{layer}_in"] = (weights[layer][name], ANY)
    return call_kernel(partial(forward_body, cfg), "layers_forward", 1, ins, outs, scratch)


def turn_sems(at):
    shape = (at.n_tensor - 1, at.parts)
    return dict(turn_send=DMA(shape), turn_recv=DMA(shape), turn_own=DMA((at.parts,)))


def turn_copies(at, r, to_pieces):
    copies = []
    for offset in range(at.n_tensor):
        other = lax.rem(at.tensor + offset, at.n_tensor)
        for k in range(at.parts):
            if to_pieces:
                mine = r.turn_in.at[k * at.n_tensor + other]
                theirs = r.turned.at[at.tensor * at.parts + k]
            else:
                mine = r.turn_in.at[other * at.parts + k]
                theirs = r.turned.at[k * at.n_tensor + at.tensor]
            if offset == 0:
                copies.append(pltpu.make_async_copy(mine, theirs, r.turn_own.at[k]))
            else:
                copies.append(
                    remote(
                        mine,
                        theirs,
                        r.turn_send.at[offset - 1, k],
                        r.turn_recv.at[offset - 1, k],
                        {TENSOR: other},
                    )
                )
    return copies


def backward_body(cfg, r):
    at = place()
    me, last = at.tensor, at.n_tensor - 1
    layer, direct = cfg.layer, cfg.direct
    tokens, width = r.h.shape
    inner, state, head_size = cfg.inner, cfg.state, cfg.head_size
    n_blocks = tokens // SCAN_BLOCK
    groups = inner // GROUP
    per_group = GROUP // head_size
    previous = {TENSOR: lax.rem(me + last, at.n_tensor)}

    def load(name, target, index):
        copy = pltpu.make_async_copy(getattr(r, name + "_in"), target, r.load_sem.at[index])
        copy.start()
        return copy

    next_load = load("h_next", r.gn, 10)
    loads = {
        name: load(name, getattr(r, name), index) for index, name in enumerate(("nx", "rms", "dtp", "bc"))
    }
    for index, name in enumerate(CONSTANTS + TERMS):
        loads[name] = load(name, getattr(r, name), 24 + index)
    small_loads = param_loads(r)

    def stream(group, slot):
        columns = lanes_of(group, GROUP)
        return [
            pltpu.make_async_copy(r.gate_in.at[:, columns], r.gate.at[slot], r.stream_sem.at[0, slot]),
            pltpu.make_async_copy(r.mixed_in.at[:, columns], r.mixed.at[slot], r.stream_sem.at[1, slot]),
        ]

    count = 0
    if direct:
        greet_all(grid_partners(at))
        count = len(grid_partners(at))
        if cfg.closing:
            greet_all(corner_partners(at))
            count = count + len(corner_partners(at))
    greet_all(tensor_partners(at))
    count = count + len(tensor_partners(at))

    earlier, own = Rounds(), Rounds()
    unit_indices = []

    def enqueue(queue, source, full, put):
        for start in range(0, full, LANES):
            index = len(unit_indices)
            unit_indices.append(index)
            queue.add(reduce_unit(at, r, index, source, start, full, partial(put, start)))

    side = []

    def tick():
        earlier.tick()
        own.tick()
        if side:
            side.pop(0)()

    def put_wide(target):
        def put(start, value):
            target[:, start : start + LANES] = value

        return put

    def put_narrow(target):
        def put(start, value):
            target[...] = value

        return put

    turned = []
    if direct:
        if cfg.more:
            enqueue(earlier, r.g_wx, r.sum_wx.shape[1], put_wide(r.sum_wx))
            enqueue(earlier, r.g_narrow, LANES, put_narrow(r.sum_narrow))
            prior_loads = [load("prior_wx", r.g_wx, 11), load("prior_narrow", r.g_narrow, 12)]
        if cfg.turn:
            turned = turn_copies(at, r, True)

    fill_live(r, at)
    for copy in small_loads:
        copy.wait()
    fill_heads(r)
    for name in CONSTANTS:
        loads[name].wait()
    spread_skip(r, layer)
    loads["nx"].wait()
    loads["rms"].wait()
    next_load.wait()

    @pl.loop(0, tokens // ROWS)
    def _(step):
        rows = rows_of(step, ROWS)
        alive = r.live[rows, 0:1]
        low = (r.gh[rows, :].astype(F32) * alive).astype(BF16)
        r.g_branch[rows, :] = low
        columns = lanes_of(step, ROWS)
        r.g_branch_t[:, columns] = low.T
        r.normed_t[:, columns] = r.nx[rows_of(step, ROWS, PAD), :].T
        branch = r.gn[rows, :] - r.h[rows, :].astype(F32)
        scale = r.rms[rows, 0:1]
        along = jnp.sum(low.astype(F32) * branch, axis=-1, keepdims=True) * (scale * scale / inner)
        r.along[rows, :] = jnp.broadcast_to(along, (ROWS, LANES))

    loads.update(
        {
            name: load(name, getattr(r, name), 4 + index)
            for index, name in enumerate(("wo", "xc", "states", "braw", "wz"))
        }
    )
    for copy in stream(0, 0):
        copy.start()
    met(count)
    if direct and cfg.more:
        for copy in prior_loads:
            copy.wait()
        earlier.start()
    if cfg.closing:
        for other in range(layer + 1, cfg.layers):
            r.packed[other] = getattr(r, f"small{other}")[...]
            side.extend(small_steps(at, r, other))
    for copy in turned:
        copy.start()
    loads["dtp"].wait()
    for name in TERMS:
        loads[name].wait()
    tick()

    loads["bc"].wait()
    row_id = lax.broadcasted_iota(jnp.int32, (SCAN_BLOCK, SCAN_BLOCK), 0)
    col_id = lax.broadcasted_iota(jnp.int32, (SCAN_BLOCK, SCAN_BLOCK), 1)
    for block in range(n_blocks):
        rows = pl.ds(block * SCAN_BLOCK, SCAN_BLOCK)
        scores = mm(r.bc[rows, :state], r.bc[rows, state:], NT)
        r.pair[block] = jnp.where(row_id <= col_id, scores, 0.0)
        r.c_t[block] = r.bc[rows, state:].astype(F32).T.astype(BF16)
    r.g_run[...] = jnp.zeros_like(r.g_run)
    r.g_heads[...] = jnp.zeros_like(r.g_heads)
    places = small_rows(width, inner, state)

    def put_small(name, row, tile, values):
        for lane in range(0, values.shape[1], LANES):
            r.g_small[pl.ds(name + row + tile + lane // LANES, 1), :] = values[
                :, lane : lane + LANES
            ]

    def put_rows(target, columns, values):
        values = values.astype(BF16)
        if direct:
            target[:, :, :, columns] = values.reshape(target.shape[:3] + values.shape[1:])
        else:
            target[:, columns] = values

    def collected(values, columns):
        rows = values.shape[0]
        both = mm(jnp.concatenate(halves(values), axis=0), r.collect[columns, :])
        return both[:rows] + both[rows:]

    loads["wo"].wait()
    loads["xc"].wait()

    def gate_group(group):
        slot = lax.rem(group, 2)
        columns = lanes_of(group, GROUP)
        for copy in stream(group, slot):
            copy.wait()

        @pl.when(group + 1 < groups)
        def _():
            for copy in stream(group + 1, 1 - slot):
                copy.start()

        gain = r.gated_gain[layer : layer + 1, columns]
        skipped = r.skip[0:1, columns]
        gained = jnp.zeros((1, GROUP), F32)
        skip_sum = jnp.zeros((1, GROUP), F32)
        r.gq[pl.ds(0, tokens), columns] = mm(r.g_branch[...], r.wo[:, columns])
        for start in range(0, tokens, ROWS):
            rows = pl.ds(start, ROWS)
            gate_in = r.gate[slot, rows, :]
            here = r.mixed[slot, rows, :]
            x_here = r.xc[rows, columns].astype(F32)
            scale = r.rms[rows, 0:1]
            sig = sigmoid(gate_in)
            act = gate_in * sig
            gated = here * act
            scaled = gated * scale
            r.go[rows, :] = (scaled * gain).astype(BF16)
            g_gated = r.gq[rows, columns]
            gained = gained + jnp.sum(g_gated * scaled, axis=0, keepdims=True)
            g_mix = scale * gain * g_gated - gated * r.along[rows, 0:1]
            g_out = g_mix * act
            r.gq[rows, columns] = g_out
            r.pz[rows, columns] = (g_mix * here * sig * (1.0 + gate_in * (1.0 - sig))).astype(BF16)
            skip_sum = skip_sum + jnp.sum(g_out * x_here, axis=0, keepdims=True)
            r.g_run[rows, :] += collected(g_out * (here - skipped * x_here), columns)
        pl.when(group == groups // 2 - 1)(tick)
        put_small(places.gate_gain, 0, group * (GROUP // LANES), gained)
        r.g_heads[2:3, :] += collected(jnp.broadcast_to(skip_sum, (8, GROUP)), columns)[0:1, :]
        put_rows(r.g_wo, columns, mm(r.g_branch_t[...], r.go[...]))
        put_rows(r.g_wz, columns, mm(r.normed_t[...], r.pz[:, columns]))
        for block in range(n_blocks):
            rows = pl.ds(block * SCAN_BLOCK, SCAN_BLOCK)
            grown = mm(r.grow_two[block], r.spread[:, columns])
            r.d_states[block, :, columns] = mm(
                r.c_t[block], (r.gq[rows, columns] * grown).astype(BF16)
            )

    pl.loop(0, groups)(gate_group)
    tick()
    wx_load = load("wx", r.wo, 13)

    if direct:
        for source, target in ((r.g_wo, r.sum_wo), (r.g_wz, r.sum_wz)):
            enqueue(own, source, target.shape[1], put_wide(target))
        own.start()

    carry_copies = [
        remote(
            r.carry_out.at[group],
            r.carry_in.at[group],
            r.carry_send.at[group],
            r.carry_recv.at[group],
            previous,
        )
        for group in range(groups)
    ]

    def chain():
        for group in range(groups):
            columns = pl.ds(group * GROUP, GROUP)

            @pl.when(me < last)
            def _():
                carry_copies[group].wait_recv()
                r.d_states[n_blocks, :, columns] = r.carry_in[group].astype(F32)

            @pl.when(me == last)
            def _():
                r.d_states[n_blocks, :, columns] = jnp.zeros((state, GROUP), F32)

            for block in reversed(range(n_blocks)):
                r.d_states[block, :, columns] += (
                    r.d_states[block + 1, :, columns] * r.decay[block, 0:1, columns]
                )
            r.carry_out[group] = r.d_states[0, :, columns].astype(BF16)

            @pl.when(me > 0)
            def _():
                carry_copies[group].start()

    pl.when(me == last)(chain)
    loads["states"].wait()
    r.gb[pl.ds(0, tokens), state:] = jnp.zeros((tokens, state), F32)
    for block in range(n_blocks):
        if block:
            tick()
        rows = pl.ds(block * SCAN_BLOCK, SCAN_BLOCK)
        r.g_pair[...] = jnp.zeros_like(r.g_pair)

        @pl.loop(0, groups)
        def _(group):
            columns = lanes_of(group, GROUP)
            sizes = mm(r.step_two[block], r.spread[:, columns])
            grown = mm(r.grow_two[block], r.spread[:, columns])
            stepped = (r.xc[rows, columns].astype(F32) * sizes).astype(BF16)
            g_out = r.gq[rows, columns]
            g_low = g_out.astype(BF16)
            rolled = columns_of(r, block, group, per_group)
            r.gb[rows, state:] += mm(
                (g_out * grown).astype(BF16), r.states[block, :, columns].astype(BF16), NT
            )
            upper, lower, up_factors, low_factors = [], [], [], []
            for head in range(per_group):
                along = r.run_t[block, pl.ds(per_group * group + head, 1), :]
                down = rolled[:, head : head + 1]
                up_factors.append(jnp.exp2(jnp.minimum(along - down[:HALF], 0.0)))
                upper.append((r.pair[block, :HALF, :] * up_factors[head]).astype(BF16))
                low_factors.append(jnp.exp2(jnp.minimum(along[:, HALF:] - down[HALF:], 0.0)))
                lower.append((r.pair[block, HALF:, HALF:] * low_factors[head]).astype(BF16))
            upper = own_lanes(mm(jnp.concatenate(upper, axis=0), g_low), per_group, head_size)
            lower = own_lanes(mm(jnp.concatenate(lower, axis=0), g_low[HALF:]), per_group, head_size)
            ones = [stepped * head_row(head, head_size) for head in range(per_group)]
            up_pairs = mm(jnp.concatenate([one[:HALF] for one in ones], axis=0), g_low, NT)
            low_pairs = mm(jnp.concatenate([one[HALF:] for one in ones], axis=0), g_low[HALF:], NT)
            pair_upper = up_pairs[:HALF] * up_factors[0]
            pair_lower = low_pairs[:HALF] * low_factors[0]
            for head in range(1, per_group):
                span = slice(head * HALF, (head + 1) * HALF)
                pair_upper = pair_upper + up_pairs[span] * up_factors[head]
                pair_lower = pair_lower + low_pairs[span] * low_factors[head]
            r.gx[rows, columns] = jnp.concatenate([upper, lower], axis=0)
            r.g_pair[:HALF, :] += pair_upper
            r.g_pair[HALF:, HALF:] += pair_lower

        g_scores = jnp.where(row_id <= col_id, r.g_pair[...], 0.0)
        r.gb[rows, :state] = mm(g_scores.astype(BF16), r.bc[rows, state:])
        r.gb[rows, state:] += mm(g_scores.T.astype(BF16), r.bc[rows, :state])
        if block < n_blocks - 1:
            pl.when(me == last - 1)(chain)

    pl.when(me < (last - 1 if n_blocks > 1 else last))(chain)
    r.direct[...] = jnp.zeros_like(r.direct)
    for block in reversed(range(n_blocks)):
        if block == n_blocks - 1:
            tick()
        rows = pl.ds(block * SCAN_BLOCK, SCAN_BLOCK)

        @pl.loop(0, groups)
        def _(group):
            columns = lanes_of(group, GROUP)
            sizes = mm(r.step_two[block], r.spread[:, columns])
            keeps = mm(r.keep_two[block], r.spread[:, columns])
            x_here = r.xc[rows, columns].astype(F32)
            stepped = x_here * sizes
            d_here = r.d_states[block + 1, :, columns].astype(BF16)
            d_x = r.gx[rows, columns] + keeps * mm(r.bc[rows, :state], d_here)
            r.gb[rows, :state] += mm((stepped * keeps).astype(BF16), d_here, NT)
            sums = collected(
                jnp.concatenate([d_x * x_here, d_x * stepped.astype(BF16).astype(F32)], axis=0), columns
            )
            r.direct[rows, :] += sums[:SCAN_BLOCK]
            r.g_run[rows, :] -= sums[SCAN_BLOCK:]
            r.gx[rows, columns] = sizes * d_x + r.skip[0:1, columns] * r.gq[rows, columns]

    raw_load = load("xraw", r.gq, 14)
    for block in range(n_blocks):
        rows = pl.ds(block * SCAN_BLOCK, SCAN_BLOCK)
        end_sum = jnp.broadcast_to(
            jnp.sum(r.d_states[block + 1] * r.states[block + 1], axis=0, keepdims=True), (8, inner)
        )
        at_end = collected(end_sum, slice(None))[0:1, :]
        rate = r.heads[layer, 1:2, :]
        g_rate = exact((row_id <= col_id).astype(F32), r.g_run[rows, :]) + at_end
        g_dt = (rate * g_rate + r.direct[rows, :]) * r.live[rows, :] * sigmoid(r.dtp[rows, :])
        r.pd[rows, :] = g_dt.astype(BF16)
        r.g_heads[0:1, :] += jnp.sum(g_dt, axis=0, keepdims=True)
        r.g_heads[1:2, :] += jnp.sum(g_rate * r.dt[block], axis=0, keepdims=True) * rate
    tick()

    def before_conv(taps, raw, grad, columns):
        for start in range(0, tokens, ROWS):
            rows = pl.ds(start, ROWS)
            before = conv_rows(raw, taps, start, columns)
            sig = sigmoid(before)
            grad[rows, columns] = grad[rows, columns] * (sig * (1.0 + before * (1.0 - sig)))

    def through_conv(taps, raw, grad, columns, name, tile, low):
        sums = [jnp.zeros((1, GROUP), F32) for tap in range(WIDTH + 1)]
        for start in range(0, tokens, ROWS):
            total = jnp.zeros((ROWS, GROUP), F32)
            here = grad[pl.ds(start, ROWS), columns]
            for tap in range(WIDTH):
                shift = WIDTH - 1 - tap
                total = total + taps(tap, columns) * grad[pl.ds(start + shift, ROWS), columns]
                sums[tap] = sums[tap] + jnp.sum(
                    here * raw[pl.ds(PAD - shift + start, ROWS), columns], axis=0, keepdims=True
                )
            sums[WIDTH] = sums[WIDTH] + jnp.sum(here, axis=0, keepdims=True)
            low[pl.ds(start, ROWS), columns] = total.astype(BF16)
        for tap in range(WIDTH + 1):
            put_small(name, tap * (grad.shape[1] // LANES), tile, sums[tap])

    earlier.drain()
    wn_load = load("wn", r.g_narrow, 15)
    loads["braw"].wait()
    for step in range(2 * state // GROUP):
        before_conv(taps_of(r.conv_bc, layer), r.braw, r.gb, pl.ds(step * GROUP, GROUP))
    raw_load.wait()

    @pl.loop(0, groups)
    def _(step):
        before_conv(taps_of(r.conv_x, layer), r.gq, r.gx, lanes_of(step, GROUP))

    halo_copies = [
        remote(
            buffer.at[pl.ds(0, PAD), :],
            buffer.at[pl.ds(tokens, PAD), :],
            r.halo_send.at[index],
            r.halo_recv.at[index],
            previous,
        )
        for index, buffer in enumerate((r.gx, r.gb))
    ]

    @pl.when(me > 0)
    def _():
        for copy in halo_copies:
            copy.start()

    wn_load.wait()
    split_narrow(r, r.g_narrow)
    put_rows(r.g_narrow, pl.ds(2 * state, LANES), mm(r.normed_t[...], r.pd[...]))
    put_rows(r.g_narrow, pl.ds(2 * state + LANES, LANES), jnp.zeros((width, LANES), F32))
    loads["wz"].wait()
    r.g_gain[...] = jnp.zeros_like(r.g_gain)

    @pl.loop(0, width // GROUP)
    def _(step):
        columns = lanes_of(step, GROUP)
        r.gn[:, columns] = mm(r.pz[...], r.wz[columns, :], NT) + mm(r.pd[...], r.wdt[columns, :], NT)

    tick()

    @pl.when(me < last)
    def _():
        for copy in halo_copies:
            copy.wait_recv()

    @pl.when(me == last)
    def _():
        for buffer in (r.gx, r.gb):
            buffer[pl.ds(tokens, PAD), :] = jnp.zeros((PAD, buffer.shape[1]), F32)

    for step in range(2 * state // GROUP):
        columns = pl.ds(step * GROUP, GROUP)
        through_conv(
            taps_of(r.conv_bc, layer), r.braw, r.gb, columns, places.tap_b, step * (GROUP // LANES), r.pb
        )
        put_rows(r.g_narrow, columns, mm(r.normed_t[...], r.pb[:, columns]))
    stores = []

    def store(source, target):
        copy = pltpu.make_async_copy(source, target, r.store_sem.at[len(stores)])
        copy.start()
        stores.append(copy)

    final = Rounds()
    if cfg.closing:
        enqueue(final, r.g_wx, r.close_wx.shape[1], put_wide(r.close_wx))
        enqueue(final, r.g_narrow, LANES, put_narrow(r.close_narrow))
    else:
        store(r.g_narrow, r.g_narrow_out)

    for first in range(0, groups, groups // 2):

        @pl.loop(first, first + groups // 2)
        def _(step):
            columns = lanes_of(step, GROUP)
            through_conv(
                taps_of(r.conv_x, layer), r.gq, r.gx, columns, places.tap_x, step * (GROUP // LANES), r.px
            )
            put_rows(r.g_wx, columns, mm(r.normed_t[...], r.px[:, columns]))

        tick()

    own.drain()
    while side:
        side.pop(0)()
    if cfg.closing:
        final.start()
    else:
        store(r.g_wx, r.g_wx_out)
    wx_load.wait()

    @pl.loop(0, width // GROUP)
    def _(step):
        columns = lanes_of(step, GROUP)
        r.gn[:, columns] += mm(r.px[...], r.wo[columns, :], NT) + mm(r.pb[...], r.wbc[columns, :], NT)

    final.tick()
    r.g_small[pl.ds(places.heads, 8), :] = r.g_heads[...]
    r.g_small[pl.ds(places.gain, 8), :] = jnp.zeros((8, LANES), F32)
    gain = r.in_gain[layer : layer + 1, :]

    @pl.loop(0, tokens // ROWS)
    def _(step):
        rows = rows_of(step, ROWS)
        values = r.h[rows, :].astype(F32)
        inv = lax.rsqrt(jnp.mean(values * values, axis=-1, keepdims=True) + EPS)
        g_normed = r.gn[rows, :]
        r.g_gain[0:1, :] += jnp.sum(g_normed * values * inv, axis=0, keepdims=True)
        scaled = g_normed * gain
        along_h = jnp.mean(scaled * values, axis=-1, keepdims=True)
        r.gh_next[rows, :] = (
            r.gh[rows, :].astype(F32) * r.live[rows, 0:1]
            + inv * scaled
            - values * (inv * inv * inv * along_h)
        ).astype(r.gh_next.dtype)

    put_small(places.gain, 0, 0, r.g_gain[0:1, :])
    if cfg.closing:
        close(cfg, at, r, final)
    for copy in turned:
        copy.wait()
    if not direct:
        store(r.g_wo, r.g_wo_out)
        store(r.g_wz, r.g_wz_out)
    for copy in stores:
        copy.wait()

    @pl.when(me > 0)
    def _():
        for copy in halo_copies + carry_copies:
            copy.wait_send()


def corner_partners(at):
    return [
        {DP: at.dp + 1 - 2 * at.y, TENSOR: lax.rem(at.tensor + k, at.n_tensor)}
        for k in range(1, at.n_tensor)
    ]


def small_steps(at, r, layer):
    depth = at.depth
    quarter = r.packed.shape[1] // depth
    send, recv = r.small_send, r.small_recv

    def part(index):
        return pl.ds(pl.multiple_of(index * quarter, 8), quarter)

    def hop(index, source, target, device):
        return remote(source, target, send.at[layer, index], recv.at[layer, index], device)

    hops = [
        hop(0, r.packed.at[layer], r.small_core.at[layer], over_core(at)),
        hop(1, r.sum_core.at[layer], r.small_x.at[layer], over_x(at)),
        hop(2, r.sum_x.at[layer], r.small_y.at[layer], over_y(at)),
    ]
    scatter = [
        hop(
            2 + k,
            r.sum_y.at[layer, part(lax.rem(at.z + k, depth))],
            r.small_z.at[layer, k - 1],
            over_z(at, k),
        )
        for k in range(1, depth)
    ]
    total = r.small_sum.at[layer, part(at.z)]
    gather = [hop(1 + depth + k, total, total, over_z(at, k)) for k in range(1, depth)]

    def begin():
        hops[0].start()

    def add(index, own, other, result):
        def step():
            hops[index].wait_recv()
            result[layer] = own[layer] + other[layer]
            for copy in [hops[index + 1]] if index < 2 else scatter:
                copy.start()

        return step

    def turn():
        value = r.sum_y[layer, part(at.z)]
        for k, copy in enumerate(scatter):
            copy.wait_recv()
            value = value + r.small_z[layer, k]
        r.small_sum[layer, part(at.z)] = value
        for copy in gather:
            copy.start()

    def end():
        for copy in gather:
            copy.wait_recv()
        for copy in hops + scatter + gather:
            copy.wait_send()

    return [
        begin,
        add(0, r.packed, r.small_core, r.sum_core),
        add(1, r.sum_core, r.small_x, r.sum_x),
        add(2, r.sum_x, r.small_y, r.sum_y),
        turn,
        end,
    ]


def close(cfg, at, r, final):
    piece = r.returned.shape[1]
    middle = r.input_grad
    r.packed[cfg.layer] = r.g_small[...]
    smalls = small_steps(at, r, cfg.layer)
    mine = 2 * at.tensor + at.y

    def run(k, other):
        return r.gh_next.at[pl.ds(pl.multiple_of((k * at.n_tensor + other) * piece, PAD), piece), :]

    stay = pltpu.make_async_copy(run(at.y, at.tensor), middle.at[mine], r.back_own.at[0])
    stay.start()
    out = []
    for k in range(2):
        for offset in range(at.n_tensor):
            other = lax.rem(at.tensor + offset, at.n_tensor)
            copy = remote(
                run(k, other),
                middle.at[mine],
                r.back_send.at[k, offset],
                r.back_recv.at[mine],
                {DP: at.z * 2 + k, TENSOR: other},
            )
            out.append((copy, at.y != k if offset == 0 else at.y >= 0))
    for copy, away in out:
        pl.when(away)(copy.start)
    smalls[0]()
    final.tick()
    smalls[1]()

    stay.wait()
    keep = pltpu.make_async_copy(
        middle.at[pl.ds(2 * at.z, 2)], r.returned.at[pl.ds(2 * at.z, 2)], r.back_own.at[1]
    )
    through = []
    for owner in range(at.n_tensor):
        for slot in (2 * owner, 2 * owner + 1):
            arrival = remote(
                run(0, 0), middle.at[slot], r.back_send.at[0, 0], r.back_recv.at[slot], over_core(at)
            )
            pl.when(mine != slot)(arrival.wait_recv)
        copy = remote(
            middle.at[pl.ds(2 * owner, 2)],
            r.returned.at[pl.ds(2 * at.z, 2)],
            r.through_send.at[owner],
            r.through_recv.at[at.z],
            {DP: owner * 2 + at.y},
        )
        through.append(copy)
        pl.when(at.z != owner)(copy.start)
    keep.start()
    final.tick()
    smalls[2]()
    final.tick()
    smalls[3]()
    final.finish(len(final.units) - 1)

    r.narrow[cfg.layer, at.tensor] = r.close_narrow[...]
    for layer in range(cfg.layer + 1, cfg.layers):
        source = r.sum_narrow if layer == cfg.layer + 1 else getattr(r, f"narrow{layer}")
        r.narrow[layer, at.tensor] = source[...]
    spread = [
        remote(
            r.narrow.at[:, at.tensor],
            r.narrow.at[:, at.tensor],
            r.narrow_send.at[k - 1],
            r.narrow_recv.at[k - 1],
            {TENSOR: lax.rem(at.tensor + k, at.n_tensor)},
        )
        for k in range(1, at.n_tensor)
    ]
    for copy in spread:
        copy.start()
    smalls[4]()
    final.drain()

    keep.wait()
    for owner in range(at.n_tensor):
        arrival = remote(
            middle.at[pl.ds(0, 2)],
            r.returned.at[pl.ds(2 * owner, 2)],
            r.through_send.at[owner],
            r.through_recv.at[owner],
            over_core(at),
        )
        pl.when(at.z != owner)(arrival.wait_recv)
        pl.when(at.z != owner)(through[owner].wait_send)
    for copy, away in out:
        pl.when(away)(copy.wait_send)
    for index in range(at.n_dp):
        source = jnp.int32(0)
        for j in range(1, at.n_dp):
            source = jnp.where(r.order[j] == index, j, source)
        r.input_grad[index] = r.returned[source]
    smalls[5]()
    for copy in spread:
        copy.wait()


def layer_backward(cfg, at, gh, h, h_next, params, saved, weights, prior, turn, others):
    tokens, width = h.shape
    inner, state = cfg.inner, cfg.state
    n_blocks = tokens // SCAN_BLOCK
    depth, rows = at.n_dp // 2, width // at.n_dp
    part = inner // at.n_tensor
    piece = tokens // at.n_dp
    narrow = at.n_tensor * LANES
    small_shape = (small_rows(width, inner, state).all, LANES)

    def blocked(columns):
        return (depth, 2, rows, columns) if cfg.direct else (width, columns)

    ins = dict(gh=(gh, VMEM), h=(h, VMEM), h_next_in=(h_next, ANY), **param_inputs(params))
    for name in SAVED + TERMS + CONSTANTS:
        ins[name + "_in"] = (saved[name], ANY)
    for name in ("wz", "wx", "wo"):
        ins[name + "_in"] = (weights[name], ANY)
    ins["wn_in"] = (weights["wn"].reshape(blocked(narrow)), ANY)
    outs = {}
    scratch = common_scratch(
        param_shapes(params), width, inner, state, n_blocks, tokens, at.n_tensor, depth
    )
    scratch.update(
        carry_out=vmem((inner // GROUP, state, GROUP), BF16),
        carry_in=vmem((inner // GROUP, state, GROUP), BF16),
        carry_send=DMA((inner // GROUP,)),
        carry_recv=DMA((inner // GROUP,)),
        nx=vmem((PAD + tokens, width), BF16),
        wz=vmem((width, inner), BF16),
        wo=vmem((width, inner), BF16),
        collect=vmem((inner, LANES), BF16),
        gate=vmem((2, tokens, GROUP)),
        mixed=vmem((2, tokens, GROUP)),
        stream_sem=DMA((2, 2)),
        braw=vmem((PAD + tokens, 2 * state)),
        g_branch=vmem((tokens, width), BF16),
        g_branch_t=vmem((width, tokens), BF16),
        normed_t=vmem((width, tokens), BF16),
        along=vmem((tokens, LANES)),
        c_t=vmem((n_blocks, state, SCAN_BLOCK), BF16),
        g_run=vmem((tokens, LANES)),
        direct=vmem((tokens, LANES)),
        g_heads=vmem((8, LANES)),
        g_gain=vmem((8, width)),
        go=vmem((tokens, GROUP), BF16),
        gq=vmem((PAD + tokens, inner)),
        gx=vmem((tokens + PAD, inner)),
        gb=vmem((tokens + PAD, 2 * state)),
        pz=vmem((tokens, inner), BF16),
        px=vmem((tokens, inner), BF16),
        pb=vmem((tokens, 2 * state), BF16),
        pd=vmem((tokens, LANES), BF16),
        d_states=vmem((n_blocks + 1, state, inner)),
        g_pair=vmem((SCAN_BLOCK, SCAN_BLOCK)),
        gn=vmem((tokens, width)),
        g_wo=vmem(blocked(inner), BF16),
        g_wz=vmem(blocked(inner), BF16),
        g_wx=vmem(blocked(inner), BF16),
        g_narrow=vmem(blocked(narrow), BF16),
        halo_send=DMA((2,)),
        halo_recv=DMA((2,)),
    )
    small, wide = shaped(small_shape), shaped((rows, part))
    if cfg.closing:
        scratch.update(gh_next=vmem((tokens, width), BF16), g_small=vmem(small_shape))
    else:
        outs.update(
            gh_next=(shaped((tokens, width), F32 if cfg.layer else BF16), VMEM),
            g_small=(small, VMEM),
            g_wx_out=(shaped(blocked(inner), BF16), ANY),
            g_narrow_out=(shaped(blocked(narrow), BF16), ANY),
        )
    if cfg.direct:
        total = 2 * (part // LANES)
        outs.update(sum_wo=(wide, VMEM), sum_wz=(wide, VMEM))
        if cfg.more:
            total += part // LANES + 1
            ins["prior_wx_in"] = (prior["g_wx_out"], ANY)
            ins["prior_narrow_in"] = (prior["g_narrow_out"], ANY)
            outs.update(sum_wx=(wide, VMEM), sum_narrow=(shaped((rows, LANES)), VMEM))
        if cfg.turn:
            ins["turn_in"] = (turn, VMEM)
            outs["turned"] = (shaped(turn.shape, BF16), ANY)
            scratch.update(turn_sems(at))
        if cfg.closing:
            total += part // LANES + 1
            packed = (cfg.layers,) + small_shape
            quarter = (small_shape[0] // depth, LANES)
            for layer in range(1, cfg.layers):
                ins[f"small{layer}"] = (others[layer]["small"], VMEM)
                if layer > 1:
                    ins[f"narrow{layer}"] = (others[layer]["narrow"], VMEM)
            outs.update(
                close_wx=(wide, VMEM),
                narrow=(shaped((cfg.layers, at.n_tensor, rows, LANES)), VMEM),
                small_sum=(shaped(packed), VMEM),
                input_grad=(shaped((at.n_dp, piece, width), BF16), VMEM),
            )
            scratch.update(
                close_narrow=vmem((rows, LANES)),
                returned=vmem((at.n_dp, piece, width), BF16),
                packed=vmem(packed),
                small_core=vmem(packed),
                through_send=DMA((depth,)),
                through_recv=DMA((depth,)),
                small_x=vmem(packed),
                small_y=vmem(packed),
                sum_core=vmem(packed),
                sum_x=vmem(packed),
                sum_y=vmem(packed),
                small_z=vmem((cfg.layers, depth - 1) + quarter),
                small_send=DMA((cfg.layers, 1 + 2 * depth)),
                small_recv=DMA((cfg.layers, 1 + 2 * depth)),
                back_send=DMA((at.parts, at.n_tensor)),
                back_recv=DMA((at.n_dp,)),
                back_own=DMA((2,)),
                narrow_send=DMA((at.n_tensor - 1,)),
                narrow_recv=DMA((at.n_tensor - 1,)),
            )
        scratch.update(reduce_scratch(total, depth, rows))
    else:
        outs.update(
            g_wo_out=(shaped((width, inner), BF16), ANY),
            g_wz_out=(shaped((width, inner), BF16), ANY),
        )
    return call_kernel(
        partial(backward_body, cfg), f"layer_{cfg.layer}_backward", 11 + cfg.layer, ins, outs, scratch
    )


def deal_sources(at):
    return [(at.tensor * at.parts + k, other) for k in range(at.parts) for other in range(at.n_tensor)]


def finish_body(cfg, r):
    tensor = lax.axis_index(TENSOR)
    places = small_rows(cfg.width, cfg.inner, cfg.state)
    own = cfg.heads // r.narrow.shape[1]
    row = lax.broadcasted_iota(jnp.int32, (own, LANES), 0)
    column = lax.broadcasted_iota(jnp.int32, (own, LANES), 1)
    pick = (row + tensor * own == column).astype(F32)
    r.out_block[...] = r.block[...]
    r.out_grad[...] = r.grad[...]

    def lay_out(target, layer, start, rows, tiles):
        for k in range(rows):
            for tile in range(tiles):
                value = r.small_sum[layer, pl.ds(start + k * tiles + tile, 1), :]
                columns = pl.ds(tile * LANES, LANES)
                if len(target.shape) == 3:
                    target[k, pl.ds(layer, 1), columns] = value
                else:
                    target[pl.ds(layer, 1), columns] = value

    for layer in range(cfg.layers):
        for name in ("wz", "wx", "wo"):
            getattr(r, "out_" + name)[layer] = getattr(r, f"{name}{layer}")[...]
        for side in range(2):
            r.out_bc[layer, :, side * LANES : (side + 1) * LANES] = r.narrow[layer, side]
        picked = lax.dot_general(
            pick, r.narrow[layer, 2], NT, precision=lax.Precision.HIGHEST, preferred_element_type=F32
        )
        for k in range(own):
            r.out_dt[k, pl.ds(layer, 1), :] = picked[k : k + 1, :]
        lay_out(r.out_gain, layer, places.gain, 1, cfg.width // LANES)
        lay_out(r.out_gate_gain, layer, places.gate_gain, 1, cfg.inner // LANES)
        lay_out(r.out_tap_x, layer, places.tap_x, WIDTH + 1, cfg.inner // LANES)
        lay_out(r.out_tap_b, layer, places.tap_b, WIDTH + 1, 2 * cfg.state // LANES)
        for index, target in enumerate((r.out_bias, r.out_alog, r.out_skip)):
            target[pl.ds(layer, 1), :] = r.small_sum[
                layer, pl.ds(places.heads + index, 1), : cfg.heads
            ]


def finish(cfg, block, grad, sums, narrow, small_sum):
    layers, tensor, rows, _ = narrow.shape
    part = cfg.inner // tensor
    ins = dict(
        block=(block, VMEM), grad=(grad, VMEM), narrow=(narrow, VMEM), small_sum=(small_sum, VMEM)
    )
    for layer in range(layers):
        for name in ("wz", "wx", "wo"):
            ins[f"{name}{layer}"] = (sums[layer][name], VMEM)
    wide = (shaped((layers, rows, part)), VMEM)
    per_head = (shaped((layers, cfg.heads)), VMEM)
    outs = dict(
        out_block=(shaped(block.shape, BF16), VMEM),
        out_grad=(shaped(grad.shape, BF16), VMEM),
        out_gain=(shaped((layers, cfg.width)), VMEM),
        out_wz=wide,
        out_wx=wide,
        out_bc=(shaped((layers, rows, 2 * cfg.state)), VMEM),
        out_dt=(shaped((cfg.heads // tensor, layers, rows)), VMEM),
        out_tap_x=(shaped((WIDTH + 1, layers, cfg.inner)), VMEM),
        out_tap_b=(shaped((WIDTH + 1, layers, 2 * cfg.state)), VMEM),
        out_bias=per_head,
        out_alog=per_head,
        out_skip=per_head,
        out_gate_gain=(shaped((layers, cfg.inner)), VMEM),
        out_wo=wide,
    )
    results = call_kernel(partial(finish_body, cfg), "finish", None, ins, outs, {})
    for name, order in (("out_dt", (1, 2, 0)), ("out_tap_x", (1, 0, 2)), ("out_tap_b", (1, 0, 2))):
        results[name] = results[name].transpose(order)
    return tuple(results.values())


def local(
    hidden_in,
    lengths,
    order,
    in_gain,
    w_z,
    w_x,
    w_bc,
    w_dt,
    conv_x,
    conv_bc,
    dt_bias,
    a_log,
    d_skip,
    gated_gain,
    w_out,
    cotangent,
):
    at = place()
    n_dp, n_tensor = at.n_dp, at.n_tensor
    piece = hidden_in.shape[2]
    width = hidden_in.shape[3]
    tokens = piece * n_dp
    layers = w_z.shape[0]
    inner = gated_gain.shape[1]
    heads = dt_bias.shape[1]
    state = conv_bc.shape[2] // 2
    rows_local = w_z.shape[1]
    part = w_z.shape[2]
    direct = rows_local % 16 == 0 and piece % 16 == 0 and n_tensor == 4 and n_dp == 2 * n_tensor

    quarter = 2 * state // n_tensor
    narrow = jnp.concatenate(
        [lax.dynamic_slice_in_dim(w_bc, at.tensor * quarter, quarter, 2), w_dt], axis=2
    )
    narrow = jnp.pad(narrow, ((0, 0), (0, 0), (0, LANES - narrow.shape[2])))
    blocks = dict(wz=w_z, wx=w_x, wn=narrow, wo=w_out)
    params = dict(
        lengths=lengths,
        order=order,
        in_gain=in_gain,
        conv_x=conv_x.transpose(1, 0, 2),
        conv_bc=conv_bc.transpose(1, 0, 2),
        dt_bias=dt_bias,
        a_log=a_log,
        d_skip=d_skip,
        gated_gain=gated_gain,
    )

    def to_run(values):
        swapped = lax.all_to_all(
            values.reshape(n_tensor, at.parts, piece, width), TENSOR, split_axis=0, concat_axis=0
        )
        return swapped.transpose(1, 0, 2, 3).reshape(tokens, width)

    def to_pieces(values):
        swapped = values.reshape(at.parts, n_tensor, piece, width).transpose(1, 0, 2, 3)
        return lax.all_to_all(swapped, TENSOR, split_axis=0, concat_axis=0).reshape(
            n_dp, piece, width
        )

    def config(layer):
        return SimpleNamespace(
            layer=layer,
            layers=layers,
            direct=direct,
            more=layer + 1 < layers,
            turn=layer + 1 == layers,
            closing=direct and layer == 0,
            tokens=tokens,
            width=width,
            inner=inner,
            state=state,
            heads=heads,
            head_size=inner // heads,
        )

    weights = [{} for layer in range(layers)]
    if direct:
        hidden = hidden_in[:, 0]
    else:
        arranged = jnp.take(hidden_in, order, axis=0)
        dealt = lax.all_to_all(arranged, DP, split_axis=0, concat_axis=1, tiled=True)
        hidden = to_run(dealt[0])

        def whole(stacked):
            gathered = lax.all_gather(stacked, DP, axis=1, tiled=True)
            return lax.all_gather(gathered, TENSOR, axis=2, tiled=True)

        for name, block in blocks.items():
            stacked = whole(block)
            for layer in range(layers):
                weights[layer][name] = stacked[layer]
    forward = layers_forward(config(0), at, hidden, params, weights, blocks, cotangent[0])
    if direct:
        hidden = forward["hidden"]
        for layer in range(layers):
            for name in blocks:
                weights[layer][name] = forward[f"whole_{name}{layer}"].reshape(width, -1)
        grad = forward["turned"].reshape(tokens, width)
    else:
        grad = to_run(cotangent[0])
    inputs = [hidden] + [forward[f"h{layer + 1}"] for layer in range(layers)]
    kept = [
        {name: forward[f"{name}{layer}_out"] for name in SAVED + TERMS} for layer in range(layers)
    ]
    for saved in kept:
        saved.update({name: forward[name + "_out"] for name in CONSTANTS})
    h_low = forward["h_low"]
    sums = [{} for layer in range(layers)]
    results = None
    for layer in reversed(range(layers)):
        results = layer_backward(
            config(layer),
            at,
            grad,
            inputs[layer],
            inputs[layer + 1],
            params,
            kept[layer],
            weights[layer],
            results,
            h_low.reshape(n_dp, piece, width),
            sums,
        )
        if direct:
            sums[layer].update(wo=results["sum_wo"], wz=results["sum_wz"])
            if layer + 1 < layers:
                sums[layer + 1].update(wx=results["sum_wx"], narrow=results["sum_narrow"])
            if layer + 1 == layers:
                block_out = results["turned"]
            if layer:
                grad, sums[layer]["small"] = results["gh_next"], results["g_small"]
        else:
            grad, sums[layer]["small"] = results["gh_next"], results["g_small"]
            for name in ("wo", "wz", "wx", "narrow"):
                sums[layer][name] = results[f"g_{name}_out"]

    if direct:
        sums[0]["wx"] = results["close_wx"]
        input_grad = results["input_grad"][:, None]
        narrow_sum, small_sum = results["narrow"], results["small_sum"]
    else:
        block_out = to_pieces(h_low)
        returned = lax.all_to_all(
            to_pieces(grad)[None], DP, split_axis=1, concat_axis=0, tiled=True
        )
        input_grad = jnp.zeros_like(returned).at[order].set(returned)

        def scattered(name):
            terms = jnp.stack([entry[name] for entry in sums]).astype(F32)
            mine = lax.psum_scatter(terms, DP, scatter_dimension=1, tiled=True)
            return lax.psum_scatter(mine, TENSOR, scatter_dimension=2, tiled=True)

        for name in ("wz", "wx", "wo"):
            total = scattered(name)
            for layer in range(layers):
                sums[layer][name] = total[layer]
        narrow_sum = lax.all_gather(scattered("narrow"), TENSOR, axis=1)
        small_sum = lax.psum(jnp.stack([entry["small"] for entry in sums]), (DP, TENSOR))
    return finish(config(0), block_out[None], input_grad, sums, narrow_sum, small_sum)


def solution(mesh):
    return jax.shard_map(
        local,
        mesh=mesh,
        in_specs=(
            P(None, DP, TENSOR, None),
            P(),
            P(),
            P(),
            P(None, DP, TENSOR),
            P(None, DP, TENSOR),
            P(None, DP, None),
            P(None, DP, TENSOR),
            P(),
            P(),
            P(),
            P(),
            P(),
            P(),
            P(None, DP, TENSOR),
            P(DP, None, TENSOR, None),
        ),
        out_specs=(
            P(DP, None, TENSOR, None),
            P(None, DP, TENSOR, None),
            P(),
            P(None, DP, TENSOR),
            P(None, DP, TENSOR),
            P(None, DP, None),
            P(None, DP, TENSOR),
            P(),
            P(),
            P(),
            P(),
            P(),
            P(),
            P(None, DP, TENSOR),
        ),
        check_vma=False,
    )
```
